128 devices in a mesh: seq: 64 (over z, y, x), mp: 2 (over core).
Axes of the slice: x: 4, y: 4, z: 4, core: 2. Of those that a mesh axis runs over, the one named last changes fastest.
Arguments:
- tokens: bfloat16 [16384, 1024], P('seq')
- token_sizes: int32 [16384], P('seq'), may hold values from 1 to 8
- merge_source: int32 [64, 128], P('seq'), may hold values from 0 to 127, each once within a row
- merge_target: int32 [64, 128], P('seq'), may hold values from 0 to 127
- merge_count: int32 [64], P('seq'), may hold values from 0 to 128, as said below
- attn_gain: float32 [1024], replicated, may hold values from 0.25 to 1.75
- qkv_weight: bfloat16 [3, 1024, 1024], P(None, None, 'mp')
- out_weight: bfloat16 [1024, 1024], P('mp'), may hold values from -0.1875 to 0.1875
- mlp_gain: float32 [1024], replicated, may hold values from 0.25 to 1.75
- up_weight: bfloat16 [1024, 4096], P(None, 'mp'), may hold values from -0.1875 to 0.1875
- down_weight: bfloat16 [4096, 1024], P('mp'), may hold values from -0.09375 to 0.09375
Outputs:
- merged_out: bfloat16 [16384, 1024], P('seq')
- best_score: float32 [8192], P('seq')
The draws below stay inside these ranges and needn't reach their ends.
Inputs may be any that keep to these rules, and one draw needn't show every extreme that they name: `merge_count`: one shard makes 128 merges and another none, in every draw.
All inputs are finite; a program needn't handle non-finite values.
Results may differ from the reference program's by a relative error of at most 0.007.
Values may be sent and summed in bfloat16 or wider, within the bound.
A program may use at most 384 MiB of HBM per device.

```python
import jax
import jax.numpy as jnp
from jax import lax

D = 1024
HEADS = 16
HEAD_DIM = 64
FF = 4096
TOK_DEV = 256
PART = 128
TOKENS = 16384
N_SEQ = 64


def draw_tokens(key, part):
    keys_all = jax.random.split(jax.random.fold_in(key, 11), 6)
    groups = TOKENS // 4
    proto = jax.random.normal(keys_all[0], (groups, D), jnp.float32)
    member = jax.random.randint(keys_all[1], (TOKENS,), 0, groups)
    noise = jax.random.normal(keys_all[2], (TOKENS, D), jnp.float32)
    result = proto[member] + 0.35 * noise
    grid = result.reshape(N_SEQ, TOK_DEV, D)
    first_half = grid[:, :PART]
    partner = jnp.roll(first_half, -1, axis=0)
    mix = jax.random.uniform(keys_all[5], (N_SEQ, PART, 1), jnp.float32, 0.0, 1.5)
    second_half = grid[:, PART:] + mix * partner
    result = jnp.concatenate([first_half, second_half], axis=1).reshape(TOKENS, D)
    return jnp.clip(result, -12.0, 12.0).astype(jnp.bfloat16)


def draw_qkv_weight(key, part):
    keys_all = jax.random.split(jax.random.fold_in(key, 23), 4)
    factor = D ** (-0.5)
    key_part = jax.random.normal(keys_all[0], (D, D), jnp.float32) * factor
    value_part = jax.random.normal(keys_all[1], (D, D), jnp.float32) * factor
    noise = jax.random.normal(keys_all[2], (D, D), jnp.float32) * factor
    strength = jax.random.uniform(keys_all[3], (HEADS,), jnp.float32, 1.0, 2.0)
    columns = jnp.repeat(strength, HEAD_DIM)
    query_part = key_part * columns[None, :] + 0.5 * noise
    return jnp.stack([query_part, key_part, value_part]).astype(jnp.bfloat16)


def draw_merge_count(key, part):
    keys_all = jax.random.split(jax.random.fold_in(key, 37), 3)
    counts = jax.random.randint(keys_all[0], (N_SEQ,), 0, PART + 1)
    highest_shard = jax.random.randint(keys_all[1], (), 0, N_SEQ)
    lowest_shard = (highest_shard + 1 + jax.random.randint(keys_all[2], (), 0, N_SEQ - 1)) % N_SEQ
    shard_ids = jnp.arange(N_SEQ)
    counts = jnp.where(shard_ids == highest_shard, PART, counts)
    counts = jnp.where(shard_ids == lowest_shard, 0, counts)
    return counts.astype(jnp.int32)


def with_ends(array, key, least, largest):
    spot = [jax.random.randint(jax.random.fold_in(key, axis), (), 0, length) for axis, length in enumerate(array.shape)]
    longest = array.shape.index(max(array.shape))
    neighbour = spot[:longest] + [(spot[longest] + 1) % array.shape[longest]] + spot[longest + 1:]
    return array.at[tuple(spot)].set(least).at[tuple(neighbour)].set(largest)


def block_levels(key, extent, shards, least, top_value):
    def one(axis_at, shards_of):
        heights = jax.random.uniform(jax.random.fold_in(jax.random.fold_in(key, 6), axis_at), (shards_of,), jnp.float32, least / len(shards), top_value / len(shards))
        return jnp.repeat(jnp.exp(heights), extent[axis_at] // shards_of).reshape((-1,) + (1,) * (len(extent) - axis_at - 1))

    level = one(*shards[0])
    for cut in shards[1:]:
        level = level * one(*cut)
    return level


def normal_values(own_key, extent, deviation, reach, cuts=(), kind=jnp.bfloat16):
    entries = deviation * jax.random.normal(own_key, extent, jnp.float32)
    if cuts:
        entries = entries * block_levels(own_key, extent, cuts, -0.22, 0.18)
    return jnp.clip(entries, -reach, reach).astype(kind)


def setup_inputs(seed: int = 0) -> dict:
    arg_keys = jax.random.split(jax.random.key(seed), 12)
    return {
        "tokens": draw_tokens(jax.random.fold_in(arg_keys[11], 71), 0),
        "token_sizes": with_ends(jax.random.randint(arg_keys[1], (TOKENS,), 1, 9), jax.random.fold_in(arg_keys[1], 1), 1, 8).astype(jnp.int32),
        "merge_source": jax.vmap(lambda own: jax.random.permutation(own, PART))(jax.random.split(arg_keys[2], N_SEQ)).reshape((N_SEQ, PART)).astype(jnp.int32),
        "merge_target": with_ends(jax.random.randint(arg_keys[3], (N_SEQ, PART), 0, PART), jax.random.fold_in(arg_keys[3], 1), 0, PART - 1).astype(jnp.int32),
        "merge_count": draw_merge_count(jax.random.fold_in(arg_keys[11], 71), 0),
        "attn_gain": jnp.clip(1.0 + 0.15 * jax.random.normal(arg_keys[5], (D,), jnp.float32), 0.25, 1.75),
        "qkv_weight": draw_qkv_weight(jax.random.fold_in(arg_keys[11], 71), 0),
        "out_weight": normal_values(arg_keys[7], (D, D), D ** -0.5, 0.1875, ((0, 2),)),
        "mlp_gain": jnp.clip(1.0 + 0.15 * jax.random.normal(arg_keys[8], (D,), jnp.float32), 0.25, 1.75),
        "up_weight": normal_values(arg_keys[9], (D, FF), D ** -0.5, 0.1875, ((1, 2),)),
        "down_weight": normal_values(arg_keys[10], (FF, D), FF ** -0.5, 0.09375, ((0, 2),)),
    }


epsilon = 1e-06
empty_bias = -10000.0

def layer_norm(values, gain_vector):
    center = values - lax.optimization_barrier(jnp.mean(values, axis=-1, keepdims=True))
    spread = lax.optimization_barrier(jnp.mean(center * center, axis=-1, keepdims=True))
    return center * lax.rsqrt(spread + epsilon) * gain_vector.astype(jnp.float32)

def reference(tokens, token_sizes, merge_source, merge_target, merge_count, attn_gain, qkv_weight, out_weight, mlp_gain, up_weight, down_weight):
    highest = lax.Precision.HIGHEST
    shard_rows = tokens.reshape(N_SEQ, TOK_DEV, D)
    normed = layer_norm(tokens.astype(jnp.float32), attn_gain).astype(jnp.bfloat16)
    metric = jnp.dot(normed, qkv_weight[1], preferred_element_type=jnp.float32).astype(jnp.bfloat16)
    metric = metric.reshape(N_SEQ, TOK_DEV, D).astype(jnp.float32)
    own_keys = metric[:, PART:]
    partner = jnp.roll(metric[:, :PART], -1, axis=0)
    products = jnp.einsum('sad,sbd->sab', own_keys, partner, precision=highest)
    own_norm = lax.rsqrt(lax.optimization_barrier(jnp.sum(own_keys * own_keys, axis=-1)) + epsilon)
    partner_norm = lax.rsqrt(lax.optimization_barrier(jnp.sum(partner * partner, axis=-1)) + epsilon)
    cosine = products * own_norm[:, :, None] * partner_norm[:, None, :]
    best_score = lax.optimization_barrier(jnp.max(cosine, axis=2)).reshape(N_SEQ * PART)
    partner_ids = jnp.arange(PART, dtype=jnp.int32)
    active = partner_ids[None, :] < merge_count[:, None]
    source_rows = (PART + merge_source).astype(jnp.int32)
    sizes_grid = token_sizes.reshape(N_SEQ, TOK_DEV)
    source_size = jnp.where(active, jnp.take_along_axis(sizes_grid, source_rows, axis=1), 0).astype(jnp.float32)
    weights = (merge_target[:, None, :] == partner_ids[None, :, None]).astype(jnp.float32) * source_size[:, None, :]
    picked = jnp.take_along_axis(shard_rows, source_rows[:, :, None], axis=1).astype(jnp.float32)
    added_rows = jnp.einsum('sbk,skd->sbd', weights, picked, precision=highest)
    added_size = lax.optimization_barrier(jnp.sum(weights, axis=2))
    added_rows = jnp.roll(added_rows, 1, axis=0)
    added_size = jnp.roll(added_size, 1, axis=0)
    base_size = sizes_grid[:, :PART].astype(jnp.float32)
    merged = (base_size[:, :, None] * shard_rows[:, :PART].astype(jnp.float32) + added_rows) / (base_size + added_size)[:, :, None]
    new_rows = jnp.concatenate([merged.astype(jnp.bfloat16), shard_rows[:, PART:]], axis=1)
    new_size = jnp.concatenate([base_size + added_size, sizes_grid[:, PART:].astype(jnp.float32)], axis=1)
    removed = jnp.any((merge_source[:, :, None] == partner_ids[None, None, :]) & active[:, :, None], axis=1)
    survive = jnp.concatenate([jnp.ones((N_SEQ, PART), bool), jnp.logical_not(removed)], axis=1)
    keep_int = survive.astype(jnp.int32)
    local_rank = (jnp.cumsum(keep_int, axis=1) - 1).astype(jnp.int32)
    counts = lax.optimization_barrier(jnp.sum(keep_int, axis=1)).astype(jnp.int32)
    before = (jnp.cumsum(counts) - counts).astype(jnp.int32)
    grand_total = jnp.sum(counts).astype(jnp.int32)
    global_rank = before[:, None] + local_rank
    position = global_rank % N_SEQ * TOK_DEV + global_rank // N_SEQ
    position = jnp.where(survive, position, TOKENS).reshape(TOKENS).astype(jnp.int32)
    bias_rows = jnp.log(new_size).astype(jnp.bfloat16).reshape(TOKENS)
    balanced = jnp.zeros((TOKENS, D), jnp.bfloat16).at[position].set(new_rows.reshape(TOKENS, D), mode='drop')
    key_bias = jnp.full((TOKENS,), empty_bias, jnp.float32).astype(jnp.bfloat16).at[position].set(bias_rows, mode='drop')
    slot_index = jnp.arange(TOKENS, dtype=jnp.int32)
    filled = slot_index % TOK_DEV * N_SEQ + slot_index // TOK_DEV < grand_total
    normed_bal = layer_norm(balanced.astype(jnp.float32), attn_gain).astype(jnp.bfloat16)
    queries = jnp.dot(normed_bal, qkv_weight[0], preferred_element_type=jnp.float32).astype(jnp.bfloat16)
    key_block = jnp.dot(normed_bal, qkv_weight[1], preferred_element_type=jnp.float32).astype(jnp.bfloat16)
    value_block = jnp.dot(normed_bal, qkv_weight[2], preferred_element_type=jnp.float32).astype(jnp.bfloat16)
    score_scale = HEAD_DIM ** (-0.5)
    key_heads = key_block.reshape(TOKENS, HEADS, HEAD_DIM).astype(jnp.float32)
    value_heads = value_block.reshape(TOKENS, HEADS, HEAD_DIM).astype(jnp.float32)
    bias_float = key_bias.astype(jnp.float32)

    def attend(query_block):
        scores = jnp.einsum('qhd,khd->hqk', query_block.astype(jnp.float32), key_heads, precision=highest) * score_scale + bias_float[None, None, :]
        row_peak = lax.optimization_barrier(jnp.max(scores, axis=-1, keepdims=True))
        exponent = jnp.exp(scores - row_peak)
        total_weight = lax.optimization_barrier(jnp.sum(exponent, axis=-1))
        rounded = lax.optimization_barrier(exponent.astype(jnp.bfloat16))
        weighted = jnp.einsum('hqk,khd->qhd', rounded.astype(jnp.float32), value_heads, precision=highest)
        return (weighted / total_weight.T[:, :, None]).astype(jnp.bfloat16)
    blocks = queries.reshape(TOKENS // TOK_DEV, TOK_DEV, HEADS, HEAD_DIM)
    mixed = lax.map(attend, blocks).reshape(TOKENS, D)
    attention = jnp.dot(mixed, out_weight, preferred_element_type=jnp.float32)
    layer_one = (balanced.astype(jnp.float32) + attention).astype(jnp.bfloat16)
    normed_mlp = layer_norm(layer_one.astype(jnp.float32), mlp_gain).astype(jnp.bfloat16)
    hidden = jax.nn.gelu(jnp.dot(normed_mlp, up_weight, preferred_element_type=jnp.float32), approximate=False).astype(jnp.bfloat16)
    result = layer_one.astype(jnp.float32) + jnp.dot(hidden, down_weight, preferred_element_type=jnp.float32)
    merged_out = jnp.where(filled[:, None], result, 0.0).astype(jnp.bfloat16)
    return (merged_out, best_score)
```

```python
import functools
import math

import jax
import jax.numpy as jnp
from jax import lax
from jax.experimental import pallas as pl
from jax.experimental.pallas import tpu as pltpu
from jax.sharding import PartitionSpec as P

HEAD_DIM = 64
LANES = 128
epsilon = 1e-06
empty_bias = -10000.0
LOG2E = math.log2(math.e)
SEQ = "seq"
NT = (((1,), (1,)), ((), ()))
TN = (((0,), (0,)), ((), ()))
NN = (((1,), (0,)), ((), ()))


def layer_norm(values, gain_vector):
    center = values - jnp.mean(values, axis=-1, keepdims=True)
    spread = jnp.mean(center * center, axis=-1, keepdims=True)
    return center * lax.rsqrt(spread + epsilon) * gain_vector


def dot32(a, b, dims=NN):
    return lax.dot_general(a, b, dims, preferred_element_type=jnp.float32)


def swap_cores(values):
    return lax.ppermute(values, "mp", [(0, 1), (1, 0)])


MESH = pl.DeviceIdType.MESH
ORDERS = ((1, 2, 4), (2, 4, 1), (4, 1, 2))
PARTS = ((0, 3), (3, 3), (6, 2))
STEP_OF = {0: 0, 1: 1, 2: 2, 4: 3, 3: 4, 5: 5, 6: 6, 7: 7}


def places():
    me = lax.axis_index("seq")
    return me // 16, me // 4 % 4, me % 4


def near(mask):
    z, y, x = places()
    if mask & 4:
        z = z + 1 - 2 * (z % 2)
    if mask & 2:
        y = y + 1 - 2 * (y % 2)
    if mask & 1:
        x = x + 1 - 2 * (x % 2)
    return z * 16 + y * 4 + x


def far(mask):
    z, y, x = places()
    if mask & 4:
        z = 3 - z
    if mask & 2:
        y = 3 - y
    if mask & 1:
        x = 3 - x
    return z * 16 + y * 4 + x


def cube_index(mask=0):
    z, y, x = places()
    z, y, x = z // 2, y // 2, x // 2
    if mask & 4:
        z = 1 - z
    if mask & 2:
        y = 1 - y
    if mask & 1:
        x = 1 - x
    return z * 4 + y * 2 + x


def layer_kernel(
    rows,
    dropped,
    total_ref,
    balanced_ref,
    bias_ref,
    attn_gain_ref,
    mlp_gain_ref,
    qkv_hbm,
    out_hbm,
    up_hbm,
    down_hbm,
    result_ref,
    qkv_w,
    out_w,
    up_w,
    down_w,
    kv_send,
    q_send,
    kv_buf,
    q_buf,
    k2,
    v2,
    acc,
    peak,
    o_send,
    o_buf,
    part_send,
    part_recv,
    layer_one,
    weight_sem,
    local_sem,
    spread_send,
    spread_recv,
    pass_send,
    pass_recv,
    back_send,
    back_recv,
    core_send,
    core_recv,
):
    core = lax.axis_index("mp")
    heads = 8
    block = rows + 16
    width = balanced_ref.shape[1]

    weight_copies = [
        pltpu.make_async_copy(src, dst, weight_sem.at[i])
        for i, (src, dst) in enumerate(((qkv_hbm, qkv_w), (out_hbm, out_w), (up_hbm, up_w), (down_hbm, down_w)))
    ]
    for copy in weight_copies:
        copy.start()

    barrier = pltpu.get_barrier_semaphore()
    for mask in range(1, 8):
        pl.semaphore_signal(barrier, inc=1, device_id=(far(mask), core), device_id_type=MESH)
    for mask in (1, 2, 4):
        pl.semaphore_signal(barrier, inc=1, device_id=(near(mask), core), device_id_type=MESH)
    pl.semaphore_signal(barrier, inc=1, device_id=(lax.axis_index("seq"), 1 - core), device_id_type=MESH)

    balanced = balanced_ref[:rows].astype(jnp.float32)
    normed = layer_norm(balanced, attn_gain_ref[...]).astype(jnp.bfloat16)
    weight_copies[0].wait()
    pl.semaphore_wait(barrier, 11)

    key = dot32(normed, qkv_w[1]).astype(jnp.bfloat16)
    value = dot32(normed, qkv_w[2]).astype(jnp.bfloat16)
    for j in range(heads):
        columns = slice(j * HEAD_DIM, (j + 1) * HEAD_DIM)
        kv_send[j, :rows, :] = jnp.concatenate([key[:, columns], value[:, columns]], axis=1)
        kv_send[j, rows:, :] = bias_ref[...]

    def spread_kv(mask):
        return pltpu.make_async_remote_copy(
            kv_send.at[cube_index(mask)], kv_buf.at[0, mask], spread_send.at[0, mask], spread_recv.at[0, mask],
            device_id=(far(mask), core), device_id_type=MESH,
        )

    def spread_q(mask):
        return pltpu.make_async_remote_copy(
            q_send.at[cube_index(mask)], q_buf.at[mask], spread_send.at[1, mask], spread_recv.at[1, mask],
            device_id=(far(mask), core), device_id_type=MESH,
        )

    def pass_on(part, near_mask, slot):
        first, size = PARTS[part]
        target = STEP_OF[slot ^ near_mask]
        return pltpu.make_async_remote_copy(
            kv_buf.at[STEP_OF[slot], pl.ds(first, size)], kv_buf.at[target, pl.ds(first, size)],
            pass_send.at[part, target], pass_recv.at[part, target],
            device_id=(near(near_mask), core), device_id_type=MESH,
        )

    for mask in range(1, 8):
        spread_kv(mask).start()
    own_kv = pltpu.make_async_copy(kv_send.at[cube_index()], kv_buf.at[0, 0], local_sem.at[0])
    own_kv.start()
    query = (dot32(normed, qkv_w[0]) * (HEAD_DIM ** (-0.5) * LOG2E)).astype(jnp.bfloat16)
    ones = (lax.broadcasted_iota(jnp.int32, (rows, HEAD_DIM), 1) < 2).astype(jnp.bfloat16)
    for j in range(heads):
        q_send[j] = jnp.concatenate([query[:, j * HEAD_DIM : (j + 1) * HEAD_DIM], ones], axis=1)
    for mask in range(1, 8):
        spread_q(mask).start()
    own_q = pltpu.make_async_copy(q_send.at[cube_index()], q_buf.at[0], local_sem.at[1])
    own_q.start()
    own_kv.wait()
    own_q.wait()
    for mask in range(1, 8):
        spread_kv(mask).wait_recv()
    for order in range(3):
        for part in range(3):
            pass_on(part, ORDERS[part][order], 0).start()
    for mask in range(1, 8):
        spread_q(mask).wait_recv()

    queries = heads * rows
    cut = queries // 2 // 256 * 256
    acc[...] = jnp.zeros_like(acc)
    empty = -9984.0 * LOG2E
    peak[...] = jnp.full(peak.shape, empty if dropped else -3e38, jnp.float32)
    lane = lax.broadcasted_iota(jnp.int32, (rows, LANES), 1)
    value_tail = (lane == HEAD_DIM).astype(jnp.bfloat16)
    if dropped:
        acc[HEAD_DIM : HEAD_DIM + 1, :] = jnp.full((1, queries), float(dropped), jnp.float32)
    pick_row = lax.broadcasted_iota(jnp.int32, (16, LANES), 0)
    pick_lane = lax.broadcasted_iota(jnp.int32, (16, LANES), 1)
    picks = [
        (((pick_row == i) & (pick_lane == HEAD_DIM)) | ((pick_row == i + 2) & (pick_lane == HEAD_DIM + 1))).astype(jnp.bfloat16)
        for i in range(2)
    ]

    def step(i, carry):
        for slot, at in STEP_OF.items():
            if slot == 0:
                continue

            @pl.when(i == at)
            def _(slot=slot):
                for part in range(3):
                    d1, d2, d3 = ORDERS[part]
                    came_by = d3 if slot & d3 else d2 if slot & d2 else d1
                    pass_on(part, came_by, slot ^ came_by).wait_recv()
                    if came_by == d1:
                        pass_on(part, d2, slot).start()
                    if came_by != d3:
                        pass_on(part, d3, slot).start()

        def unpack(a, carry):
            here = pl.ds(pl.multiple_of(a * rows, 16), rows)
            kv = kv_buf[i, a, :rows, :]
            tile = kv_buf[i, a, rows:, :]
            bias = jnp.concatenate(
                [dot32(tile, picks[0], TN), dot32(tile, picks[1], TN)], axis=0
            )[:rows].astype(jnp.bfloat16)
            k2[here, :] = jnp.where(lane < HEAD_DIM, kv, bias)
            v2[here, :] = jnp.concatenate([kv[:, HEAD_DIM:], value_tail[:, HEAD_DIM:]], axis=1)
            return carry

        lax.fori_loop(0, heads, unpack, 0)
        for begin, end in ((0, cut), (cut, queries)):
            first_a = begin
            q = q_buf[...].reshape(queries, LANES)[begin:end]
            s = dot32(k2[...], q, NT)
            old = peak[:, begin:end]
            new = jnp.maximum(old, jnp.max(s, axis=0, keepdims=True))
            p = jnp.exp2(s - new).astype(jnp.bfloat16)
            peak[:, begin:end] = new
            acc[:, begin:end] = acc[:, begin:end] * jnp.exp2(old - new) + dot32(v2[...], p, TN)
        return carry

    lax.fori_loop(0, 8, step, 0)

    def back(mask):
        return pltpu.make_async_remote_copy(
            o_send.at[mask], o_buf.at[cube_index()], back_send.at[mask], back_recv.at[mask],
            device_id=(far(mask), core), device_id_type=MESH,
        )

    def back_in(mask):
        return pltpu.make_async_remote_copy(
            o_send.at[mask], o_buf.at[cube_index(mask)], back_send.at[mask], back_recv.at[mask],
            device_id=(far(mask), core), device_id_type=MESH,
        )

    scaled = acc[...] / acc[HEAD_DIM : HEAD_DIM + 1, :]
    o_send[...] = scaled.T.astype(jnp.bfloat16).reshape(heads, rows, LANES)
    for mask in range(1, 8):
        back(mask).start()
    own_o = pltpu.make_async_copy(o_send.at[0], o_buf.at[cube_index()], local_sem.at[2])
    own_o.start()
    weight_copies[1].wait()
    own_o.wait()
    for mask in range(1, 8):
        back_in(mask).wait_recv()

    def swap(which, size):
        return pltpu.make_async_remote_copy(
            part_send.at[which], part_recv.at[which], core_send.at[which], core_recv.at[which],
            device_id=(lax.axis_index("seq"), 1 - core), device_id_type=MESH,
        )

    mixed = jnp.concatenate([o_buf[j, :, :HEAD_DIM] for j in range(heads)], axis=1)
    part_send[0] = dot32(mixed, out_w[...]).astype(jnp.bfloat16)
    swap(0, rows).start()
    swap(0, rows).wait_recv()
    attention = part_send[0].astype(jnp.float32) + part_recv[0].astype(jnp.float32)
    layer_one[...] = (balanced_ref[:rows].astype(jnp.float32) + attention).astype(jnp.bfloat16)
    normed_mlp = layer_norm(layer_one[...].astype(jnp.float32), mlp_gain_ref[...]).astype(jnp.bfloat16)
    weight_copies[2].wait()
    weight_copies[3].wait()
    hidden = dot32(normed_mlp, up_w[...])
    hidden = (0.5 * hidden * (1.0 + lax.erf(hidden * math.sqrt(0.5)))).astype(jnp.bfloat16)
    part_send[1] = dot32(hidden, down_w[...]).astype(jnp.bfloat16)
    swap(1, rows).start()
    swap(1, rows).wait_recv()
    mlp = part_send[1].astype(jnp.float32) + part_recv[1].astype(jnp.float32)
    result = layer_one[...].astype(jnp.float32) + mlp
    slot = lax.broadcasted_iota(jnp.int32, (rows, width), 0) * 64 + lax.axis_index("seq")
    result_ref[:rows, :] = jnp.where(slot < total_ref[0], result, 0.0).astype(jnp.bfloat16)
    if rows < result_ref.shape[0]:
        result_ref[rows:, :] = jnp.zeros((result_ref.shape[0] - rows, width), jnp.bfloat16)

    for mask in range(1, 8):
        spread_kv(mask).wait_send()
        spread_q(mask).wait_send()
        back(mask).wait_send()
    for part in range(3):
        d1, d2, d3 = ORDERS[part]
        for near_mask, slot in ((d1, 0), (d2, 0), (d3, 0), (d2, d1), (d3, d1), (d3, d2), (d3, d1 | d2)):
            pass_on(part, near_mask, slot).wait_send()
    swap(0, rows).wait_send()
    swap(1, rows).wait_send()


def layer(rows, which, total, balanced, bias_tile, attn_gain, mlp_gain, qkv_weight, out_weight, up_weight, down_weight):
    total_rows, width = balanced.shape
    heads = 8
    hidden = up_weight.shape[1]
    queries = heads * rows
    bf16 = jnp.bfloat16
    vmem = pl.BlockSpec(memory_space=pltpu.VMEM)
    anywhere = pl.BlockSpec(memory_space=pl.ANY)
    dma = pltpu.SemaphoreType.DMA
    return pl.pallas_call(
        functools.partial(layer_kernel, rows, 64 * (total_rows - rows)),
        in_specs=[pl.BlockSpec(memory_space=pltpu.SMEM), vmem, vmem, vmem, vmem] + [anywhere] * 4,
        out_specs=vmem,
        out_shape=jax.ShapeDtypeStruct((total_rows, width), bf16),
        scratch_shapes=[
            pltpu.VMEM(qkv_weight.shape, bf16),
            pltpu.VMEM(out_weight.shape, bf16),
            pltpu.VMEM(up_weight.shape, bf16),
            pltpu.VMEM(down_weight.shape, bf16),
            pltpu.VMEM((heads, rows + 16, LANES), bf16),
            pltpu.VMEM((heads, rows, LANES), bf16),
            pltpu.VMEM((8, heads, rows + 16, LANES), bf16),
            pltpu.VMEM((heads, rows, LANES), bf16),
            pltpu.VMEM((queries, LANES), bf16),
            pltpu.VMEM((queries, LANES), bf16),
            pltpu.VMEM((LANES, queries), jnp.float32),
            pltpu.VMEM((1, queries), jnp.float32),
            pltpu.VMEM((heads, rows, LANES), bf16),
            pltpu.VMEM((heads, rows, LANES), bf16),
            pltpu.VMEM((2, rows, width), bf16),
            pltpu.VMEM((2, rows, width), bf16),
            pltpu.VMEM((rows, width), bf16),
            dma((4,)),
            dma((3,)),
            dma((2, 8)),
            dma((2, 8)),
            dma((3, 8)),
            dma((3, 8)),
            dma((8,)),
            dma((8,)),
            dma((2,)),
            dma((2,)),
        ],
        compiler_params=pltpu.CompilerParams(
            vmem_limit_bytes=60 * 2**20, collective_id=which, has_side_effects=True
        ),
        cost_estimate=pl.CostEstimate(
            flops=queries * queries * 8 * 256, bytes_accessed=16 * 2**20, transcendentals=queries * queries * 8
        ),
    )(total, balanced, bias_tile, attn_gain, mlp_gain, qkv_weight, out_weight, up_weight, down_weight)


def on_device(
    tokens,
    token_sizes,
    merge_source,
    merge_target,
    merge_count,
    attn_gain,
    qkv_weight,
    out_weight,
    mlp_gain,
    up_weight,
    down_weight,
):
    shards = 64
    me = lax.axis_index(SEQ)
    rows, width = tokens.shape
    half = rows // 2
    slots = rows // shards
    ids = jnp.arange(half, dtype=jnp.int32)
    row_ids = jnp.arange(rows, dtype=jnp.int32)
    shard_ids = jnp.arange(shards, dtype=jnp.int32)
    ahead = [(i, (i + 1) % shards) for i in range(shards)]
    behind = [(i, (i - 1) % shards) for i in range(shards)]

    counts = rows - lax.all_gather(merge_count, SEQ, axis=0, tiled=True)
    active = ids < merge_count[0]
    hit = (merge_source[0][:, None] == ids[None, :]) & active[:, None]
    removed = jnp.any(hit, axis=0)
    goal = jnp.sum(jnp.where(hit, merge_target[0][:, None], 0), axis=0)
    weights = jnp.where(
        (goal[None, :] == ids[:, None]) & removed[None, :], token_sizes[half:][None, :], 0
    ).astype(jnp.bfloat16)
    merging = lax.ppermute(jnp.concatenate([tokens[half:], weights], axis=1), SEQ, ahead)
    weights = merging[:, width:]
    added_rows = dot32(weights, merging[:, :width])
    added_size = jnp.sum(weights.astype(jnp.float32), axis=1)
    base_size = token_sizes[:half].astype(jnp.float32)
    merged = (base_size[:, None] * tokens[:half].astype(jnp.float32) + added_rows) / (
        base_size + added_size
    )[:, None]
    new_rows = jnp.concatenate([merged.astype(jnp.bfloat16), tokens[half:]], axis=0)
    new_size = jnp.concatenate([base_size + added_size, token_sizes[half:].astype(jnp.float32)])
    bias_rows = jnp.log(new_size).astype(jnp.bfloat16)
    bias_lanes = jnp.where(jnp.arange(LANES)[None, :] == 0, bias_rows[:, None], 0).astype(jnp.bfloat16)
    payload = jnp.concatenate([new_rows, bias_lanes], axis=1)

    survive = jnp.concatenate([jnp.ones((half,), bool), jnp.logical_not(removed)])
    local_rank = jnp.sum((row_ids[:, None] > row_ids[None, :]) & survive[None, :], axis=1, dtype=jnp.int32)
    before = jnp.sum(jnp.where(shard_ids[:, None] > shard_ids[None, :], counts[None, :], 0), axis=1)
    my_start = jnp.sum(jnp.where(shard_ids < me, counts, 0))
    grand_total = jnp.sum(counts)
    flat_slot = (my_start + local_rank) % shards * slots + local_rank // shards
    put = ((flat_slot[None, :] == row_ids[:, None]) & survive[None, :]).astype(jnp.bfloat16)
    outgoing = dot32(put, payload).astype(jnp.bfloat16).reshape(shards, slots, width + LANES)
    arrived = lax.all_to_all(outgoing, SEQ, split_axis=0, concat_axis=0, tiled=True)
    wanted = row_ids * shards + me
    filled = wanted < grand_total
    sender = jnp.sum((before[None, :] <= wanted[:, None]).astype(jnp.int32), axis=1) - 1
    sender_start = jnp.sum(jnp.where(sender[:, None] == shard_ids[None, :], before[None, :], 0), axis=1)
    fetch = sender * slots + (wanted - sender_start) // shards
    take = ((fetch[:, None] == row_ids[None, :]) & filled[:, None]).astype(jnp.bfloat16)
    balanced = dot32(take, arrived.reshape(rows, width + LANES)).astype(jnp.bfloat16)
    key_bias = jnp.where(filled, balanced[:, width], jnp.bfloat16(empty_bias))
    balanced = balanced[:, :width]

    bias = key_bias.astype(jnp.float32) * LOG2E
    high = bias.astype(jnp.bfloat16)
    low = (bias - high.astype(jnp.float32)).astype(jnp.bfloat16)
    bias_tile = jnp.concatenate(
        [high.reshape(2, LANES), low.reshape(2, LANES), jnp.zeros((12, LANES), jnp.bfloat16)], axis=0
    )
    sizes = (192, 208, rows)
    needed = (grand_total + shards - 1) // shards
    index = sum((needed > size).astype(jnp.int32) for size in sizes[:-1])
    merged_out = lax.switch(
        index,
        [functools.partial(layer, size, at + 1) for at, size in enumerate(sizes)],
        grand_total[None], balanced, bias_tile, attn_gain[None, :], mlp_gain[None, :],
        qkv_weight, out_weight, up_weight, down_weight,
    )

    normed = layer_norm(tokens.astype(jnp.float32), attn_gain).astype(jnp.bfloat16)
    metric = dot32(normed, qkv_weight[1]).astype(jnp.bfloat16)
    partner = lax.ppermute(metric[:half], SEQ, behind)
    own_keys = metric[half:]
    products = dot32(own_keys, partner, NT)
    own_square = jnp.sum(jnp.square(own_keys.astype(jnp.float32)), axis=1)
    partner_square = jnp.sum(jnp.square(partner.astype(jnp.float32)), axis=1)
    sums = jnp.concatenate(
        [products, jnp.broadcast_to(own_square[:, None], (half, LANES)), jnp.broadcast_to(partner_square[:, None], (half, LANES))], axis=1
    )
    sums = sums + swap_cores(sums)
    cosine = (
        sums[:, :LANES]
        * lax.rsqrt(sums[:, LANES] + epsilon)[:, None]
        * lax.rsqrt(sums[:, 2 * LANES] + epsilon)[None, :]
    )
    best_score = jnp.max(cosine, axis=1)
    return (merged_out, best_score)


def solution(mesh):
    placed = (
        P(SEQ, None),
        P(SEQ),
        P(SEQ, None),
        P(SEQ, None),
        P(SEQ),
        P(),
        P(None, None, "mp"),
        P("mp", None),
        P(),
        P(None, "mp"),
        P("mp", None),
    )
    return jax.shard_map(
        on_device, mesh=mesh, in_specs=placed, out_specs=(P(SEQ, None), P(SEQ)), check_vma=False
    )
```

```python
import functools
import math

import jax
import jax.numpy as jnp
from jax import lax
from jax.experimental import pallas as pl
from jax.experimental.pallas import tpu as pltpu
from jax.sharding import PartitionSpec as P

HEAD_DIM = 64
LANES = 128
epsilon = 1e-06
LOG2E = math.log2(math.e)
NT = (((1,), (1,)), ((), ()))
TN = (((0,), (0,)), ((), ()))
NN = (((1,), (0,)), ((), ()))


def layer_norm(values, gain_vector):
    center = values - jnp.mean(values, axis=-1, keepdims=True)
    spread = jnp.mean(center * center, axis=-1, keepdims=True)
    return center * lax.rsqrt(spread + epsilon) * gain_vector


def dot32(a, b, dims=NN):
    return lax.dot_general(a, b, dims, preferred_element_type=jnp.float32)


MESH = pl.DeviceIdType.MESH
ORDERS = ((1, 2, 4), (2, 4, 1), (4, 1, 2))
PARTS = ((0, 3), (3, 3), (6, 2))
STEP_OF = {0: 0, 1: 1, 2: 2, 4: 3, 3: 4, 5: 5, 6: 6, 7: 7}


def places():
    me = lax.axis_index("seq")
    return me // 16, me // 4 % 4, me % 4


def near(mask):
    z, y, x = places()
    if mask & 4:
        z = z + 1 - 2 * (z % 2)
    if mask & 2:
        y = y + 1 - 2 * (y % 2)
    if mask & 1:
        x = x + 1 - 2 * (x % 2)
    return z * 16 + y * 4 + x


def far(mask):
    z, y, x = places()
    if mask & 4:
        z = 3 - z
    if mask & 2:
        y = 3 - y
    if mask & 1:
        x = 3 - x
    return z * 16 + y * 4 + x


def cube_index(mask=0):
    z, y, x = places()
    z, y, x = z // 2, y // 2, x // 2
    if mask & 4:
        z = 1 - z
    if mask & 2:
        y = 1 - y
    if mask & 1:
        x = 1 - x
    return z * 4 + y * 2 + x


def layer_kernel(
    rows,
    dropped,
    total_ref,
    balanced_ref,
    bias_ref,
    attn_gain_ref,
    mlp_gain_ref,
    qkv_hbm,
    out_hbm,
    up_hbm,
    down_hbm,
    result_ref,
    qkv_w,
    out_w,
    up_w,
    down_w,
    kv_send,
    q_send,
    kv_buf,
    q_buf,
    k2,
    v2,
    acc,
    peak,
    o_send,
    o_buf,
    part_send,
    part_recv,
    layer_one,
    weight_sem,
    local_sem,
    spread_send,
    spread_recv,
    pass_send,
    pass_recv,
    back_send,
    back_recv,
    core_send,
    core_recv,
):
    core = lax.axis_index("mp")
    heads = 8
    block = rows + 16
    width = balanced_ref.shape[1]

    weight_copies = [
        pltpu.make_async_copy(src, dst, weight_sem.at[i])
        for i, (src, dst) in enumerate(((qkv_hbm, qkv_w), (out_hbm, out_w), (up_hbm, up_w), (down_hbm, down_w)))
    ]
    for copy in weight_copies:
        copy.start()

    barrier = pltpu.get_barrier_semaphore()
    for mask in range(1, 8):
        pl.semaphore_signal(barrier, inc=1, device_id=(far(mask), core), device_id_type=MESH)
    for mask in (1, 2, 4):
        pl.semaphore_signal(barrier, inc=1, device_id=(near(mask), core), device_id_type=MESH)
    pl.semaphore_signal(barrier, inc=1, device_id=(lax.axis_index("seq"), 1 - core), device_id_type=MESH)

    balanced = balanced_ref[:rows].astype(jnp.float32)
    normed = layer_norm(balanced, attn_gain_ref[...]).astype(jnp.bfloat16)
    weight_copies[0].wait()
    pl.semaphore_wait(barrier, 11)

    key = dot32(normed, qkv_w[1]).astype(jnp.bfloat16)
    value = dot32(normed, qkv_w[2]).astype(jnp.bfloat16)
    for j in range(heads):
        columns = slice(j * HEAD_DIM, (j + 1) * HEAD_DIM)
        kv_send[j, :rows, :] = jnp.concatenate([key[:, columns], value[:, columns]], axis=1)
        kv_send[j, rows:, :] = bias_ref[...]

    def spread_kv(mask):
        return pltpu.make_async_remote_copy(
            kv_send.at[cube_index(mask)], kv_buf.at[0, mask], spread_send.at[0, mask], spread_recv.at[0, mask],
            device_id=(far(mask), core), device_id_type=MESH,
        )

    def spread_q(mask):
        return pltpu.make_async_remote_copy(
            q_send.at[cube_index(mask)], q_buf.at[mask], spread_send.at[1, mask], spread_recv.at[1, mask],
            device_id=(far(mask), core), device_id_type=MESH,
        )

    def pass_on(part, near_mask, slot):
        first, size = PARTS[part]
        target = STEP_OF[slot ^ near_mask]
        return pltpu.make_async_remote_copy(
            kv_buf.at[STEP_OF[slot], pl.ds(first, size)], kv_buf.at[target, pl.ds(first, size)],
            pass_send.at[part, target], pass_recv.at[part, target],
            device_id=(near(near_mask), core), device_id_type=MESH,
        )

    for mask in range(1, 8):
        spread_kv(mask).start()
    own_kv = pltpu.make_async_copy(kv_send.at[cube_index()], kv_buf.at[0, 0], local_sem.at[0])
    own_kv.start()
    query = (dot32(normed, qkv_w[0]) * (HEAD_DIM ** (-0.5) * LOG2E)).astype(jnp.bfloat16)
    ones = (lax.broadcasted_iota(jnp.int32, (rows, HEAD_DIM), 1) < 2).astype(jnp.bfloat16)
    for j in range(heads):
        q_send[j] = jnp.concatenate([query[:, j * HEAD_DIM : (j + 1) * HEAD_DIM], ones], axis=1)
    for mask in range(1, 8):
        spread_q(mask).start()
    own_q = pltpu.make_async_copy(q_send.at[cube_index()], q_buf.at[0], local_sem.at[1])
    own_q.start()
    own_kv.wait()
    own_q.wait()
    for mask in range(1, 8):
        spread_kv(mask).wait_recv()
    for order in range(3):
        for part in range(3):
            pass_on(part, ORDERS[part][order], 0).start()
    for mask in range(1, 8):
        spread_q(mask).wait_recv()

    queries = heads * rows
    cut = queries // 2 // 256 * 256
    acc[...] = jnp.zeros_like(acc)
    empty = -9984.0 * LOG2E
    peak[...] = jnp.full(peak.shape, empty if dropped else -3e38, jnp.float32)
    lane = lax.broadcasted_iota(jnp.int32, (rows, LANES), 1)
    value_tail = (lane == HEAD_DIM).astype(jnp.bfloat16)
    if dropped:
        acc[HEAD_DIM : HEAD_DIM + 1, :] = jnp.full((1, queries), float(dropped), jnp.float32)
    pick_row = lax.broadcasted_iota(jnp.int32, (16, LANES), 0)
    pick_lane = lax.broadcasted_iota(jnp.int32, (16, LANES), 1)
    picks = [
        (((pick_row == i) & (pick_lane == HEAD_DIM)) | ((pick_row == i + 2) & (pick_lane == HEAD_DIM + 1))).astype(jnp.bfloat16)
        for i in range(2)
    ]

    def step(i, carry):
        for slot, at in STEP_OF.items():
            if slot == 0:
                continue

            @pl.when(i == at)
            def _(slot=slot):
                for part in range(3):
                    d1, d2, d3 = ORDERS[part]
                    came_by = d3 if slot & d3 else d2 if slot & d2 else d1
                    pass_on(part, came_by, slot ^ came_by).wait_recv()
                    if came_by == d1:
                        pass_on(part, d2, slot).start()
                    if came_by != d3:
                        pass_on(part, d3, slot).start()

        def unpack(a, carry):
            here = pl.ds(pl.multiple_of(a * rows, 16), rows)
            kv = kv_buf[i, a, :rows, :]
            tile = kv_buf[i, a, rows:, :]
            bias = jnp.concatenate(
                [dot32(tile, picks[0], TN), dot32(tile, picks[1], TN)], axis=0
            )[:rows].astype(jnp.bfloat16)
            k2[here, :] = jnp.where(lane < HEAD_DIM, kv, bias)
            v2[here, :] = jnp.concatenate([kv[:, HEAD_DIM:], value_tail[:, HEAD_DIM:]], axis=1)
            return carry

        lax.fori_loop(0, heads, unpack, 0)
        for begin, end in ((0, cut), (cut, queries)):
            first_a = begin
            q = q_buf[...].reshape(queries, LANES)[begin:end]
            s = dot32(k2[...], q, NT)
            old = peak[:, begin:end]
            new = jnp.maximum(old, jnp.max(s, axis=0, keepdims=True))
            p = jnp.exp2(s - new).astype(jnp.bfloat16)
            peak[:, begin:end] = new
            acc[:, begin:end] = acc[:, begin:end] * jnp.exp2(old - new) + dot32(v2[...], p, TN)
        return carry

    lax.fori_loop(0, 8, step, 0)

    def back(mask):
        return pltpu.make_async_remote_copy(
            o_send.at[mask], o_buf.at[cube_index()], back_send.at[mask], back_recv.at[mask],
            device_id=(far(mask), core), device_id_type=MESH,
        )

    def back_in(mask):
        return pltpu.make_async_remote_copy(
            o_send.at[mask], o_buf.at[cube_index(mask)], back_send.at[mask], back_recv.at[mask],
            device_id=(far(mask), core), device_id_type=MESH,
        )

    scaled = acc[...] / acc[HEAD_DIM : HEAD_DIM + 1, :]
    o_send[...] = scaled.T.astype(jnp.bfloat16).reshape(heads, rows, LANES)
    for mask in range(1, 8):
        back(mask).start()
    own_o = pltpu.make_async_copy(o_send.at[0], o_buf.at[cube_index()], local_sem.at[2])
    own_o.start()
    weight_copies[1].wait()
    own_o.wait()
    for mask in range(1, 8):
        back_in(mask).wait_recv()

    def swap(which, size):
        return pltpu.make_async_remote_copy(
            part_send.at[which], part_recv.at[which], core_send.at[which], core_recv.at[which],
            device_id=(lax.axis_index("seq"), 1 - core), device_id_type=MESH,
        )

    mixed = jnp.concatenate([o_buf[j, :, :HEAD_DIM] for j in range(heads)], axis=1)
    part_send[0] = dot32(mixed, out_w[...]).astype(jnp.bfloat16)
    swap(0, rows).start()
    swap(0, rows).wait_recv()
    attention = part_send[0].astype(jnp.float32) + part_recv[0].astype(jnp.float32)
    layer_one[...] = (balanced_ref[:rows].astype(jnp.float32) + attention).astype(jnp.bfloat16)
    normed_mlp = layer_norm(layer_one[...].astype(jnp.float32), mlp_gain_ref[...]).astype(jnp.bfloat16)
    weight_copies[2].wait()
    weight_copies[3].wait()
    hidden = dot32(normed_mlp, up_w[...])
    hidden = (0.5 * hidden * (1.0 + lax.erf(hidden * math.sqrt(0.5)))).astype(jnp.bfloat16)
    part_send[1] = dot32(hidden, down_w[...]).astype(jnp.bfloat16)
    swap(1, rows).start()
    swap(1, rows).wait_recv()
    mlp = part_send[1].astype(jnp.float32) + part_recv[1].astype(jnp.float32)
    result = layer_one[...].astype(jnp.float32) + mlp
    slot = lax.broadcasted_iota(jnp.int32, (rows, width), 0) * 64 + lax.axis_index("seq")
    result_ref[:rows, :] = jnp.where(slot < total_ref[0], result, 0.0).astype(jnp.bfloat16)
    if rows < result_ref.shape[0]:
        result_ref[rows:, :] = jnp.zeros((result_ref.shape[0] - rows, width), jnp.bfloat16)

    for mask in range(1, 8):
        spread_kv(mask).wait_send()
        spread_q(mask).wait_send()
        back(mask).wait_send()
    for part in range(3):
        d1, d2, d3 = ORDERS[part]
        for near_mask, slot in ((d1, 0), (d2, 0), (d3, 0), (d2, d1), (d3, d1), (d3, d2), (d3, d1 | d2)):
            pass_on(part, near_mask, slot).wait_send()
    swap(0, rows).wait_send()
    swap(1, rows).wait_send()


def layer(rows, which, total, balanced, bias_tile, attn_gain, mlp_gain, qkv_weight, out_weight, up_weight, down_weight):
    total_rows, width = balanced.shape
    heads = 8
    hidden = up_weight.shape[1]
    queries = heads * rows
    bf16 = jnp.bfloat16
    vmem = pl.BlockSpec(memory_space=pltpu.VMEM)
    anywhere = pl.BlockSpec(memory_space=pl.ANY)
    dma = pltpu.SemaphoreType.DMA
    return pl.pallas_call(
        functools.partial(layer_kernel, rows, 64 * (total_rows - rows)),
        in_specs=[pl.BlockSpec(memory_space=pltpu.SMEM), vmem, vmem, vmem, vmem] + [anywhere] * 4,
        out_specs=vmem,
        out_shape=jax.ShapeDtypeStruct((total_rows, width), bf16),
        scratch_shapes=[
            pltpu.VMEM(qkv_weight.shape, bf16),
            pltpu.VMEM(out_weight.shape, bf16),
            pltpu.VMEM(up_weight.shape, bf16),
            pltpu.VMEM(down_weight.shape, bf16),
            pltpu.VMEM((heads, rows + 16, LANES), bf16),
            pltpu.VMEM((heads, rows, LANES), bf16),
            pltpu.VMEM((8, heads, rows + 16, LANES), bf16),
            pltpu.VMEM((heads, rows, LANES), bf16),
            pltpu.VMEM((queries, LANES), bf16),
            pltpu.VMEM((queries, LANES), bf16),
            pltpu.VMEM((LANES, queries), jnp.float32),
            pltpu.VMEM((1, queries), jnp.float32),
            pltpu.VMEM((heads, rows, LANES), bf16),
            pltpu.VMEM((heads, rows, LANES), bf16),
            pltpu.VMEM((2, rows, width), bf16),
            pltpu.VMEM((2, rows, width), bf16),
            pltpu.VMEM((rows, width), bf16),
            dma((4,)),
            dma((3,)),
            dma((2, 8)),
            dma((2, 8)),
            dma((3, 8)),
            dma((3, 8)),
            dma((8,)),
            dma((8,)),
            dma((2,)),
            dma((2,)),
        ],
        compiler_params=pltpu.CompilerParams(
            vmem_limit_bytes=60 * 2**20, collective_id=which, has_side_effects=True
        ),
        cost_estimate=pl.CostEstimate(
            flops=queries * queries * 8 * 256, bytes_accessed=16 * 2**20, transcendentals=queries * queries * 8
        ),
    )(total, balanced, bias_tile, attn_gain, mlp_gain, qkv_weight, out_weight, up_weight, down_weight)


def near_index(mask=0):
    z, y, x = places()
    bits = [(c // 2 + c % 2) % 2 for c in (z, y, x)]
    bits = [1 - b if mask & m else b for b, m in zip(bits, (4, 2, 1))]
    return bits[0] * 4 + bits[1] * 2 + bits[2]


def cube_and_near(shard):
    parts = (shard >> 4, (shard >> 2) & 3, shard & 3)
    cube = sum((c >> 1) * m for c, m in zip(parts, (4, 2, 1)))
    near = sum(((c >> 1) ^ (c & 1)) * m for c, m in zip(parts, (4, 2, 1)))
    return cube, near


def iota(shape, dim):
    return lax.broadcasted_iota(jnp.int32, shape, dim)


def to_column(row):
    n = row.shape[1]
    return jnp.sum(jnp.where(iota((n, n), 0) == iota((n, n), 1), row, 0), axis=1, keepdims=True)


def to_row(column):
    n = column.shape[0]
    return jnp.sum(jnp.where(iota((n, n), 0) == iota((n, n), 1), column, 0), axis=0, keepdims=True)


def deal_kernel(
    tokens_ref,
    sizes_ref,
    source_ref,
    target_ref,
    count_ref,
    gain_ref,
    key_w,
    balanced_ref,
    bias_ref,
    total_ref,
    best_ref,
    shift_send,
    shift_recv,
    count_send,
    count_recv,
    metric_send,
    metric_recv,
    score_send,
    score_recv,
    far_out,
    far_in,
    near_out,
    near_in,
    half_send,
    half_recv,
    shift_sem,
    count_send_sem,
    count_recv_sem,
    metric_sem,
    score_sem,
    far_send_sem,
    far_recv_sem,
    near_send_sem,
    near_recv_sem,
    half_sem,
    local_sem,
):
    me = lax.axis_index("seq")
    core = lax.axis_index("mp")
    shards = 64
    rows, width = tokens_ref.shape
    half = rows // 2
    part = width // 2
    slots = rows // shards
    ahead, behind = (me + 1) % shards, (me + shards - 1) % shards
    own_columns = pl.ds(pl.multiple_of(core * part, part), part)
    f32, bf16 = jnp.float32, jnp.bfloat16

    barrier = pltpu.get_barrier_semaphore()
    for mask in range(1, 8):
        pl.semaphore_signal(barrier, inc=1, device_id=(far(mask), core), device_id_type=MESH)
        pl.semaphore_signal(barrier, inc=1, device_id=(near(mask), core), device_id_type=MESH)
    for other in (ahead, behind):
        pl.semaphore_signal(barrier, inc=1, device_id=(other, core), device_id_type=MESH)
    pl.semaphore_signal(barrier, inc=1, device_id=(me, 1 - core), device_id_type=MESH)

    def remote(src, dst, send_sem, recv_sem, seq, mp):
        return pltpu.make_async_remote_copy(
            src, dst, send_sem, recv_sem, device_id=(seq, mp), device_id_type=MESH
        )

    shift = remote(shift_send, shift_recv, shift_sem.at[0], shift_sem.at[1], ahead, core)
    metric_copy = remote(metric_send, metric_recv, metric_sem.at[0], metric_sem.at[1], behind, core)
    score_copy = remote(score_send, score_recv, score_sem.at[0], score_sem.at[1], me, 1 - core)
    half_copy = remote(half_send, half_recv, half_sem.at[0], half_sem.at[1], me, 1 - core)

    def counts_to(stage, mask):
        return remote(
            count_send.at[stage], count_recv.at[stage, mask], count_send_sem.at[stage, mask],
            count_recv_sem.at[stage, mask], (far, near)[stage](mask), core,
        )

    def far_copy(mask, landed=False):
        return remote(
            far_out.at[cube_index(mask)], far_in.at[cube_index(mask) if landed else cube_index()],
            far_send_sem.at[mask], far_recv_sem.at[mask], far(mask), core,
        )

    def near_copy(mask, landed=False):
        return remote(
            near_out.at[near_index(mask)], near_in.at[near_index(mask) if landed else near_index()],
            near_send_sem.at[mask], near_recv_sem.at[mask], near(mask), core,
        )

    count = count_ref[0]
    active = iota((1, half), 1) < count
    hit = (source_ref[...] == iota((half, half), 0)) & active
    removed = jnp.max(jnp.where(hit, 1, 0), axis=1, keepdims=True)
    goal = jnp.sum(jnp.where(hit, target_ref[...], 0), axis=1, keepdims=True)
    late_size = to_column(sizes_ref[:, half:])
    weights = jnp.where((goal == iota((half, half), 1)) & (removed > 0), late_size, 0)
    shift_send[:, :part] = tokens_ref[half:, own_columns]
    shift_send[:, part:] = weights.astype(f32).astype(bf16)
    lanes = iota((8, LANES), 1)
    count_send[0] = jnp.where(lanes == me, rows - count, 0).astype(f32)

    pl.semaphore_wait(barrier, 17)
    shift.start()
    for mask in range(1, 8):
        counts_to(0, mask).start()

    normed = layer_norm(tokens_ref[...].astype(f32), gain_ref[...]).astype(bf16)
    metric = dot32(normed, key_w[...]).astype(bf16)
    metric_send[...] = metric[:half]
    metric_copy.start()

    for mask in range(1, 8):
        counts_to(0, mask).wait_recv()
    total = count_send[0]
    for mask in range(1, 8):
        total = total + count_recv[0, mask]
    count_send[1] = total
    for mask in range(1, 8):
        counts_to(1, mask).start()

    survive = jnp.concatenate([jnp.ones((1, half), f32), 1.0 - to_row(removed.astype(f32))], axis=1)
    upper = (iota((rows, rows), 0) < iota((rows, rows), 1)).astype(bf16)
    local_rank = dot32(jnp.broadcast_to(survive, (16, rows)).astype(bf16), upper)[:1].astype(jnp.int32)
    early_size = to_column(sizes_ref[:, :half]).astype(f32)

    shift.wait_recv()
    came = shift_recv[:, part:]
    added_size = dot32(came, jnp.ones((half, LANES), bf16), TN)[:, :1]
    added_rows = dot32(came, shift_recv[:, :part], TN)
    new_size = early_size + added_size
    merged = (early_size * tokens_ref[:half, own_columns].astype(f32) + added_rows) / new_size
    biases = jnp.log(jnp.concatenate([new_size, late_size.astype(f32)], axis=0))
    payload = jnp.concatenate(
        [
            jnp.concatenate([merged.astype(bf16), tokens_ref[half:, own_columns]], axis=0),
            jnp.where(iota((rows, LANES), 1) == 0, biases, 0.0).astype(bf16),
        ],
        axis=1,
    )

    for mask in range(1, 8):
        counts_to(1, mask).wait_recv()
    total = count_send[1]
    for mask in range(1, 8):
        total = total + count_recv[1, mask]
    counts = total[:1]
    before = dot32(
        total.astype(bf16), (iota((LANES, LANES), 0) < iota((LANES, LANES), 1)).astype(bf16)
    )[:1].astype(jnp.int32)
    shard_lane = iota((1, LANES), 1)
    start = jnp.sum(jnp.where(shard_lane == me, before, 0), axis=1, keepdims=True)
    everyone = jnp.sum(counts, axis=1, keepdims=True).astype(jnp.int32)
    owner_cube, owner_near = cube_and_near((start + local_rank) & (shards - 1))
    spot = owner_cube * 32 + owner_near * slots + (local_rank >> 6)
    spot = jnp.where(survive > 0, spot, rows)
    put = (spot == iota((rows, rows), 0)).astype(bf16)
    far_out[...] = dot32(put, payload).astype(bf16).reshape(far_out.shape)
    for mask in range(1, 8):
        far_copy(mask).start()
    own_far = pltpu.make_async_copy(far_out.at[cube_index()], far_in.at[cube_index()], local_sem.at[0])
    own_far.start()

    metric_copy.wait_recv()
    partner = metric_recv[...]
    own_keys = metric[half:]
    score_send[0] = dot32(own_keys, partner, NT)
    own_keys = own_keys.astype(f32)
    partner = partner.astype(f32)
    score_send[1] = jnp.broadcast_to(jnp.sum(own_keys * own_keys, axis=1, keepdims=True), (half, LANES))
    score_send[2] = jnp.broadcast_to(jnp.sum(partner * partner, axis=1, keepdims=True), (half, LANES))
    score_copy.start()

    own_far.wait()
    for mask in range(1, 8):
        far_copy(mask, True).wait_recv()
    line = iota((rows, rows), 0)
    turned = ((line // slots) % 8) * 32 + (line // 32) * slots + line % slots
    turn = (turned == iota((rows, rows), 1)).astype(bf16)
    near_out[...] = dot32(turn, far_in[...].reshape(rows, part + LANES)).astype(bf16).reshape(near_out.shape)
    for mask in range(1, 8):
        near_copy(mask).start()
    own_near = pltpu.make_async_copy(near_out.at[near_index()], near_in.at[near_index()], local_sem.at[1])
    own_near.start()

    wanted = iota((rows, LANES), 0) * shards + me
    from_cube, from_near = cube_and_near(shard_lane)
    mine = (before <= wanted) & (wanted < before + counts.astype(jnp.int32))
    fetch = jnp.sum(
        jnp.where(mine, from_near * 32 + from_cube * slots + ((wanted - before) >> 6), 0), axis=1, keepdims=True
    )
    filled = wanted[:, :1] < everyone
    take = ((fetch == iota((rows, rows), 1)) & filled).astype(bf16)
    total_ref[...] = jnp.broadcast_to(everyone, total_ref.shape)

    score_copy.wait_recv()
    sums = score_send[...] + score_recv[...]
    cosine = sums[0] * lax.rsqrt(sums[1] + epsilon) * to_row(lax.rsqrt(sums[2][:, :1] + epsilon))
    best_ref[...] = jnp.broadcast_to(to_row(jnp.max(cosine, axis=1, keepdims=True)), best_ref.shape)

    own_near.wait()
    for mask in range(1, 8):
        near_copy(mask, True).wait_recv()
    taken = dot32(take, near_in[...].reshape(rows, part + LANES))
    half_send[...] = taken[:, :part].astype(bf16)
    half_copy.start()
    balanced_ref[:, own_columns] = half_send[...]
    bias = jnp.where(filled, taken[:, part : part + 1], -9984.0) * LOG2E
    high = bias.astype(bf16).astype(f32)
    low = bias - high
    tile = iota((16, LANES), 0)
    tiles = jnp.zeros((16, LANES), f32)
    for i, column in enumerate((high[:half], high[half:], low[:half], low[half:])):
        tiles = jnp.where(tile == i, to_row(column), tiles)
    bias_ref[...] = tiles.astype(bf16)
    half_copy.wait_recv()
    balanced_ref[:, pl.ds(pl.multiple_of((1 - core) * part, part), part)] = half_recv[...]

    shift.wait_send()
    metric_copy.wait_send()
    score_copy.wait_send()
    half_copy.wait_send()
    for mask in range(1, 8):
        counts_to(0, mask).wait_send()
        counts_to(1, mask).wait_send()
        far_copy(mask).wait_send()
        near_copy(mask).wait_send()


def deal(tokens, sizes, source, target, count, gain, key_weight):
    rows, width = tokens.shape
    half, part = rows // 2, width // 2
    f32, bf16 = jnp.float32, jnp.bfloat16
    vmem = pl.BlockSpec(memory_space=pltpu.VMEM)
    dma = pltpu.SemaphoreType.DMA
    carried = part + LANES
    return pl.pallas_call(
        deal_kernel,
        in_specs=[vmem, vmem, vmem, vmem, pl.BlockSpec(memory_space=pltpu.SMEM), vmem,
                  pl.BlockSpec((None, width, key_weight.shape[2]), lambda i: (1, 0, 0))],
        grid=(1,),
        out_specs=[vmem] * 4,
        out_shape=[
            jax.ShapeDtypeStruct((rows, width), bf16),
            jax.ShapeDtypeStruct((16, LANES), bf16),
            jax.ShapeDtypeStruct((8, LANES), jnp.int32),
            jax.ShapeDtypeStruct((8, LANES), f32),
        ],
        scratch_shapes=[
            pltpu.VMEM((half, carried), bf16),
            pltpu.VMEM((half, carried), bf16),
            pltpu.VMEM((2, 8, LANES), f32),
            pltpu.VMEM((2, 8, 8, LANES), f32),
            pltpu.VMEM((half, key_weight.shape[2]), bf16),
            pltpu.VMEM((half, key_weight.shape[2]), bf16),
            pltpu.VMEM((3, half, LANES), f32),
            pltpu.VMEM((3, half, LANES), f32),
            pltpu.VMEM((8, rows // 8, carried), bf16),
            pltpu.VMEM((8, rows // 8, carried), bf16),
            pltpu.VMEM((8, rows // 8, carried), bf16),
            pltpu.VMEM((8, rows // 8, carried), bf16),
            pltpu.VMEM((rows, part), bf16),
            pltpu.VMEM((rows, part), bf16),
            dma((2,)),
            dma((2, 8)),
            dma((2, 8)),
            dma((2,)),
            dma((2,)),
            dma((8,)),
            dma((8,)),
            dma((8,)),
            dma((8,)),
            dma((2,)),
            dma((2,)),
        ],
        compiler_params=pltpu.CompilerParams(
            vmem_limit_bytes=32 * 2**20, collective_id=8, has_side_effects=True
        ),
        cost_estimate=pl.CostEstimate(flops=10**9, bytes_accessed=4 * 2**20, transcendentals=0),
    )(tokens, sizes, source, target, count, gain, key_weight)


def on_device(
    tokens,
    token_sizes,
    merge_source,
    merge_target,
    merge_count,
    attn_gain,
    qkv_weight,
    out_weight,
    mlp_gain,
    up_weight,
    down_weight,
):
    rows = tokens.shape[0]
    balanced, bias_tile, grand_total, best = deal(
        tokens, token_sizes[None, :], merge_source, merge_target, merge_count, attn_gain[None, :], qkv_weight
    )
    grand_total = grand_total[0, :1]
    shards = 64
    sizes = (192, 208, rows)
    needed = (grand_total[0] + shards - 1) // shards
    index = sum((needed > size).astype(jnp.int32) for size in sizes[:-1])
    merged_out = lax.switch(
        index,
        [functools.partial(layer, size, at + 1) for at, size in enumerate(sizes)],
        grand_total, balanced, bias_tile, attn_gain[None, :], mlp_gain[None, :],
        qkv_weight, out_weight, up_weight, down_weight,
    )
    return (merged_out, best[0])


def solution(mesh):
    placed = (
        P("seq", None),
        P("seq"),
        P("seq", None),
        P("seq", None),
        P("seq"),
        P(),
        P(None, None, "mp"),
        P("mp", None),
        P(),
        P(None, "mp"),
        P("mp", None),
    )
    return jax.shard_map(
        on_device, mesh=mesh, in_specs=placed, out_specs=(P("seq", None), P("seq")), check_vma=False
    )
```

```python
import functools
import math

import jax
import jax.numpy as jnp
from jax import lax
from jax.experimental import pallas as pl
from jax.experimental.pallas import tpu as pltpu
from jax.sharding import PartitionSpec as P

HEAD_DIM = 64
LANES = 128
epsilon = 1e-06
LOG2E = math.log2(math.e)
NT = (((1,), (1,)), ((), ()))
TN = (((0,), (0,)), ((), ()))
NN = (((1,), (0,)), ((), ()))


def layer_norm(values, gain_vector):
    center = values - jnp.mean(values, axis=-1, keepdims=True)
    spread = jnp.mean(center * center, axis=-1, keepdims=True)
    return center * lax.rsqrt(spread + epsilon) * gain_vector


def dot32(a, b, dims=NN):
    return lax.dot_general(a, b, dims, preferred_element_type=jnp.float32)


MESH = pl.DeviceIdType.MESH
ORDERS = ((1, 2, 4), (2, 4, 1), (4, 1, 2))
PARTS = ((0, 3), (3, 3), (6, 3))
STEP_OF = {0: 0, 1: 1, 2: 2, 4: 3, 3: 4, 5: 5, 6: 6, 7: 7}


def places():
    me = lax.axis_index("seq")
    return me // 16, me // 4 % 4, me % 4


def near(mask):
    z, y, x = places()
    if mask & 4:
        z = z + 1 - 2 * (z % 2)
    if mask & 2:
        y = y + 1 - 2 * (y % 2)
    if mask & 1:
        x = x + 1 - 2 * (x % 2)
    return z * 16 + y * 4 + x


def far(mask):
    z, y, x = places()
    if mask & 4:
        z = 3 - z
    if mask & 2:
        y = 3 - y
    if mask & 1:
        x = 3 - x
    return z * 16 + y * 4 + x


def cube_index(mask=0):
    z, y, x = places()
    z, y, x = z // 2, y // 2, x // 2
    if mask & 4:
        z = 1 - z
    if mask & 2:
        y = 1 - y
    if mask & 1:
        x = 1 - x
    return z * 4 + y * 2 + x


def layer_kernel(
    rows,
    dropped,
    online,
    total_ref,
    balanced_ref,
    bias_ref,
    attn_gain_ref,
    mlp_gain_ref,
    qkv_hbm,
    out_hbm,
    up_hbm,
    down_hbm,
    result_ref,
    plain_ref,
    qkv_w,
    out_w,
    up_w,
    down_w,
    kv_send,
    q_send,
    kv_buf,
    q_buf,
    tile_send,
    tile_buf,
    q_all,
    k2,
    v2,
    acc,
    peak,
    o_send,
    o_buf,
    part_send,
    part_recv,
    layer_one,
    norm_send,
    norm_recv,
    weight_sem,
    local_sem,
    spread_send,
    spread_recv,
    pass_send,
    pass_recv,
    back_send,
    back_recv,
    core_send,
    core_recv,
):
    core = lax.axis_index("mp")
    heads = 8
    upper = -(-rows // 32) * 16
    lower = rows - upper
    width = balanced_ref.shape[1]

    weight_copies = [
        pltpu.make_async_copy(src, dst, weight_sem.at[i])
        for i, (src, dst) in enumerate(((qkv_hbm, qkv_w), (out_hbm, out_w), (up_hbm, up_w), (down_hbm, down_w)))
    ]
    weight_copies[0].start()

    barrier = pltpu.get_barrier_semaphore()
    for mask in range(1, 8):
        pl.semaphore_signal(barrier, inc=1, device_id=(far(mask), core), device_id_type=MESH)
    for mask in (1, 2, 4):
        pl.semaphore_signal(barrier, inc=1, device_id=(near(mask), core), device_id_type=MESH)
    pl.semaphore_signal(barrier, inc=1, device_id=(lax.axis_index("seq"), 1 - core), device_id_type=MESH)

    balanced = balanced_ref[:rows].astype(jnp.float32)
    normed = layer_norm(balanced, attn_gain_ref[...]).astype(jnp.bfloat16)
    weight_copies[0].wait()
    for copy in weight_copies[1:]:
        copy.start()
    pl.semaphore_wait(barrier, 11)

    key = dot32(normed, qkv_w[1]).astype(jnp.bfloat16)
    value = dot32(normed, qkv_w[2]).astype(jnp.bfloat16)
    for j in range(heads):
        columns = slice(j * HEAD_DIM, (j + 1) * HEAD_DIM)
        kv_send[j] = jnp.concatenate([key[:, columns], value[:, columns]], axis=1)

    def spread_kv(mask):
        return pltpu.make_async_remote_copy(
            kv_send.at[cube_index(mask)], kv_buf.at[0, mask], spread_send.at[0, mask], spread_recv.at[0, mask],
            device_id=(far(mask), core), device_id_type=MESH,
        )

    def spread_q(mask):
        return pltpu.make_async_remote_copy(
            q_send.at[cube_index(mask)], q_buf.at[mask], spread_send.at[1, mask], spread_recv.at[1, mask],
            device_id=(far(mask), core), device_id_type=MESH,
        )

    def spread_tile(mask):
        return pltpu.make_async_remote_copy(
            tile_send, tile_buf.at[pl.ds(mask * 16, 16)], spread_send.at[2, mask], spread_recv.at[2, mask],
            device_id=(far(mask), core), device_id_type=MESH,
        )

    def pass_on(part, near_mask, slot):
        first, size = PARTS[part]
        target = STEP_OF[slot ^ near_mask]
        return pltpu.make_async_remote_copy(
            kv_buf.at[STEP_OF[slot], pl.ds(first, size)], kv_buf.at[target, pl.ds(first, size)],
            pass_send.at[part, target], pass_recv.at[part, target],
            device_id=(near(near_mask), core), device_id_type=MESH,
        )

    for mask in range(1, 8):
        spread_kv(mask).start()
    own_kv = pltpu.make_async_copy(kv_send.at[cube_index()], kv_buf.at[0, 0], local_sem.at[0])
    own_kv.start()
    query = (dot32(normed, qkv_w[0]) * (HEAD_DIM ** (-0.5) * LOG2E)).astype(jnp.bfloat16)
    for j in range(heads):
        mine = query[:, j * HEAD_DIM : (j + 1) * HEAD_DIM]
        other = mine[upper:]
        if lower < upper:
            other = jnp.concatenate([other, jnp.zeros((upper - lower, HEAD_DIM), jnp.bfloat16)], axis=0)
        q_send[j] = jnp.concatenate([mine[:upper], other], axis=1)
    for mask in range(1, 8):
        spread_q(mask).start()
    own_q = pltpu.make_async_copy(q_send.at[cube_index()], q_buf.at[0], local_sem.at[1])
    own_q.start()

    head_of = (
        iota((heads * HEAD_DIM, LANES), 0) // HEAD_DIM == iota((heads * HEAD_DIM, LANES), 1)
    ).astype(jnp.bfloat16)

    def widest(values):
        values = values.astype(jnp.float32)
        squares = dot32((values * values).astype(jnp.bfloat16), head_of)
        return jnp.max(jnp.max(squares, axis=1, keepdims=True), axis=0, keepdims=True)

    largest = jnp.max(
        jnp.max(jnp.abs(value.astype(jnp.float32)), axis=1, keepdims=True), axis=0, keepdims=True
    )
    tile = bias_ref[...].astype(jnp.float32)
    tile_row = iota((16, LANES), 0)
    for i, bound in ((4, widest(query)), (5, widest(key)), (6, largest)):
        tile = jnp.where(tile_row == i, jnp.minimum(bound * 1.02, 1e37), tile)
    tile_send[...] = tile.astype(jnp.bfloat16)
    for mask in range(1, 8):
        spread_tile(mask).start()
    tile_buf[:16] = tile_send[...]

    own_kv.wait()
    for mask in range(1, 8):
        spread_kv(mask).wait_recv()
    for order in range(3):
        for part in range(2):
            pass_on(part, ORDERS[part][order], 0).start()

    for mask in range(1, 8):
        spread_tile(mask).wait_recv()
    tiles = tile_buf[...]
    pick_row = iota((8 * 16, LANES), 0)
    pick_lane = iota((8 * 16, LANES), 1) - HEAD_DIM - pick_row // 16 * 2
    pick_row = pick_row % 16
    columns = jnp.concatenate(
        [
            dot32(
                tiles,
                (((pick_row == i) & (pick_lane == 0)) | ((pick_row == i + 2) & (pick_lane == 1))).astype(jnp.bfloat16),
                TN,
            )
            for i in range(2)
        ],
        axis=0,
    )[:rows]
    lane = iota((rows, LANES), 1)
    tiles = tiles.astype(jnp.float32)
    for i in (4, 5, 6):
        bound = jnp.max(jnp.where(pick_row == i, tiles, 0.0), axis=0, keepdims=True)
        columns = jnp.where(lane == 96 + i, bound, columns)
    kv_buf[0, heads] = columns.astype(jnp.bfloat16)
    for order in range(3):
        pass_on(2, ORDERS[2][order], 0).start()

    own_q.wait()
    for mask in range(1, 8):
        spread_q(mask).wait_recv()
    queries = heads * rows
    cut = queries // 2 // 256 * 256
    q_lane = iota((upper, LANES), 1)
    q_tail = ((q_lane >= HEAD_DIM) & (q_lane < HEAD_DIM + 16)).astype(jnp.bfloat16)
    for a in range(heads):
        both = q_buf[a]
        other = jnp.concatenate([both[:, HEAD_DIM:], q_tail[:, HEAD_DIM:]], axis=1)
        q_all[a * rows : a * rows + upper, :] = jnp.where(q_lane < HEAD_DIM, both, q_tail)
        q_all[a * rows + upper : (a + 1) * rows, :] = other[:lower]

    empty = -9984.0 * LOG2E
    head = jnp.where(
        iota((8, queries), 0) == 0,
        float(dropped) if online else float(dropped) * jnp.exp2(jnp.full((8, queries), empty, jnp.float32)),
        0.0,
    )
    acc[...] = jnp.zeros_like(acc)
    acc[:8, :] = head
    peak[...] = jnp.full(peak.shape, empty if dropped else -3e38, jnp.float32)
    zero = jnp.zeros((), jnp.bfloat16)
    value_head = (lane == 0).astype(jnp.bfloat16)

    def step(i, carry):
        for slot, at in STEP_OF.items():
            if slot == 0:
                continue

            @pl.when(i == at)
            def _(slot=slot):
                for part in range(3):
                    d1, d2, d3 = ORDERS[part]
                    came_by = d3 if slot & d3 else d2 if slot & d2 else d1
                    pass_on(part, came_by, slot ^ came_by).wait_recv()
                    if came_by == d1:
                        pass_on(part, d2, slot).start()
                    if came_by != d3:
                        pass_on(part, d3, slot).start()

        columns = kv_buf[i, heads]
        for a in range(heads):
            kv = kv_buf[i, a]
            bias = jnp.where((lane - HEAD_DIM) // 2 == a, columns, zero)
            k2[a * rows : (a + 1) * rows, :] = jnp.where(lane < HEAD_DIM, kv, bias)
            v2[a * rows : (a + 1) * rows, :] = jnp.where(lane < HEAD_DIM, value_head, kv)
        for begin, end in ((0, cut), (cut, queries)):
            s = dot32(k2[...], q_all[begin:end, :], NT)
            if online:
                old = peak[:, begin:end]
                new = jnp.maximum(old, jnp.max(s, axis=0, keepdims=True))
                p = jnp.exp2(s - new).astype(jnp.bfloat16)
                peak[:, begin:end] = new
                acc[:, begin:end] = acc[:, begin:end] * jnp.exp2(old - new) + dot32(v2[...], p, TN)
            else:
                p = jnp.exp2(s).astype(jnp.bfloat16)
                acc[:, begin:end] += dot32(v2[...], p, TN)
        return carry

    lax.fori_loop(0, 8, step, 0)

    def back(mask):
        return pltpu.make_async_remote_copy(
            o_send.at[mask], o_buf.at[cube_index()], back_send.at[mask], back_recv.at[mask],
            device_id=(far(mask), core), device_id_type=MESH,
        )

    def back_in(mask):
        return pltpu.make_async_remote_copy(
            o_send.at[mask], o_buf.at[cube_index(mask)], back_send.at[mask], back_recv.at[mask],
            device_id=(far(mask), core), device_id_type=MESH,
        )

    scaled = (acc[...] / acc[:1, :]).T.astype(jnp.bfloat16)
    for a in range(heads):
        first = scaled[a * rows : a * rows + upper, HEAD_DIM:]
        other = scaled[a * rows + upper : (a + 1) * rows, HEAD_DIM:]
        if lower < upper:
            other = jnp.concatenate([other, jnp.zeros((upper - lower, HEAD_DIM), jnp.bfloat16)], axis=0)
        o_send[a] = jnp.concatenate([first, other], axis=1)
    for mask in range(1, 8):
        back(mask).start()
    own_o = pltpu.make_async_copy(o_send.at[0], o_buf.at[cube_index()], local_sem.at[2])
    own_o.start()
    weight_copies[1].wait()
    own_o.wait()
    for mask in range(1, 8):
        back_in(mask).wait_recv()

    def swap(which, size):
        return pltpu.make_async_remote_copy(
            part_send.at[which], part_recv.at[which], core_send.at[which], core_recv.at[which],
            device_id=(lax.axis_index("seq"), 1 - core), device_id_type=MESH,
        )

    mixed = jnp.concatenate(
        [
            jnp.concatenate([o_buf[j, :, :HEAD_DIM] for j in range(heads)], axis=1),
            jnp.concatenate([o_buf[j, :lower, HEAD_DIM:] for j in range(heads)], axis=1),
        ],
        axis=0,
    )
    part_send[0] = dot32(mixed, out_w[...]).astype(jnp.bfloat16)
    swap(0, rows).start()
    bounds = kv_buf[0, heads, :16, :].astype(jnp.float32)
    for i in range(1, 8):
        bounds = jnp.maximum(bounds, kv_buf[i, heads, :16, :].astype(jnp.float32))
    norm_send[...] = bounds
    norm_swap = pltpu.make_async_remote_copy(
        norm_send, norm_recv, core_send.at[2], core_recv.at[2],
        device_id=(lax.axis_index("seq"), 1 - core), device_id_type=MESH,
    )
    norm_swap.start()
    swap(0, rows).wait_recv()
    attention = part_send[0].astype(jnp.float32) + part_recv[0].astype(jnp.float32)
    layer_one[...] = (balanced_ref[:rows].astype(jnp.float32) + attention).astype(jnp.bfloat16)
    normed_mlp = layer_norm(layer_one[...].astype(jnp.float32), mlp_gain_ref[...]).astype(jnp.bfloat16)
    weight_copies[2].wait()
    weight_copies[3].wait()
    hidden = dot32(normed_mlp, up_w[...])
    hidden = (0.5 * hidden * (1.0 + lax.erf(hidden * math.sqrt(0.5)))).astype(jnp.bfloat16)
    part_send[1] = dot32(hidden, down_w[...]).astype(jnp.bfloat16)
    swap(1, rows).start()
    swap(1, rows).wait_recv()
    mlp = part_send[1].astype(jnp.float32) + part_recv[1].astype(jnp.float32)
    result = layer_one[...].astype(jnp.float32) + mlp
    norm_swap.wait_recv()
    bounds = jnp.maximum(norm_send[:8], norm_recv[:8])
    plain = (bounds[:, 100:101] * bounds[:, 101:102] <= 68.0 * 68.0) & (bounds[:, 102:103] <= 2.0**30)
    plain_ref[...] = jnp.broadcast_to(jnp.where(plain, 1, 0), plain_ref.shape)
    slot = lax.broadcasted_iota(jnp.int32, (rows, width), 0) * 64 + lax.axis_index("seq")
    result_ref[:rows, :] = jnp.where(slot < total_ref[0], result, 0.0).astype(jnp.bfloat16)
    if rows < result_ref.shape[0]:
        result_ref[rows:, :] = jnp.zeros((result_ref.shape[0] - rows, width), jnp.bfloat16)

    for mask in range(1, 8):
        spread_kv(mask).wait_send()
        spread_q(mask).wait_send()
        spread_tile(mask).wait_send()
        back(mask).wait_send()
    for part in range(3):
        d1, d2, d3 = ORDERS[part]
        for near_mask, slot in ((d1, 0), (d2, 0), (d3, 0), (d2, d1), (d3, d1), (d3, d2), (d3, d1 | d2)):
            pass_on(part, near_mask, slot).wait_send()
    swap(0, rows).wait_send()
    swap(1, rows).wait_send()
    norm_swap.wait_send()


def layer(rows, which, online, total, balanced, bias_tile, attn_gain, mlp_gain, qkv_weight, out_weight, up_weight, down_weight):
    total_rows, width = balanced.shape
    heads = 8
    hidden = up_weight.shape[1]
    queries = heads * rows
    packed = -(-rows // 32) * 16
    bf16 = jnp.bfloat16
    vmem = pl.BlockSpec(memory_space=pltpu.VMEM)
    anywhere = pl.BlockSpec(memory_space=pl.ANY)
    dma = pltpu.SemaphoreType.DMA
    return pl.pallas_call(
        functools.partial(layer_kernel, rows, 64 * (total_rows - rows), online),
        in_specs=[pl.BlockSpec(memory_space=pltpu.SMEM), vmem, vmem, vmem, vmem] + [anywhere] * 4,
        out_specs=[vmem, vmem],
        out_shape=[
            jax.ShapeDtypeStruct((total_rows, width), bf16),
            jax.ShapeDtypeStruct((8, LANES), jnp.int32),
        ],
        scratch_shapes=[
            pltpu.VMEM(qkv_weight.shape, bf16),
            pltpu.VMEM(out_weight.shape, bf16),
            pltpu.VMEM(up_weight.shape, bf16),
            pltpu.VMEM(down_weight.shape, bf16),
            pltpu.VMEM((heads, rows, LANES), bf16),
            pltpu.VMEM((heads, packed, LANES), bf16),
            pltpu.VMEM((8, heads + 1, rows, LANES), bf16),
            pltpu.VMEM((heads, packed, LANES), bf16),
            pltpu.VMEM((16, LANES), bf16),
            pltpu.VMEM((8 * 16, LANES), bf16),
            pltpu.VMEM((queries, LANES), bf16),
            pltpu.VMEM((queries, LANES), bf16),
            pltpu.VMEM((queries, LANES), bf16),
            pltpu.VMEM((LANES, queries), jnp.float32),
            pltpu.VMEM((1, queries), jnp.float32),
            pltpu.VMEM((heads, packed, LANES), bf16),
            pltpu.VMEM((heads, packed, LANES), bf16),
            pltpu.VMEM((2, rows, width), bf16),
            pltpu.VMEM((2, rows, width), bf16),
            pltpu.VMEM((rows, width), bf16),
            pltpu.VMEM((16, LANES), jnp.float32),
            pltpu.VMEM((16, LANES), jnp.float32),
            dma((4,)),
            dma((3,)),
            dma((3, 8)),
            dma((3, 8)),
            dma((3, 8)),
            dma((3, 8)),
            dma((8,)),
            dma((8,)),
            dma((3,)),
            dma((3,)),
        ],
        compiler_params=pltpu.CompilerParams(
            vmem_limit_bytes=60 * 2**20, collective_id=which, has_side_effects=True
        ),
        cost_estimate=pl.CostEstimate(
            flops=queries * queries * 8 * 256, bytes_accessed=16 * 2**20, transcendentals=queries * queries * 8
        ),
    )(total, balanced, bias_tile, attn_gain, mlp_gain, qkv_weight, out_weight, up_weight, down_weight)


def near_index(mask=0):
    z, y, x = places()
    bits = [(c // 2 + c % 2) % 2 for c in (z, y, x)]
    bits = [1 - b if mask & m else b for b, m in zip(bits, (4, 2, 1))]
    return bits[0] * 4 + bits[1] * 2 + bits[2]


def cube_and_near(shard):
    parts = (shard >> 4, (shard >> 2) & 3, shard & 3)
    cube = sum((c >> 1) * m for c, m in zip(parts, (4, 2, 1)))
    near = sum(((c >> 1) ^ (c & 1)) * m for c, m in zip(parts, (4, 2, 1)))
    return cube, near


def iota(shape, dim):
    return lax.broadcasted_iota(jnp.int32, shape, dim)


def to_column(row):
    n = row.shape[1]
    return jnp.sum(jnp.where(iota((n, n), 0) == iota((n, n), 1), row, 0), axis=1, keepdims=True)


def to_row(column):
    n = column.shape[0]
    return jnp.sum(jnp.where(iota((n, n), 0) == iota((n, n), 1), column, 0), axis=0, keepdims=True)


def deal_kernel(
    tokens_ref,
    sizes_ref,
    source_ref,
    target_ref,
    count_ref,
    gain_ref,
    key_w,
    balanced_ref,
    bias_ref,
    total_ref,
    best_ref,
    shift_send,
    shift_recv,
    count_send,
    count_recv,
    metric_send,
    metric_recv,
    score_send,
    score_recv,
    far_out,
    far_in,
    near_out,
    near_in,
    half_send,
    half_recv,
    shift_sem,
    count_send_sem,
    count_recv_sem,
    metric_sem,
    score_sem,
    far_send_sem,
    far_recv_sem,
    near_send_sem,
    near_recv_sem,
    half_sem,
    local_sem,
):
    me = lax.axis_index("seq")
    core = lax.axis_index("mp")
    shards = 64
    rows, width = tokens_ref.shape
    half = rows // 2
    part = width // 2
    slots = rows // shards
    ahead, behind = (me + 1) % shards, (me + shards - 1) % shards
    own_columns = pl.ds(pl.multiple_of(core * part, part), part)
    f32, bf16 = jnp.float32, jnp.bfloat16

    barrier = pltpu.get_barrier_semaphore()
    for mask in range(1, 8):
        pl.semaphore_signal(barrier, inc=1, device_id=(far(mask), core), device_id_type=MESH)
        pl.semaphore_signal(barrier, inc=1, device_id=(near(mask), core), device_id_type=MESH)
    for other in (ahead, behind):
        pl.semaphore_signal(barrier, inc=1, device_id=(other, core), device_id_type=MESH)
    pl.semaphore_signal(barrier, inc=1, device_id=(me, 1 - core), device_id_type=MESH)

    def remote(src, dst, send_sem, recv_sem, seq, mp):
        return pltpu.make_async_remote_copy(
            src, dst, send_sem, recv_sem, device_id=(seq, mp), device_id_type=MESH
        )

    shift = remote(shift_send, shift_recv, shift_sem.at[0], shift_sem.at[1], ahead, core)
    metric_copy = remote(metric_send, metric_recv, metric_sem.at[0], metric_sem.at[1], behind, core)
    score_copy = remote(score_send, score_recv, score_sem.at[0], score_sem.at[1], me, 1 - core)
    half_copy = remote(half_send, half_recv, half_sem.at[0], half_sem.at[1], me, 1 - core)

    def counts_to(stage, mask):
        return remote(
            count_send.at[stage], count_recv.at[stage, mask], count_send_sem.at[stage, mask],
            count_recv_sem.at[stage, mask], (far, near)[stage](mask), core,
        )

    def far_copy(mask, landed=False):
        return remote(
            far_out.at[cube_index(mask)], far_in.at[cube_index(mask) if landed else cube_index()],
            far_send_sem.at[mask], far_recv_sem.at[mask], far(mask), core,
        )

    def near_copy(mask, landed=False):
        return remote(
            near_out.at[near_index(mask)], near_in.at[near_index(mask) if landed else near_index()],
            near_send_sem.at[mask], near_recv_sem.at[mask], near(mask), core,
        )

    count = count_ref[0]
    active = iota((1, half), 1) < count
    hit = (source_ref[...] == iota((half, half), 0)) & active
    removed = jnp.max(jnp.where(hit, 1, 0), axis=1, keepdims=True)
    goal = jnp.sum(jnp.where(hit, target_ref[...], 0), axis=1, keepdims=True)
    late_size = to_column(sizes_ref[:, half:])
    weights = jnp.where((goal == iota((half, half), 1)) & (removed > 0), late_size, 0)
    shift_send[:, :part] = tokens_ref[half:, own_columns]
    shift_send[:, part:] = weights.astype(f32).astype(bf16)
    lanes = iota((8, LANES), 1)
    count_send[0] = jnp.where(lanes == me, rows - count, 0).astype(f32)

    pl.semaphore_wait(barrier, 17)
    shift.start()
    for mask in range(1, 8):
        counts_to(0, mask).start()

    normed = layer_norm(tokens_ref[...].astype(f32), gain_ref[...]).astype(bf16)
    metric = dot32(normed, key_w[...]).astype(bf16)
    metric_send[...] = metric[:half]
    metric_copy.start()

    for mask in range(1, 8):
        counts_to(0, mask).wait_recv()
    total = count_send[0]
    for mask in range(1, 8):
        total = total + count_recv[0, mask]
    count_send[1] = total
    for mask in range(1, 8):
        counts_to(1, mask).start()

    survive = jnp.concatenate([jnp.ones((1, half), f32), 1.0 - to_row(removed.astype(f32))], axis=1)
    upper = (iota((rows, rows), 0) < iota((rows, rows), 1)).astype(bf16)
    local_rank = dot32(jnp.broadcast_to(survive, (16, rows)).astype(bf16), upper)[:1].astype(jnp.int32)
    early_size = to_column(sizes_ref[:, :half]).astype(f32)

    shift.wait_recv()
    came = shift_recv[:, part:]
    added_size = dot32(came, jnp.ones((half, LANES), bf16), TN)[:, :1]
    added_rows = dot32(came, shift_recv[:, :part], TN)
    new_size = early_size + added_size
    merged = (early_size * tokens_ref[:half, own_columns].astype(f32) + added_rows) / new_size
    biases = jnp.log(jnp.concatenate([new_size, late_size.astype(f32)], axis=0))
    payload = jnp.concatenate(
        [
            jnp.concatenate([merged.astype(bf16), tokens_ref[half:, own_columns]], axis=0),
            jnp.where(iota((rows, LANES), 1) == 0, biases, 0.0).astype(bf16),
        ],
        axis=1,
    )

    for mask in range(1, 8):
        counts_to(1, mask).wait_recv()
    total = count_send[1]
    for mask in range(1, 8):
        total = total + count_recv[1, mask]
    counts = total[:1]
    before = dot32(
        total.astype(bf16), (iota((LANES, LANES), 0) < iota((LANES, LANES), 1)).astype(bf16)
    )[:1].astype(jnp.int32)
    shard_lane = iota((1, LANES), 1)
    start = jnp.sum(jnp.where(shard_lane == me, before, 0), axis=1, keepdims=True)
    everyone = jnp.sum(counts, axis=1, keepdims=True).astype(jnp.int32)
    owner_cube, owner_near = cube_and_near((start + local_rank) & (shards - 1))
    spot = owner_cube * 32 + owner_near * slots + (local_rank >> 6)
    spot = jnp.where(survive > 0, spot, rows)
    put = (spot == iota((rows, rows), 0)).astype(bf16)
    far_out[...] = dot32(put, payload).astype(bf16).reshape(far_out.shape)
    for mask in range(1, 8):
        far_copy(mask).start()
    own_far = pltpu.make_async_copy(far_out.at[cube_index()], far_in.at[cube_index()], local_sem.at[0])
    own_far.start()

    metric_copy.wait_recv()
    partner = metric_recv[...]
    own_keys = metric[half:]
    score_send[0] = dot32(own_keys, partner, NT)
    own_keys = own_keys.astype(f32)
    partner = partner.astype(f32)
    score_send[1] = jnp.broadcast_to(jnp.sum(own_keys * own_keys, axis=1, keepdims=True), (half, LANES))
    score_send[2] = jnp.broadcast_to(jnp.sum(partner * partner, axis=1, keepdims=True), (half, LANES))
    score_copy.start()

    own_far.wait()
    for mask in range(1, 8):
        far_copy(mask, True).wait_recv()
    line = iota((rows, rows), 0)
    turned = ((line // slots) % 8) * 32 + (line // 32) * slots + line % slots
    turn = (turned == iota((rows, rows), 1)).astype(bf16)
    near_out[...] = dot32(turn, far_in[...].reshape(rows, part + LANES)).astype(bf16).reshape(near_out.shape)
    for mask in range(1, 8):
        near_copy(mask).start()
    own_near = pltpu.make_async_copy(near_out.at[near_index()], near_in.at[near_index()], local_sem.at[1])
    own_near.start()

    wanted = iota((rows, LANES), 0) * shards + me
    from_cube, from_near = cube_and_near(shard_lane)
    mine = (before <= wanted) & (wanted < before + counts.astype(jnp.int32))
    fetch = jnp.sum(
        jnp.where(mine, from_near * 32 + from_cube * slots + ((wanted - before) >> 6), 0), axis=1, keepdims=True
    )
    filled = wanted[:, :1] < everyone
    take = ((fetch == iota((rows, rows), 1)) & filled).astype(bf16)
    total_ref[...] = jnp.broadcast_to(everyone, total_ref.shape)

    score_copy.wait_recv()
    sums = score_send[...] + score_recv[...]
    cosine = sums[0] * lax.rsqrt(sums[1] + epsilon) * to_row(lax.rsqrt(sums[2][:, :1] + epsilon))
    best_ref[...] = jnp.broadcast_to(to_row(jnp.max(cosine, axis=1, keepdims=True)), best_ref.shape)

    own_near.wait()
    for mask in range(1, 8):
        near_copy(mask, True).wait_recv()
    taken = dot32(take, near_in[...].reshape(rows, part + LANES))
    half_send[...] = taken[:, :part].astype(bf16)
    half_copy.start()
    balanced_ref[:, own_columns] = half_send[...]
    bias = jnp.where(filled, taken[:, part : part + 1], -9984.0) * LOG2E
    high = bias.astype(bf16).astype(f32)
    low = bias - high
    tile = iota((16, LANES), 0)
    tiles = jnp.zeros((16, LANES), f32)
    for i, column in enumerate((high[:half], high[half:], low[:half], low[half:])):
        tiles = jnp.where(tile == i, to_row(column), tiles)
    bias_ref[...] = tiles.astype(bf16)
    half_copy.wait_recv()
    balanced_ref[:, pl.ds(pl.multiple_of((1 - core) * part, part), part)] = half_recv[...]

    shift.wait_send()
    metric_copy.wait_send()
    score_copy.wait_send()
    half_copy.wait_send()
    for mask in range(1, 8):
        counts_to(0, mask).wait_send()
        counts_to(1, mask).wait_send()
        far_copy(mask).wait_send()
        near_copy(mask).wait_send()


def deal(tokens, sizes, source, target, count, gain, key_weight):
    rows, width = tokens.shape
    half, part = rows // 2, width // 2
    f32, bf16 = jnp.float32, jnp.bfloat16
    vmem = pl.BlockSpec(memory_space=pltpu.VMEM)
    dma = pltpu.SemaphoreType.DMA
    carried = part + LANES
    return pl.pallas_call(
        deal_kernel,
        in_specs=[vmem, vmem, vmem, vmem, pl.BlockSpec(memory_space=pltpu.SMEM), vmem,
                  pl.BlockSpec((None, width, key_weight.shape[2]), lambda i: (1, 0, 0))],
        grid=(1,),
        out_specs=[vmem] * 4,
        out_shape=[
            jax.ShapeDtypeStruct((rows, width), bf16),
            jax.ShapeDtypeStruct((16, LANES), bf16),
            jax.ShapeDtypeStruct((8, LANES), jnp.int32),
            jax.ShapeDtypeStruct((8, LANES), f32),
        ],
        scratch_shapes=[
            pltpu.VMEM((half, carried), bf16),
            pltpu.VMEM((half, carried), bf16),
            pltpu.VMEM((2, 8, LANES), f32),
            pltpu.VMEM((2, 8, 8, LANES), f32),
            pltpu.VMEM((half, key_weight.shape[2]), bf16),
            pltpu.VMEM((half, key_weight.shape[2]), bf16),
            pltpu.VMEM((3, half, LANES), f32),
            pltpu.VMEM((3, half, LANES), f32),
            pltpu.VMEM((8, rows // 8, carried), bf16),
            pltpu.VMEM((8, rows // 8, carried), bf16),
            pltpu.VMEM((8, rows // 8, carried), bf16),
            pltpu.VMEM((8, rows // 8, carried), bf16),
            pltpu.VMEM((rows, part), bf16),
            pltpu.VMEM((rows, part), bf16),
            dma((2,)),
            dma((2, 8)),
            dma((2, 8)),
            dma((2,)),
            dma((2,)),
            dma((8,)),
            dma((8,)),
            dma((8,)),
            dma((8,)),
            dma((2,)),
            dma((2,)),
        ],
        compiler_params=pltpu.CompilerParams(
            vmem_limit_bytes=32 * 2**20, collective_id=8, has_side_effects=True
        ),
        cost_estimate=pl.CostEstimate(flops=10**9, bytes_accessed=4 * 2**20, transcendentals=0),
    )(tokens, sizes, source, target, count, gain, key_weight)


def on_device(
    tokens,
    token_sizes,
    merge_source,
    merge_target,
    merge_count,
    attn_gain,
    qkv_weight,
    out_weight,
    mlp_gain,
    up_weight,
    down_weight,
):
    rows = tokens.shape[0]
    balanced, bias_tile, grand_total, best = deal(
        tokens, token_sizes[None, :], merge_source, merge_target, merge_count, attn_gain[None, :], qkv_weight
    )
    grand_total = grand_total[0, :1]
    shards = 64
    sizes = (192, 208, rows)
    needed = (grand_total[0] + shards - 1) // shards
    index = sum((needed > size).astype(jnp.int32) for size in sizes[:-1])
    operands = (
        grand_total, balanced, bias_tile, attn_gain[None, :], mlp_gain[None, :],
        qkv_weight, out_weight, up_weight, down_weight,
    )
    merged_out, plain = lax.switch(
        index, [functools.partial(layer, size, at + 1, False) for at, size in enumerate(sizes)], *operands
    )
    merged_out = lax.cond(
        plain[0, 0] == 1, lambda done, *_: done, lambda _, *given: layer(rows, 9, True, *given)[0], merged_out, *operands
    )
    return (merged_out, best[0])


def solution(mesh):
    placed = (
        P("seq", None),
        P("seq"),
        P("seq", None),
        P("seq", None),
        P("seq"),
        P(),
        P(None, None, "mp"),
        P("mp", None),
        P(),
        P(None, "mp"),
        P("mp", None),
    )
    return jax.shard_map(
        on_device, mesh=mesh, in_specs=placed, out_specs=(P("seq", None), P("seq")), check_vma=False
    )
```

```python
import functools
import math

import jax
import jax.numpy as jnp
from jax import lax
from jax.experimental import pallas as pl
from jax.experimental.pallas import tpu as pltpu
from jax.sharding import PartitionSpec as P

HEAD_DIM = 64
LANES = 128
epsilon = 1e-06
LOG2E = math.log2(math.e)
NT = (((1,), (1,)), ((), ()))
TN = (((0,), (0,)), ((), ()))
NN = (((1,), (0,)), ((), ()))


def layer_norm(values, gain_vector):
    center = values - jnp.mean(values, axis=-1, keepdims=True)
    spread = jnp.mean(center * center, axis=-1, keepdims=True)
    return center * lax.rsqrt(spread + epsilon) * gain_vector


def dot32(a, b, dims=NN):
    return lax.dot_general(a, b, dims, preferred_element_type=jnp.float32)


MESH = pl.DeviceIdType.MESH
ORDERS = ((1, 2, 4), (2, 4, 1), (4, 1, 2))
PARTS = ((0, 3), (3, 3), (6, 2))
CAME = {1: (0, 0), 2: (1, 0), 3: (2, 0), 4: (1, 1), 5: (2, 1), 6: (2, 2), 7: (2, 4)}


def places():
    me = lax.axis_index("seq")
    return me // 16, me // 4 % 4, me % 4


def near(mask):
    z, y, x = places()
    if mask & 4:
        z = z + 1 - 2 * (z % 2)
    if mask & 2:
        y = y + 1 - 2 * (y % 2)
    if mask & 1:
        x = x + 1 - 2 * (x % 2)
    return z * 16 + y * 4 + x


def far(mask):
    z, y, x = places()
    if mask & 4:
        z = 3 - z
    if mask & 2:
        y = 3 - y
    if mask & 1:
        x = 3 - x
    return z * 16 + y * 4 + x


def cube_index(mask=0):
    z, y, x = places()
    z, y, x = z // 2, y // 2, x // 2
    if mask & 4:
        z = 1 - z
    if mask & 2:
        y = 1 - y
    if mask & 1:
        x = 1 - x
    return z * 4 + y * 2 + x


def layer_kernel(
    rows,
    dropped,
    online,
    total_ref,
    balanced_ref,
    bias_ref,
    attn_gain_ref,
    mlp_gain_ref,
    qkv_hbm,
    out_hbm,
    up_hbm,
    down_hbm,
    result_ref,
    plain_ref,
    qkv_w,
    out_w,
    up_w,
    down_w,
    kv_send,
    q_send,
    kv_buf,
    q_buf,
    tile_send,
    q_all,
    k2,
    v2,
    acc,
    peak,
    o_send,
    o_buf,
    part_send,
    part_recv,
    layer_one,
    hidden_buf,
    norm_send,
    norm_recv,
    weight_sem,
    local_sem,
    spread_send,
    spread_recv,
    pass_send,
    pass_recv,
    back_send,
    back_recv,
    core_send,
    core_recv,
):
    core = lax.axis_index("mp")
    heads = 8
    upper = -(-rows // 32) * 16
    lower = rows - upper
    width = balanced_ref.shape[1]

    weight_copies = [
        pltpu.make_async_copy(src, dst, weight_sem.at[i])
        for i, (src, dst) in enumerate(((qkv_hbm, qkv_w), (out_hbm, out_w), (up_hbm, up_w), (down_hbm, down_w)))
    ]
    weight_copies[0].start()

    barrier = pltpu.get_barrier_semaphore()
    for mask in range(1, 8):
        pl.semaphore_signal(barrier, inc=1, device_id=(far(mask), core), device_id_type=MESH)
    for mask in (1, 2, 4):
        pl.semaphore_signal(barrier, inc=1, device_id=(near(mask), core), device_id_type=MESH)
    pl.semaphore_signal(barrier, inc=1, device_id=(lax.axis_index("seq"), 1 - core), device_id_type=MESH)

    balanced = balanced_ref[:rows].astype(jnp.float32)
    normed = layer_norm(balanced, attn_gain_ref[...]).astype(jnp.bfloat16)
    weight_copies[0].wait()
    for copy in weight_copies[1:]:
        copy.start()
    pl.semaphore_wait(barrier, 11)

    key = dot32(normed, qkv_w[1]).astype(jnp.bfloat16)
    value = dot32(normed, qkv_w[2]).astype(jnp.bfloat16)
    for j in range(heads):
        columns = slice(j * HEAD_DIM, (j + 1) * HEAD_DIM)
        kv_send[j] = jnp.concatenate([key[:, columns], value[:, columns]], axis=1)

    def spread_kv(mask):
        return pltpu.make_async_remote_copy(
            kv_send.at[cube_index(mask)], kv_buf.at[0, mask, pl.ds(0, rows)], spread_send.at[0, mask], spread_recv.at[0, mask],
            device_id=(far(mask), core), device_id_type=MESH,
        )

    def spread_q(mask):
        return pltpu.make_async_remote_copy(
            q_send.at[cube_index(mask)], q_buf.at[mask], spread_send.at[1, mask], spread_recv.at[1, mask],
            device_id=(far(mask), core), device_id_type=MESH,
        )

    def spread_tile(mask):
        return pltpu.make_async_remote_copy(
            tile_send, kv_buf.at[0, mask, pl.ds(rows, 16)], spread_send.at[2, mask], spread_recv.at[2, mask],
            device_id=(far(mask), core), device_id_type=MESH,
        )

    def pass_on(part, target):
        first, size = PARTS[part]
        order, place = CAME[target]
        return pltpu.make_async_remote_copy(
            kv_buf.at[place, pl.ds(first, size)], kv_buf.at[target, pl.ds(first, size)],
            pass_send.at[part, target], pass_recv.at[part, target],
            device_id=(near(ORDERS[part][order]), core), device_id_type=MESH,
        )

    for mask in range(1, 8):
        spread_kv(mask).start()
    own_kv = pltpu.make_async_copy(kv_send.at[cube_index()], kv_buf.at[0, 0, pl.ds(0, rows)], local_sem.at[0])
    own_kv.start()
    query = (dot32(normed, qkv_w[0]) * (HEAD_DIM ** (-0.5) * LOG2E)).astype(jnp.bfloat16)
    for j in range(heads):
        mine = query[:, j * HEAD_DIM : (j + 1) * HEAD_DIM]
        other = mine[upper:]
        if lower < upper:
            other = jnp.concatenate([other, jnp.zeros((upper - lower, HEAD_DIM), jnp.bfloat16)], axis=0)
        q_send[j] = jnp.concatenate([mine[:upper], other], axis=1)
    for mask in range(1, 8):
        spread_q(mask).start()
    own_q = pltpu.make_async_copy(q_send.at[cube_index()], q_buf.at[0], local_sem.at[1])
    own_q.start()

    head_of = (
        iota((heads * HEAD_DIM, LANES), 0) // HEAD_DIM == iota((heads * HEAD_DIM, LANES), 1)
    ).astype(jnp.bfloat16)

    def widest(values):
        values = values.astype(jnp.float32)
        squares = dot32((values * values).astype(jnp.bfloat16), head_of)
        return jnp.max(jnp.max(squares, axis=1, keepdims=True), axis=0, keepdims=True)

    largest = jnp.max(
        jnp.max(jnp.abs(value.astype(jnp.float32)), axis=1, keepdims=True), axis=0, keepdims=True
    )
    tile = bias_ref[...].astype(jnp.float32)
    tile_row = iota((16, LANES), 0)
    for i, bound in ((4, widest(query)), (5, widest(key)), (6, largest)):
        tile = jnp.where(tile_row == i, jnp.minimum(bound * 1.02, 1e37), tile)
    tile_send[...] = tile.astype(jnp.bfloat16)
    for mask in range(1, 8):
        spread_tile(mask).start()
    kv_buf[0, 0, rows:, :] = tile_send[...]

    own_kv.wait()
    for mask in range(1, 8):
        spread_kv(mask).wait_recv()
        spread_tile(mask).wait_recv()
    for target in (1, 2, 3):
        for part in range(3):
            pass_on(part, target).start()

    pick_row = iota((8 * 16, LANES), 0)
    pick_lane = iota((8 * 16, LANES), 1) - HEAD_DIM - pick_row // 16 * 2
    pick_row = pick_row % 16
    picks = [
        (((pick_row == i) & (pick_lane == 0)) | ((pick_row == i + 2) & (pick_lane == 1))).astype(jnp.bfloat16)
        for i in range(2)
    ]
    lane = iota((rows, LANES), 1)

    own_q.wait()
    for mask in range(1, 8):
        spread_q(mask).wait_recv()
    queries = heads * rows
    cut = queries // 2 // 256 * 256
    q_lane = iota((upper, LANES), 1)
    q_tail = ((q_lane >= HEAD_DIM) & (q_lane < HEAD_DIM + 16)).astype(jnp.bfloat16)
    for a in range(heads):
        both = q_buf[a]
        other = jnp.concatenate([both[:, HEAD_DIM:], q_tail[:, HEAD_DIM:]], axis=1)
        q_all[a * rows : a * rows + upper, :] = jnp.where(q_lane < HEAD_DIM, both, q_tail)
        q_all[a * rows + upper : (a + 1) * rows, :] = other[:lower]

    empty = -9984.0 * LOG2E
    head = jnp.where(
        iota((8, queries), 0) == 0,
        float(dropped) if online else float(dropped) * jnp.exp2(jnp.full((8, queries), empty, jnp.float32)),
        0.0,
    )
    acc[...] = jnp.zeros_like(acc)
    acc[:8, :] = head
    peak[...] = jnp.full(peak.shape, empty if dropped else -3e38, jnp.float32)
    zero = jnp.zeros((), jnp.bfloat16)
    value_head = (lane == 0).astype(jnp.bfloat16)

    def step(i, carry):
        for place in CAME:

            @pl.when(i == place)
            def _(place=place):
                for part in range(3):
                    pass_on(part, place).wait_recv()
                for target, (_, start) in CAME.items():
                    if start == place:
                        for part in range(3):
                            pass_on(part, target).start()

        tiles = kv_buf[i, :, rows:, :].reshape(8 * 16, LANES)
        columns = jnp.concatenate([dot32(tiles, pick, TN) for pick in picks], axis=0)[:rows].astype(jnp.bfloat16)
        for a in range(heads):
            kv = kv_buf[i, a, :rows, :]
            bias = jnp.where((lane - HEAD_DIM) // 2 == a, columns, zero)
            k2[a * rows : (a + 1) * rows, :] = jnp.where(lane < HEAD_DIM, kv, bias)
            v2[a * rows : (a + 1) * rows, :] = jnp.where(lane < HEAD_DIM, value_head, kv)
        for begin, end in ((0, cut), (cut, queries)):
            s = dot32(k2[...], q_all[begin:end, :], NT)
            if online:
                old = peak[:, begin:end]
                new = jnp.maximum(old, jnp.max(s, axis=0, keepdims=True))
                p = jnp.exp2(s - new).astype(jnp.bfloat16)
                peak[:, begin:end] = new
                acc[:, begin:end] = acc[:, begin:end] * jnp.exp2(old - new) + dot32(v2[...], p, TN)
            else:
                p = jnp.exp2(s).astype(jnp.bfloat16)
                acc[:, begin:end] += dot32(v2[...], p, TN)
        return carry

    lax.fori_loop(0, 8, step, 0)

    def back(mask):
        return pltpu.make_async_remote_copy(
            o_send.at[mask], o_buf.at[cube_index()], back_send.at[mask], back_recv.at[mask],
            device_id=(far(mask), core), device_id_type=MESH,
        )

    def back_in(mask):
        return pltpu.make_async_remote_copy(
            o_send.at[mask], o_buf.at[cube_index(mask)], back_send.at[mask], back_recv.at[mask],
            device_id=(far(mask), core), device_id_type=MESH,
        )

    scaled = (acc[...] / acc[:1, :]).T.astype(jnp.bfloat16)
    for a in range(heads):
        first = scaled[a * rows : a * rows + upper, HEAD_DIM:]
        other = scaled[a * rows + upper : (a + 1) * rows, HEAD_DIM:]
        if lower < upper:
            other = jnp.concatenate([other, jnp.zeros((upper - lower, HEAD_DIM), jnp.bfloat16)], axis=0)
        o_send[a] = jnp.concatenate([first, other], axis=1)
    for mask in range(1, 8):
        back(mask).start()
    own_o = pltpu.make_async_copy(o_send.at[0], o_buf.at[cube_index()], local_sem.at[2])
    own_o.start()
    weight_copies[1].wait()
    own_o.wait()
    for mask in range(1, 8):
        back_in(mask).wait_recv()

    def swap(which, piece):
        return pltpu.make_async_remote_copy(
            part_send.at[which, piece], part_recv.at[which, piece],
            core_send.at[2 * which + piece], core_recv.at[2 * which + piece],
            device_id=(lax.axis_index("seq"), 1 - core), device_id_type=MESH,
        )

    half = width // 2

    def both(which):
        return jnp.concatenate(
            [
                part_send[which, piece].astype(jnp.float32) + part_recv[which, piece].astype(jnp.float32)
                for piece in range(2)
            ],
            axis=1,
        )

    mixed = jnp.concatenate(
        [
            jnp.concatenate([o_buf[j, :, :HEAD_DIM] for j in range(heads)], axis=1),
            jnp.concatenate([o_buf[j, :lower, HEAD_DIM:] for j in range(heads)], axis=1),
        ],
        axis=0,
    )
    for piece in range(2):
        part_send[0, piece] = dot32(mixed, out_w[:, piece * half : (piece + 1) * half]).astype(jnp.bfloat16)
        swap(0, piece).start()
    bounds = jnp.max(kv_buf[:, :, rows:, :].reshape(8 * heads, 16, LANES).astype(jnp.float32), axis=0)
    norm_send[...] = bounds
    norm_swap = pltpu.make_async_remote_copy(
        norm_send, norm_recv, core_send.at[4], core_recv.at[4],
        device_id=(lax.axis_index("seq"), 1 - core), device_id_type=MESH,
    )
    norm_swap.start()
    swap(0, 0).wait_recv()
    swap(0, 1).wait_recv()
    attention = both(0)
    layer_one[...] = (balanced_ref[:rows].astype(jnp.float32) + attention).astype(jnp.bfloat16)
    normed_mlp = layer_norm(layer_one[...].astype(jnp.float32), mlp_gain_ref[...]).astype(jnp.bfloat16)
    weight_copies[2].wait()
    weight_copies[3].wait()
    step_width = up_w.shape[1] // 4
    for piece in range(4):
        columns = slice(piece * step_width, (piece + 1) * step_width)
        hidden = dot32(normed_mlp, up_w[:, columns])
        hidden_buf[:, columns] = (0.5 * hidden * (1.0 + lax.erf(hidden * math.sqrt(0.5)))).astype(jnp.bfloat16)
    for piece in range(2):
        part_send[1, piece] = dot32(hidden_buf[...], down_w[:, piece * half : (piece + 1) * half]).astype(jnp.bfloat16)
        swap(1, piece).start()
    norm_swap.wait_recv()
    bounds = jnp.maximum(norm_send[...], norm_recv[...])
    plain = (bounds[4:5] * bounds[5:6] <= 68.0 * 68.0) & (bounds[6:7] <= 2.0**30)
    plain_ref[0] = jnp.min(jnp.where(plain, 1, 0))
    swap(1, 0).wait_recv()
    swap(1, 1).wait_recv()
    mlp = both(1)
    result = layer_one[...].astype(jnp.float32) + mlp
    slot = lax.broadcasted_iota(jnp.int32, (rows, width), 0) * 64 + lax.axis_index("seq")
    result_ref[:rows, :] = jnp.where(slot < total_ref[0], result, 0.0).astype(jnp.bfloat16)
    if rows < result_ref.shape[0]:
        result_ref[rows:, :] = jnp.zeros((result_ref.shape[0] - rows, width), jnp.bfloat16)

    for mask in range(1, 8):
        spread_kv(mask).wait_send()
        spread_q(mask).wait_send()
        spread_tile(mask).wait_send()
        back(mask).wait_send()
    for part in range(3):
        for target in CAME:
            pass_on(part, target).wait_send()
    for which in range(2):
        swap(which, 0).wait_send()
        swap(which, 1).wait_send()
    norm_swap.wait_send()


def layer(rows, which, online, total, balanced, bias_tile, attn_gain, mlp_gain, qkv_weight, out_weight, up_weight, down_weight):
    total_rows, width = balanced.shape
    heads = 8
    hidden = up_weight.shape[1]
    queries = heads * rows
    packed = -(-rows // 32) * 16
    bf16 = jnp.bfloat16
    vmem = pl.BlockSpec(memory_space=pltpu.VMEM)
    anywhere = pl.BlockSpec(memory_space=pl.ANY)
    dma = pltpu.SemaphoreType.DMA
    return pl.pallas_call(
        functools.partial(layer_kernel, rows, 64 * (total_rows - rows), online),
        in_specs=[pl.BlockSpec(memory_space=pltpu.SMEM), vmem, vmem, vmem, vmem] + [anywhere] * 4,
        out_specs=[vmem, pl.BlockSpec(memory_space=pltpu.SMEM)],
        out_shape=[
            jax.ShapeDtypeStruct((total_rows, width), bf16),
            jax.ShapeDtypeStruct((1,), jnp.int32),
        ],
        scratch_shapes=[
            pltpu.VMEM(qkv_weight.shape, bf16),
            pltpu.VMEM(out_weight.shape, bf16),
            pltpu.VMEM(up_weight.shape, bf16),
            pltpu.VMEM(down_weight.shape, bf16),
            pltpu.VMEM((heads, rows, LANES), bf16),
            pltpu.VMEM((heads, packed, LANES), bf16),
            pltpu.VMEM((8, heads, rows + 16, LANES), bf16),
            pltpu.VMEM((heads, packed, LANES), bf16),
            pltpu.VMEM((16, LANES), bf16),
            pltpu.VMEM((queries, LANES), bf16),
            pltpu.VMEM((queries, LANES), bf16),
            pltpu.VMEM((queries, LANES), bf16),
            pltpu.VMEM((LANES, queries), jnp.float32),
            pltpu.VMEM((1, queries), jnp.float32),
            pltpu.VMEM((heads, packed, LANES), bf16),
            pltpu.VMEM((heads, packed, LANES), bf16),
            pltpu.VMEM((2, 2, rows, width // 2), bf16),
            pltpu.VMEM((2, 2, rows, width // 2), bf16),
            pltpu.VMEM((rows, width), bf16),
            pltpu.VMEM((rows, hidden), bf16),
            pltpu.VMEM((16, LANES), jnp.float32),
            pltpu.VMEM((16, LANES), jnp.float32),
            dma((4,)),
            dma((3,)),
            dma((3, 8)),
            dma((3, 8)),
            dma((3, 8)),
            dma((3, 8)),
            dma((8,)),
            dma((8,)),
            dma((5,)),
            dma((5,)),
        ],
        compiler_params=pltpu.CompilerParams(
            vmem_limit_bytes=60 * 2**20, collective_id=which, has_side_effects=True
        ),
        cost_estimate=pl.CostEstimate(
            flops=queries * queries * 8 * 256, bytes_accessed=16 * 2**20, transcendentals=queries * queries * 8
        ),
    )(total, balanced, bias_tile, attn_gain, mlp_gain, qkv_weight, out_weight, up_weight, down_weight)


def near_index(mask=0):
    z, y, x = places()
    bits = [(c // 2 + c % 2) % 2 for c in (z, y, x)]
    bits = [1 - b if mask & m else b for b, m in zip(bits, (4, 2, 1))]
    return bits[0] * 4 + bits[1] * 2 + bits[2]


def cube_and_near(shard):
    parts = (shard >> 4, (shard >> 2) & 3, shard & 3)
    cube = sum((c >> 1) * m for c, m in zip(parts, (4, 2, 1)))
    near = sum(((c >> 1) ^ (c & 1)) * m for c, m in zip(parts, (4, 2, 1)))
    return cube, near


def iota(shape, dim):
    return lax.broadcasted_iota(jnp.int32, shape, dim)


def to_column(row):
    n = row.shape[1]
    return jnp.sum(jnp.where(iota((n, n), 0) == iota((n, n), 1), row, 0), axis=1, keepdims=True)


def to_row(column):
    n = column.shape[0]
    return jnp.sum(jnp.where(iota((n, n), 0) == iota((n, n), 1), column, 0), axis=0, keepdims=True)


def deal_kernel(
    choices,
    tokens_hbm,
    sizes_hbm,
    source_hbm,
    target_hbm,
    count_ref,
    gain_ref,
    qkv_hbm,
    balanced_ref,
    bias_ref,
    total_ref,
    index_ref,
    best_ref,
    tokens_ref,
    sizes_ref,
    source_ref,
    target_ref,
    key_w,
    metric,
    shift_send,
    shift_recv,
    count_send,
    count_recv,
    metric_send,
    metric_recv,
    score_send,
    score_recv,
    far_out,
    far_in,
    near_out,
    near_in,
    half_send,
    half_recv,
    shift_sem,
    count_send_sem,
    count_recv_sem,
    metric_sem,
    score_sem,
    far_send_sem,
    far_recv_sem,
    near_send_sem,
    near_recv_sem,
    half_sem,
    local_sem,
    load_sem,
):
    me = lax.axis_index("seq")
    core = lax.axis_index("mp")
    shards = 64
    rows, width = tokens_ref.shape
    half = rows // 2
    part = width // 2
    slots = rows // shards
    ahead, behind = (me + 1) % shards, (me + shards - 1) % shards
    own_columns = pl.ds(pl.multiple_of(core * part, part), part)
    f32, bf16 = jnp.float32, jnp.bfloat16

    loads = [
        pltpu.make_async_copy(src, dst, load_sem.at[i])
        for i, (src, dst) in enumerate(
            (
                (sizes_hbm, sizes_ref),
                (source_hbm, source_ref),
                (target_hbm, target_ref),
                (tokens_hbm, tokens_ref),
                (qkv_hbm.at[1], key_w),
            )
        )
    ]
    for load in loads:
        load.start()
    barrier = pltpu.get_barrier_semaphore()
    for mask in range(1, 8):
        pl.semaphore_signal(barrier, inc=1, device_id=(far(mask), core), device_id_type=MESH)
        pl.semaphore_signal(barrier, inc=1, device_id=(near(mask), core), device_id_type=MESH)
    for other in (ahead, behind):
        pl.semaphore_signal(barrier, inc=1, device_id=(other, core), device_id_type=MESH)
    pl.semaphore_signal(barrier, inc=1, device_id=(me, 1 - core), device_id_type=MESH)

    def remote(src, dst, send_sem, recv_sem, seq, mp):
        return pltpu.make_async_remote_copy(
            src, dst, send_sem, recv_sem, device_id=(seq, mp), device_id_type=MESH
        )

    shift = remote(shift_send, shift_recv, shift_sem.at[0], shift_sem.at[1], ahead, core)
    metric_copy = remote(metric_send, metric_recv, metric_sem.at[0], metric_sem.at[1], behind, core)
    score_copy = remote(score_send, score_recv, score_sem.at[0], score_sem.at[1], me, 1 - core)
    half_copy = remote(half_send, half_recv, half_sem.at[0], half_sem.at[1], me, 1 - core)

    def counts_to(stage, mask):
        return remote(
            count_send.at[stage], count_recv.at[stage, mask], count_send_sem.at[stage, mask],
            count_recv_sem.at[stage, mask], (far, near)[stage](mask), core,
        )

    def far_copy(mask, landed=False):
        return remote(
            far_out.at[cube_index(mask)], far_in.at[cube_index(mask) if landed else cube_index()],
            far_send_sem.at[mask], far_recv_sem.at[mask], far(mask), core,
        )

    def near_copy(mask, landed=False):
        return remote(
            near_out.at[near_index(mask)], near_in.at[near_index(mask) if landed else near_index()],
            near_send_sem.at[mask], near_recv_sem.at[mask], near(mask), core,
        )

    for load in loads[:4]:
        load.wait()
    count = count_ref[0]
    active = iota((1, half), 1) < count
    hit = (source_ref[...] == iota((half, half), 0)) & active
    removed = jnp.max(jnp.where(hit, 1, 0), axis=1, keepdims=True)
    goal = jnp.sum(jnp.where(hit, target_ref[...], 0), axis=1, keepdims=True)
    late_size = to_column(sizes_ref[:, half:])
    weights = jnp.where((goal == iota((half, half), 1)) & (removed > 0), late_size, 0)
    shift_send[:, :part] = tokens_ref[half:, own_columns]
    shift_send[:, part:] = weights.astype(f32).astype(bf16)
    lanes = iota((8, LANES), 1)
    count_send[0] = jnp.where(lanes == me, rows - count, 0).astype(f32)

    pl.semaphore_wait(barrier, 17)
    shift.start()
    for mask in range(1, 8):
        counts_to(0, mask).start()

    for mask in range(1, 8):
        counts_to(0, mask).wait_recv()
    total = count_send[0]
    for mask in range(1, 8):
        total = total + count_recv[0, mask]
    count_send[1] = total
    for mask in range(1, 8):
        counts_to(1, mask).start()

    survive = jnp.concatenate([jnp.ones((1, half), f32), 1.0 - to_row(removed.astype(f32))], axis=1)
    upper = (iota((rows, rows), 0) < iota((rows, rows), 1)).astype(bf16)
    local_rank = dot32(jnp.broadcast_to(survive, (16, rows)).astype(bf16), upper)[:1].astype(jnp.int32)
    early_size = to_column(sizes_ref[:, :half]).astype(f32)

    shift.wait_recv()
    came = shift_recv[:, part:]
    added_size = dot32(came, jnp.ones((half, LANES), bf16), TN)[:, :1]
    added_rows = dot32(came, shift_recv[:, :part], TN)
    new_size = early_size + added_size
    merged = (early_size * tokens_ref[:half, own_columns].astype(f32) + added_rows) / new_size
    biases = jnp.log(jnp.concatenate([new_size, late_size.astype(f32)], axis=0))
    payload = jnp.concatenate(
        [
            jnp.concatenate([merged.astype(bf16), tokens_ref[half:, own_columns]], axis=0),
            jnp.where(iota((rows, LANES), 1) == 0, biases, 0.0).astype(bf16),
        ],
        axis=1,
    )

    for mask in range(1, 8):
        counts_to(1, mask).wait_recv()
    total = count_send[1]
    for mask in range(1, 8):
        total = total + count_recv[1, mask]
    counts = total[:1]
    before = dot32(
        total.astype(bf16), (iota((LANES, LANES), 0) < iota((LANES, LANES), 1)).astype(bf16)
    )[:1].astype(jnp.int32)
    shard_lane = iota((1, LANES), 1)
    start = jnp.sum(jnp.where(shard_lane == me, before, 0), axis=1, keepdims=True)
    everyone = jnp.sum(counts, axis=1, keepdims=True).astype(jnp.int32)
    owner_cube, owner_near = cube_and_near((start + local_rank) & (shards - 1))
    spot = owner_cube * 32 + owner_near * slots + (local_rank >> 6)
    spot = jnp.where(survive > 0, spot, rows)
    put = (spot == iota((rows, rows), 0)).astype(bf16)
    far_out[...] = dot32(put, payload).astype(bf16).reshape(far_out.shape)
    for mask in range(1, 8):
        far_copy(mask).start()
    own_far = pltpu.make_async_copy(far_out.at[cube_index()], far_in.at[cube_index()], local_sem.at[0])
    own_far.start()

    normed = layer_norm(tokens_ref[...].astype(f32), gain_ref[...]).astype(bf16)
    loads[4].wait()
    metric[...] = dot32(normed, key_w[...]).astype(bf16)
    metric_send[...] = metric[:half]
    metric_copy.start()
    own_far.wait()
    for mask in range(1, 8):
        far_copy(mask, True).wait_recv()
    line = iota((rows, rows), 0)
    turned = ((line // slots) % 8) * 32 + (line // 32) * slots + line % slots
    turn = (turned == iota((rows, rows), 1)).astype(bf16)
    near_out[...] = dot32(turn, far_in[...].reshape(rows, part + LANES)).astype(bf16).reshape(near_out.shape)
    for mask in range(1, 8):
        near_copy(mask).start()
    own_near = pltpu.make_async_copy(near_out.at[near_index()], near_in.at[near_index()], local_sem.at[1])
    own_near.start()

    wanted = iota((rows, LANES), 0) * shards + me
    from_cube, from_near = cube_and_near(shard_lane)
    mine = (before <= wanted) & (wanted < before + counts.astype(jnp.int32))
    fetch = jnp.sum(
        jnp.where(mine, from_near * 32 + from_cube * slots + ((wanted - before) >> 6), 0), axis=1, keepdims=True
    )
    filled = wanted[:, :1] < everyone
    take = ((fetch == iota((rows, rows), 1)) & filled).astype(bf16)
    everything = jnp.sum(counts.astype(jnp.int32))
    total_ref[0] = everything
    needed = (everything + shards - 1) >> 6
    index_ref[0] = sum((needed > size).astype(jnp.int32) for size in choices[:-1])

    metric_copy.wait_recv()
    partner = metric_recv[...]
    own_keys = metric[half:]
    score_send[0] = dot32(own_keys, partner, NT)
    own_keys = own_keys.astype(f32)
    partner = partner.astype(f32)
    score_send[1] = jnp.broadcast_to(jnp.sum(own_keys * own_keys, axis=1, keepdims=True), (half, LANES))
    score_send[2] = jnp.broadcast_to(jnp.sum(partner * partner, axis=1, keepdims=True), (half, LANES))
    score_copy.start()

    own_near.wait()
    for mask in range(1, 8):
        near_copy(mask, True).wait_recv()
    taken = dot32(take, near_in[...].reshape(rows, part + LANES))
    half_send[...] = taken[:, :part].astype(bf16)
    half_copy.start()
    balanced_ref[:, own_columns] = half_send[...]
    bias = jnp.where(filled, taken[:, part : part + 1], -9984.0) * LOG2E
    high = bias.astype(bf16).astype(f32)
    low = bias - high
    tile = iota((16, LANES), 0)
    tiles = jnp.zeros((16, LANES), f32)
    for i, column in enumerate((high[:half], high[half:], low[:half], low[half:])):
        tiles = jnp.where(tile == i, to_row(column), tiles)
    bias_ref[...] = tiles.astype(bf16)
    score_copy.wait_recv()
    sums = score_send[...] + score_recv[...]
    cosine = sums[0] * lax.rsqrt(sums[1] + epsilon) * to_row(lax.rsqrt(sums[2][:, :1] + epsilon))
    best_ref[...] = to_row(jnp.max(cosine, axis=1, keepdims=True))
    half_copy.wait_recv()
    balanced_ref[:, pl.ds(pl.multiple_of((1 - core) * part, part), part)] = half_recv[...]

    shift.wait_send()
    metric_copy.wait_send()
    score_copy.wait_send()
    half_copy.wait_send()
    for mask in range(1, 8):
        counts_to(0, mask).wait_send()
        counts_to(1, mask).wait_send()
        far_copy(mask).wait_send()
        near_copy(mask).wait_send()


def deal(choices, tokens, sizes, source, target, count, gain, qkv_weight):
    rows, width = tokens.shape
    half, part = rows // 2, width // 2
    f32, bf16 = jnp.float32, jnp.bfloat16
    vmem = pl.BlockSpec(memory_space=pltpu.VMEM)
    dma = pltpu.SemaphoreType.DMA
    carried = part + LANES
    hbm = pl.BlockSpec(memory_space=pltpu.HBM)
    smem = pl.BlockSpec(memory_space=pltpu.SMEM)
    local_width = qkv_weight.shape[2]
    return pl.pallas_call(
        functools.partial(deal_kernel, choices),
        in_specs=[hbm, hbm, hbm, hbm, smem, vmem, hbm],
        out_specs=[vmem, vmem, smem, smem, vmem],
        out_shape=[
            jax.ShapeDtypeStruct((rows, width), bf16),
            jax.ShapeDtypeStruct((16, LANES), bf16),
            jax.ShapeDtypeStruct((1,), jnp.int32),
            jax.ShapeDtypeStruct((1,), jnp.int32),
            jax.ShapeDtypeStruct((1, half), f32),
        ],
        scratch_shapes=[
            pltpu.VMEM((rows, width), bf16),
            pltpu.VMEM((1, rows), jnp.int32),
            pltpu.VMEM((1, half), jnp.int32),
            pltpu.VMEM((1, half), jnp.int32),
            pltpu.VMEM((width, local_width), bf16),
            pltpu.VMEM((rows, local_width), bf16),
            pltpu.VMEM((half, carried), bf16),
            pltpu.VMEM((half, carried), bf16),
            pltpu.VMEM((2, 8, LANES), f32),
            pltpu.VMEM((2, 8, 8, LANES), f32),
            pltpu.VMEM((half, local_width), bf16),
            pltpu.VMEM((half, local_width), bf16),
            pltpu.VMEM((3, half, LANES), f32),
            pltpu.VMEM((3, half, LANES), f32),
            pltpu.VMEM((8, rows // 8, carried), bf16),
            pltpu.VMEM((8, rows // 8, carried), bf16),
            pltpu.VMEM((8, rows // 8, carried), bf16),
            pltpu.VMEM((8, rows // 8, carried), bf16),
            pltpu.VMEM((rows, part), bf16),
            pltpu.VMEM((rows, part), bf16),
            dma((2,)),
            dma((2, 8)),
            dma((2, 8)),
            dma((2,)),
            dma((2,)),
            dma((8,)),
            dma((8,)),
            dma((8,)),
            dma((8,)),
            dma((2,)),
            dma((2,)),
            dma((5,)),
        ],
        compiler_params=pltpu.CompilerParams(
            vmem_limit_bytes=32 * 2**20, collective_id=8, has_side_effects=True
        ),
        cost_estimate=pl.CostEstimate(flops=10**9, bytes_accessed=4 * 2**20, transcendentals=0),
    )(tokens, sizes, source, target, count, gain, qkv_weight)


def on_device(
    tokens,
    token_sizes,
    merge_source,
    merge_target,
    merge_count,
    attn_gain,
    qkv_weight,
    out_weight,
    mlp_gain,
    up_weight,
    down_weight,
):
    rows = tokens.shape[0]
    sizes = (192, 208, rows)
    balanced, bias_tile, grand_total, index, best = deal(
        sizes, tokens, token_sizes[None, :], merge_source, merge_target, merge_count, attn_gain[None, :], qkv_weight
    )
    operands = (
        grand_total, balanced, bias_tile, attn_gain[None, :], mlp_gain[None, :],
        qkv_weight, out_weight, up_weight, down_weight,
    )
    merged_out, plain = lax.switch(
        index[0], [functools.partial(layer, size, at + 1, False) for at, size in enumerate(sizes)], *operands
    )
    merged_out = lax.cond(
        plain[0] == 1, lambda done, *_: done, lambda _, *given: layer(rows, 9, True, *given)[0], merged_out, *operands
    )
    return (merged_out, best[0])


def solution(mesh):
    placed = (
        P("seq", None),
        P("seq"),
        P("seq", None),
        P("seq", None),
        P("seq"),
        P(),
        P(None, None, "mp"),
        P("mp", None),
        P(),
        P(None, "mp"),
        P("mp", None),
    )
    return jax.shard_map(
        on_device, mesh=mesh, in_specs=placed, out_specs=(P("seq", None), P("seq")), check_vma=False
    )
```

```python
import functools
import math

import jax
import jax.numpy as jnp
from jax import lax
from jax.experimental import pallas as pl
from jax.experimental.pallas import tpu as pltpu
from jax.sharding import PartitionSpec as P

HEAD_DIM = 64
LANES = 128
epsilon = 1e-06
LOG2E = math.log2(math.e)
NT = (((1,), (1,)), ((), ()))
TN = (((0,), (0,)), ((), ()))
NN = (((1,), (0,)), ((), ()))


def layer_norm(values, gain_vector):
    center = values - jnp.mean(values, axis=-1, keepdims=True)
    spread = jnp.mean(center * center, axis=-1, keepdims=True)
    return center * lax.rsqrt(spread + epsilon) * gain_vector


def dot32(a, b, dims=NN):
    return lax.dot_general(a, b, dims, preferred_element_type=jnp.float32)


MESH = pl.DeviceIdType.MESH
ORDERS = ((1, 2, 4), (2, 4, 1), (4, 1, 2))
PARTS = ((0, 3), (3, 3), (6, 2))
CAME = {1: (0, 0), 2: (1, 0), 3: (2, 0), 4: (1, 1), 5: (2, 1), 6: (2, 2), 7: (2, 4)}


def places():
    me = lax.axis_index("seq")
    return me // 16, me // 4 % 4, me % 4


def near(mask):
    z, y, x = places()
    if mask & 4:
        z = z + 1 - 2 * (z % 2)
    if mask & 2:
        y = y + 1 - 2 * (y % 2)
    if mask & 1:
        x = x + 1 - 2 * (x % 2)
    return z * 16 + y * 4 + x


def far(mask):
    z, y, x = places()
    if mask & 4:
        z = 3 - z
    if mask & 2:
        y = 3 - y
    if mask & 1:
        x = 3 - x
    return z * 16 + y * 4 + x


def cube_index(mask=0):
    z, y, x = places()
    z, y, x = z // 2, y // 2, x // 2
    if mask & 4:
        z = 1 - z
    if mask & 2:
        y = 1 - y
    if mask & 1:
        x = 1 - x
    return z * 4 + y * 2 + x


def layer_kernel(
    rows,
    dropped,
    online,
    total_ref,
    balanced_ref,
    bias_ref,
    attn_gain_ref,
    mlp_gain_ref,
    qkv_hbm,
    out_hbm,
    up_hbm,
    down_hbm,
    result_ref,
    plain_ref,
    qkv_w,
    out_w,
    up_w,
    down_w,
    kv_send,
    q_send,
    kv_buf,
    q_buf,
    tile_send,
    q_all,
    k2,
    v2,
    acc,
    peak,
    o_send,
    o_buf,
    part_send,
    part_recv,
    layer_one,
    hidden_buf,
    norm_send,
    norm_recv,
    weight_sem,
    local_sem,
    spread_send,
    spread_recv,
    pass_send,
    pass_recv,
    back_send,
    back_recv,
    core_send,
    core_recv,
):
    core = lax.axis_index("mp")
    heads = 8
    upper = -(-rows // 32) * 16
    lower = rows - upper
    width = balanced_ref.shape[1]

    weight_copies = [
        pltpu.make_async_copy(src, dst, weight_sem.at[i])
        for i, (src, dst) in enumerate(((qkv_hbm, qkv_w), (out_hbm, out_w), (up_hbm, up_w), (down_hbm, down_w)))
    ]
    weight_copies[0].start()

    barrier = pltpu.get_barrier_semaphore()
    for mask in range(1, 8):
        pl.semaphore_signal(barrier, inc=1, device_id=(far(mask), core), device_id_type=MESH)
    for mask in (1, 2, 4):
        pl.semaphore_signal(barrier, inc=1, device_id=(near(mask), core), device_id_type=MESH)
    pl.semaphore_signal(barrier, inc=1, device_id=(lax.axis_index("seq"), 1 - core), device_id_type=MESH)

    balanced = balanced_ref[:rows].astype(jnp.float32)
    normed = layer_norm(balanced, attn_gain_ref[...]).astype(jnp.bfloat16)
    weight_copies[0].wait()
    for copy in weight_copies[1:]:
        copy.start()
    pl.semaphore_wait(barrier, 11)

    key = dot32(normed, qkv_w[1]).astype(jnp.bfloat16)
    value = dot32(normed, qkv_w[2]).astype(jnp.bfloat16)
    for j in range(heads):
        columns = slice(j * HEAD_DIM, (j + 1) * HEAD_DIM)
        kv_send[j] = jnp.concatenate([key[:, columns], value[:, columns]], axis=1)

    def spread_kv(mask):
        return pltpu.make_async_remote_copy(
            kv_send.at[cube_index(mask)], kv_buf.at[0, mask, pl.ds(0, rows)], spread_send.at[0, mask], spread_recv.at[0, mask],
            device_id=(far(mask), core), device_id_type=MESH,
        )

    def spread_q(mask):
        return pltpu.make_async_remote_copy(
            q_send.at[cube_index(mask)], q_buf.at[mask], spread_send.at[1, mask], spread_recv.at[1, mask],
            device_id=(far(mask), core), device_id_type=MESH,
        )

    def spread_tile(mask):
        return pltpu.make_async_remote_copy(
            tile_send, kv_buf.at[0, mask, pl.ds(rows, 16)], spread_send.at[2, mask], spread_recv.at[2, mask],
            device_id=(far(mask), core), device_id_type=MESH,
        )

    def pass_on(part, target):
        first, size = PARTS[part]
        order, place = CAME[target]
        return pltpu.make_async_remote_copy(
            kv_buf.at[place, pl.ds(first, size)], kv_buf.at[target, pl.ds(first, size)],
            pass_send.at[part, target], pass_recv.at[part, target],
            device_id=(near(ORDERS[part][order]), core), device_id_type=MESH,
        )

    for mask in range(1, 8):
        spread_kv(mask).start()
    own_kv = pltpu.make_async_copy(kv_send.at[cube_index()], kv_buf.at[0, 0, pl.ds(0, rows)], local_sem.at[0])
    own_kv.start()
    query = (dot32(normed, qkv_w[0]) * (HEAD_DIM ** (-0.5) * LOG2E)).astype(jnp.bfloat16)
    for j in range(heads):
        mine = query[:, j * HEAD_DIM : (j + 1) * HEAD_DIM]
        other = mine[upper:]
        if lower < upper:
            other = jnp.concatenate([other, jnp.zeros((upper - lower, HEAD_DIM), jnp.bfloat16)], axis=0)
        q_send[j] = jnp.concatenate([mine[:upper], other], axis=1)
    for mask in range(1, 8):
        spread_q(mask).start()
    own_q = pltpu.make_async_copy(q_send.at[cube_index()], q_buf.at[0], local_sem.at[1])
    own_q.start()

    head_of = (
        iota((heads * HEAD_DIM, LANES), 0) // HEAD_DIM == iota((heads * HEAD_DIM, LANES), 1)
    ).astype(jnp.bfloat16)

    def widest(values):
        values = values.astype(jnp.float32)
        squares = dot32((values * values).astype(jnp.bfloat16), head_of)
        return jnp.max(jnp.max(squares, axis=1, keepdims=True), axis=0, keepdims=True)

    largest = jnp.max(
        jnp.max(jnp.abs(value.astype(jnp.float32)), axis=1, keepdims=True), axis=0, keepdims=True
    )
    tile = bias_ref[...].astype(jnp.float32)
    tile_row = iota((16, LANES), 0)
    for i, bound in ((4, widest(query)), (5, widest(key)), (6, largest)):
        tile = jnp.where(tile_row == i, jnp.minimum(bound * 1.02, 1e37), tile)
    tile_send[...] = tile.astype(jnp.bfloat16)
    for mask in range(1, 8):
        spread_tile(mask).start()
    kv_buf[0, 0, rows:, :] = tile_send[...]

    own_kv.wait()
    for mask in range(1, 8):
        spread_kv(mask).wait_recv()
        spread_tile(mask).wait_recv()
    for target in (1, 2, 3):
        for part in range(3):
            pass_on(part, target).start()

    pick_row = iota((8 * 16, LANES), 0)
    pick_lane = iota((8 * 16, LANES), 1) - HEAD_DIM - pick_row // 16 * 2
    pick_row = pick_row % 16
    picks = [
        (((pick_row == i) & (pick_lane == 0)) | ((pick_row == i + 2) & (pick_lane == 1))).astype(jnp.bfloat16)
        for i in range(2)
    ]
    lane = iota((rows, LANES), 1)

    own_q.wait()
    for mask in range(1, 8):
        spread_q(mask).wait_recv()
    queries = heads * rows
    cut = queries // 2 // 256 * 256
    q_lane = iota((upper, LANES), 1)
    q_tail = ((q_lane >= HEAD_DIM) & (q_lane < HEAD_DIM + 16)).astype(jnp.bfloat16)
    for a in range(heads):
        both = q_buf[a]
        other = jnp.concatenate([both[:, HEAD_DIM:], q_tail[:, HEAD_DIM:]], axis=1)
        q_all[a * rows : a * rows + upper, :] = jnp.where(q_lane < HEAD_DIM, both, q_tail)
        q_all[a * rows + upper : (a + 1) * rows, :] = other[:lower]

    empty = -9984.0 * LOG2E
    head = jnp.where(
        iota((8, queries), 0) == 0,
        float(dropped) if online else float(dropped) * jnp.exp2(jnp.full((8, queries), empty, jnp.float32)),
        0.0,
    )
    acc[...] = jnp.zeros_like(acc)
    acc[:8, :] = head
    peak[...] = jnp.full(peak.shape, empty if dropped else -3e38, jnp.float32)
    zero = jnp.zeros((), jnp.bfloat16)
    value_head = (lane == 0).astype(jnp.bfloat16)

    def step(i, carry):
        for place in CAME:

            @pl.when(i == place)
            def _(place=place):
                for part in range(3):
                    pass_on(part, place).wait_recv()
                for target, (_, start) in CAME.items():
                    if start == place:
                        for part in range(3):
                            pass_on(part, target).start()

        tiles = kv_buf[i, :, rows:, :].reshape(8 * 16, LANES)
        columns = jnp.concatenate([dot32(tiles, pick, TN) for pick in picks], axis=0)[:rows].astype(jnp.bfloat16)
        for a in range(heads):
            kv = kv_buf[i, a, :rows, :]
            bias = jnp.where((lane - HEAD_DIM) // 2 == a, columns, zero)
            k2[a * rows : (a + 1) * rows, :] = jnp.where(lane < HEAD_DIM, kv, bias)
            v2[a * rows : (a + 1) * rows, :] = jnp.where(lane < HEAD_DIM, value_head, kv)
        for begin, end in ((0, cut), (cut, queries)):
            s = dot32(k2[...], q_all[begin:end, :], NT)
            if online:
                old = peak[:, begin:end]
                new = jnp.maximum(old, jnp.max(s, axis=0, keepdims=True))
                p = jnp.exp2(s - new).astype(jnp.bfloat16)
                peak[:, begin:end] = new
                acc[:, begin:end] = acc[:, begin:end] * jnp.exp2(old - new) + dot32(v2[...], p, TN)
            else:
                p = jnp.exp2(s).astype(jnp.bfloat16)
                acc[:, begin:end] += dot32(v2[...], p, TN)
        return carry

    lax.fori_loop(0, 8, step, 0)

    def back(mask):
        return pltpu.make_async_remote_copy(
            o_send.at[mask], o_buf.at[cube_index()], back_send.at[mask], back_recv.at[mask],
            device_id=(far(mask), core), device_id_type=MESH,
        )

    def back_in(mask):
        return pltpu.make_async_remote_copy(
            o_send.at[mask], o_buf.at[cube_index(mask)], back_send.at[mask], back_recv.at[mask],
            device_id=(far(mask), core), device_id_type=MESH,
        )

    scaled = (acc[...] / acc[:1, :]).T.astype(jnp.bfloat16)
    for a in range(heads):
        first = scaled[a * rows : a * rows + upper, HEAD_DIM:]
        other = scaled[a * rows + upper : (a + 1) * rows, HEAD_DIM:]
        if lower < upper:
            other = jnp.concatenate([other, jnp.zeros((upper - lower, HEAD_DIM), jnp.bfloat16)], axis=0)
        o_send[a] = jnp.concatenate([first, other], axis=1)
    for mask in range(1, 8):
        back(mask).start()
    own_o = pltpu.make_async_copy(o_send.at[0], o_buf.at[cube_index()], local_sem.at[2])
    own_o.start()
    weight_copies[1].wait()
    own_o.wait()
    for mask in range(1, 8):
        back_in(mask).wait_recv()

    def swap(which, piece):
        return pltpu.make_async_remote_copy(
            part_send.at[which, piece], part_recv.at[which, piece],
            core_send.at[2 * which + piece], core_recv.at[2 * which + piece],
            device_id=(lax.axis_index("seq"), 1 - core), device_id_type=MESH,
        )

    half = width // 2

    def both(which):
        return jnp.concatenate(
            [
                part_send[which, piece].astype(jnp.float32) + part_recv[which, piece].astype(jnp.float32)
                for piece in range(2)
            ],
            axis=1,
        )

    mixed = jnp.concatenate(
        [
            jnp.concatenate([o_buf[j, :, :HEAD_DIM] for j in range(heads)], axis=1),
            jnp.concatenate([o_buf[j, :lower, HEAD_DIM:] for j in range(heads)], axis=1),
        ],
        axis=0,
    )
    for piece in range(2):
        part_send[0, piece] = dot32(mixed, out_w[:, piece * half : (piece + 1) * half]).astype(jnp.bfloat16)
        swap(0, piece).start()
    bounds = jnp.max(kv_buf[:, :, rows:, :].reshape(8 * heads, 16, LANES).astype(jnp.float32), axis=0)
    norm_send[...] = bounds
    norm_swap = pltpu.make_async_remote_copy(
        norm_send, norm_recv, core_send.at[4], core_recv.at[4],
        device_id=(lax.axis_index("seq"), 1 - core), device_id_type=MESH,
    )
    norm_swap.start()
    swap(0, 0).wait_recv()
    swap(0, 1).wait_recv()
    attention = both(0)
    layer_one[...] = (balanced_ref[:rows].astype(jnp.float32) + attention).astype(jnp.bfloat16)
    normed_mlp = layer_norm(layer_one[...].astype(jnp.float32), mlp_gain_ref[...]).astype(jnp.bfloat16)
    weight_copies[2].wait()
    weight_copies[3].wait()
    step_width = up_w.shape[1] // 4
    for piece in range(4):
        columns = slice(piece * step_width, (piece + 1) * step_width)
        hidden = dot32(normed_mlp, up_w[:, columns])
        hidden_buf[:, columns] = (0.5 * hidden * (1.0 + lax.erf(hidden * math.sqrt(0.5)))).astype(jnp.bfloat16)
    for piece in range(2):
        part_send[1, piece] = dot32(hidden_buf[...], down_w[:, piece * half : (piece + 1) * half]).astype(jnp.bfloat16)
        swap(1, piece).start()
    norm_swap.wait_recv()
    bounds = jnp.maximum(norm_send[...], norm_recv[...])
    plain = (bounds[4:5] * bounds[5:6] <= 68.0 * 68.0) & (bounds[6:7] <= 2.0**30)
    plain_ref[0] = jnp.min(jnp.where(plain, 1, 0))
    swap(1, 0).wait_recv()
    swap(1, 1).wait_recv()
    mlp = both(1)
    result = layer_one[...].astype(jnp.float32) + mlp
    slot = lax.broadcasted_iota(jnp.int32, (rows, width), 0) * 64 + lax.axis_index("seq")
    result_ref[:rows, :] = jnp.where(slot < total_ref[0], result, 0.0).astype(jnp.bfloat16)
    if rows < result_ref.shape[0]:
        result_ref[rows:, :] = jnp.zeros((result_ref.shape[0] - rows, width), jnp.bfloat16)

    for mask in range(1, 8):
        spread_kv(mask).wait_send()
        spread_q(mask).wait_send()
        spread_tile(mask).wait_send()
        back(mask).wait_send()
    for part in range(3):
        for target in CAME:
            pass_on(part, target).wait_send()
    for which in range(2):
        swap(which, 0).wait_send()
        swap(which, 1).wait_send()
    norm_swap.wait_send()


def layer(rows, which, online, total, balanced, bias_tile, attn_gain, mlp_gain, qkv_weight, out_weight, up_weight, down_weight):
    total_rows, width = balanced.shape
    heads = 8
    hidden = up_weight.shape[1]
    queries = heads * rows
    packed = -(-rows // 32) * 16
    bf16 = jnp.bfloat16
    vmem = pl.BlockSpec(memory_space=pltpu.VMEM)
    anywhere = pl.BlockSpec(memory_space=pl.ANY)
    dma = pltpu.SemaphoreType.DMA
    return pl.pallas_call(
        functools.partial(layer_kernel, rows, 64 * (total_rows - rows), online),
        in_specs=[pl.BlockSpec(memory_space=pltpu.SMEM), vmem, vmem, vmem, vmem] + [anywhere] * 4,
        out_specs=[vmem, pl.BlockSpec(memory_space=pltpu.SMEM)],
        out_shape=[
            jax.ShapeDtypeStruct((total_rows, width), bf16),
            jax.ShapeDtypeStruct((1,), jnp.int32),
        ],
        scratch_shapes=[
            pltpu.VMEM(qkv_weight.shape, bf16),
            pltpu.VMEM(out_weight.shape, bf16),
            pltpu.VMEM(up_weight.shape, bf16),
            pltpu.VMEM(down_weight.shape, bf16),
            pltpu.VMEM((heads, rows, LANES), bf16),
            pltpu.VMEM((heads, packed, LANES), bf16),
            pltpu.VMEM((8, heads, rows + 16, LANES), bf16),
            pltpu.VMEM((heads, packed, LANES), bf16),
            pltpu.VMEM((16, LANES), bf16),
            pltpu.VMEM((queries, LANES), bf16),
            pltpu.VMEM((queries, LANES), bf16),
            pltpu.VMEM((queries, LANES), bf16),
            pltpu.VMEM((LANES, queries), jnp.float32),
            pltpu.VMEM((1, queries), jnp.float32),
            pltpu.VMEM((heads, packed, LANES), bf16),
            pltpu.VMEM((heads, packed, LANES), bf16),
            pltpu.VMEM((2, 2, rows, width // 2), bf16),
            pltpu.VMEM((2, 2, rows, width // 2), bf16),
            pltpu.VMEM((rows, width), bf16),
            pltpu.VMEM((rows, hidden), bf16),
            pltpu.VMEM((16, LANES), jnp.float32),
            pltpu.VMEM((16, LANES), jnp.float32),
            dma((4,)),
            dma((3,)),
            dma((3, 8)),
            dma((3, 8)),
            dma((3, 8)),
            dma((3, 8)),
            dma((8,)),
            dma((8,)),
            dma((5,)),
            dma((5,)),
        ],
        compiler_params=pltpu.CompilerParams(
            vmem_limit_bytes=60 * 2**20, collective_id=which, has_side_effects=True
        ),
        cost_estimate=pl.CostEstimate(
            flops=queries * queries * 8 * 256, bytes_accessed=16 * 2**20, transcendentals=queries * queries * 8
        ),
    )(total, balanced, bias_tile, attn_gain, mlp_gain, qkv_weight, out_weight, up_weight, down_weight)


def near_index(mask=0):
    z, y, x = places()
    bits = [(c // 2 + c % 2) % 2 for c in (z, y, x)]
    bits = [1 - b if mask & m else b for b, m in zip(bits, (4, 2, 1))]
    return bits[0] * 4 + bits[1] * 2 + bits[2]


def cube_and_near(shard):
    parts = (shard >> 4, (shard >> 2) & 3, shard & 3)
    cube = sum((c >> 1) * m for c, m in zip(parts, (4, 2, 1)))
    near = sum(((c >> 1) ^ (c & 1)) * m for c, m in zip(parts, (4, 2, 1)))
    return cube, near


def iota(shape, dim):
    return lax.broadcasted_iota(jnp.int32, shape, dim)


def to_column(row):
    n = row.shape[1]
    return jnp.sum(jnp.where(iota((n, n), 0) == iota((n, n), 1), row, 0), axis=1, keepdims=True)


def to_row(column):
    n = column.shape[0]
    return jnp.sum(jnp.where(iota((n, n), 0) == iota((n, n), 1), column, 0), axis=0, keepdims=True)


def deal_kernel(
    choices,
    tokens_hbm,
    sizes_hbm,
    source_hbm,
    target_hbm,
    count_ref,
    gain_ref,
    qkv_hbm,
    balanced_ref,
    bias_ref,
    total_ref,
    index_ref,
    best_ref,
    tokens_ref,
    sizes_ref,
    source_ref,
    target_ref,
    key_w,
    metric,
    shift_send,
    shift_recv,
    count_send,
    count_recv,
    metric_send,
    metric_recv,
    score_send,
    score_recv,
    far_out,
    far_in,
    near_out,
    near_in,
    half_send,
    half_recv,
    shift_sem,
    count_send_sem,
    count_recv_sem,
    metric_sem,
    score_sem,
    far_send_sem,
    far_recv_sem,
    near_send_sem,
    near_recv_sem,
    half_sem,
    local_sem,
    load_sem,
):
    me = lax.axis_index("seq")
    core = lax.axis_index("mp")
    shards = 64
    rows, width = tokens_ref.shape
    half = rows // 2
    part = width // 2
    slots = rows // shards
    ahead, behind = (me + 1) % shards, (me + shards - 1) % shards
    own_columns = pl.ds(pl.multiple_of(core * part, part), part)
    f32, bf16 = jnp.float32, jnp.bfloat16

    loads = [
        pltpu.make_async_copy(src, dst, load_sem.at[i])
        for i, (src, dst) in enumerate(
            (
                (sizes_hbm, sizes_ref),
                (source_hbm, source_ref),
                (target_hbm, target_ref),
                (tokens_hbm, tokens_ref),
                (qkv_hbm.at[1], key_w),
            )
        )
    ]
    for load in loads:
        load.start()
    barrier = pltpu.get_barrier_semaphore()
    for mask in range(1, 8):
        pl.semaphore_signal(barrier, inc=1, device_id=(far(mask), core), device_id_type=MESH)
        pl.semaphore_signal(barrier, inc=1, device_id=(near(mask), core), device_id_type=MESH)
    for other in (ahead, behind):
        pl.semaphore_signal(barrier, inc=1, device_id=(other, core), device_id_type=MESH)
    pl.semaphore_signal(barrier, inc=1, device_id=(me, 1 - core), device_id_type=MESH)

    def remote(src, dst, send_sem, recv_sem, seq, mp):
        return pltpu.make_async_remote_copy(
            src, dst, send_sem, recv_sem, device_id=(seq, mp), device_id_type=MESH
        )

    shift = remote(shift_send, shift_recv, shift_sem.at[0], shift_sem.at[1], ahead, core)
    metric_copy = remote(metric_send, metric_recv, metric_sem.at[0], metric_sem.at[1], behind, core)
    score_copy = remote(score_send, score_recv, score_sem.at[0], score_sem.at[1], me, 1 - core)
    half_copy = remote(half_send, half_recv, half_sem.at[0], half_sem.at[1], me, 1 - core)

    def counts_to(stage, mask):
        return remote(
            count_send.at[stage], count_recv.at[stage, mask], count_send_sem.at[stage, mask],
            count_recv_sem.at[stage, mask], (far, near)[stage](mask), core,
        )

    def far_copy(mask, landed=False):
        return remote(
            far_out.at[cube_index(mask)], far_in.at[cube_index(mask) if landed else cube_index()],
            far_send_sem.at[mask], far_recv_sem.at[mask], far(mask), core,
        )

    def near_copy(mask, landed=False):
        return remote(
            near_out.at[near_index(mask)], near_in.at[near_index(mask) if landed else near_index()],
            near_send_sem.at[mask], near_recv_sem.at[mask], near(mask), core,
        )

    for load in loads[:4]:
        load.wait()
    count = count_ref[0]
    active = iota((1, half), 1) < count
    hit = (source_ref[...] == iota((half, half), 0)) & active
    removed = jnp.max(jnp.where(hit, 1, 0), axis=1, keepdims=True)
    goal = jnp.sum(jnp.where(hit, target_ref[...], 0), axis=1, keepdims=True)
    late_size = to_column(sizes_ref[:, half:])
    weights = jnp.where((goal == iota((half, half), 1)) & (removed > 0), late_size, 0)
    shift_send[:, :part] = tokens_ref[half:, own_columns]
    shift_send[:, part:] = weights.astype(f32).astype(bf16)
    lanes = iota((8, LANES), 1)
    count_send[0] = jnp.where(lanes == me, rows - count, 0).astype(f32)

    pl.semaphore_wait(barrier, 17)
    shift.start()
    for mask in range(1, 8):
        counts_to(0, mask).start()

    for mask in range(1, 8):
        counts_to(0, mask).wait_recv()
    total = count_send[0]
    for mask in range(1, 8):
        total = total + count_recv[0, mask]
    count_send[1] = total
    for mask in range(1, 8):
        counts_to(1, mask).start()

    survive = jnp.concatenate([jnp.ones((1, half), f32), 1.0 - to_row(removed.astype(f32))], axis=1)
    upper = (iota((rows, rows), 0) < iota((rows, rows), 1)).astype(bf16)
    local_rank = dot32(jnp.broadcast_to(survive, (16, rows)).astype(bf16), upper)[:1].astype(jnp.int32)
    early_size = to_column(sizes_ref[:, :half]).astype(f32)

    shift.wait_recv()
    came = shift_recv[:, part:]
    added_size = dot32(came, jnp.ones((half, LANES), bf16), TN)[:, :1]
    added_rows = dot32(came, shift_recv[:, :part], TN)
    new_size = early_size + added_size
    merged = (early_size * tokens_ref[:half, own_columns].astype(f32) + added_rows) / new_size
    biases = jnp.log(jnp.concatenate([new_size, late_size.astype(f32)], axis=0))
    payload = jnp.concatenate(
        [
            jnp.concatenate([merged.astype(bf16), tokens_ref[half:, own_columns]], axis=0),
            jnp.where(iota((rows, LANES), 1) == 0, biases, 0.0).astype(bf16),
        ],
        axis=1,
    )

    for mask in range(1, 8):
        counts_to(1, mask).wait_recv()
    total = count_send[1]
    for mask in range(1, 8):
        total = total + count_recv[1, mask]
    counts = total[:1]
    before = dot32(
        total.astype(bf16), (iota((LANES, LANES), 0) < iota((LANES, LANES), 1)).astype(bf16)
    )[:1].astype(jnp.int32)
    shard_lane = iota((1, LANES), 1)
    start = jnp.sum(jnp.where(shard_lane == me, before, 0), axis=1, keepdims=True)
    everyone = jnp.sum(counts, axis=1, keepdims=True).astype(jnp.int32)
    owner_cube, owner_near = cube_and_near((start + local_rank) & (shards - 1))
    spot = owner_cube * 32 + owner_near * slots + (local_rank >> 6)
    spot = jnp.where(survive > 0, spot, rows)
    put = (spot == iota((rows, rows), 0)).astype(bf16)
    far_out[...] = dot32(put, payload).astype(bf16).reshape(far_out.shape)
    for mask in range(1, 8):
        far_copy(mask).start()
    own_far = pltpu.make_async_copy(far_out.at[cube_index()], far_in.at[cube_index()], local_sem.at[0])
    own_far.start()

    normed = layer_norm(tokens_ref[...].astype(f32), gain_ref[...]).astype(bf16)
    loads[4].wait()
    metric[...] = dot32(normed, key_w[...]).astype(bf16)
    metric_send[...] = metric[:half]
    metric_copy.start()
    own_far.wait()
    for mask in range(1, 8):
        far_copy(mask, True).wait_recv()
    line = iota((rows, rows), 0)
    turned = ((line // slots) % 8) * 32 + (line // 32) * slots + line % slots
    turn = (turned == iota((rows, rows), 1)).astype(bf16)
    near_out[...] = dot32(turn, far_in[...].reshape(rows, part + LANES)).astype(bf16).reshape(near_out.shape)
    for mask in range(1, 8):
        near_copy(mask).start()
    own_near = pltpu.make_async_copy(near_out.at[near_index()], near_in.at[near_index()], local_sem.at[1])
    own_near.start()

    wanted = iota((rows, LANES), 0) * shards + me
    from_cube, from_near = cube_and_near(shard_lane)
    mine = (before <= wanted) & (wanted < before + counts.astype(jnp.int32))
    fetch = jnp.sum(
        jnp.where(mine, from_near * 32 + from_cube * slots + ((wanted - before) >> 6), 0), axis=1, keepdims=True
    )
    filled = wanted[:, :1] < everyone
    take = ((fetch == iota((rows, rows), 1)) & filled).astype(bf16)
    everything = jnp.sum(counts.astype(jnp.int32))
    total_ref[0] = everything
    needed = (everything + shards - 1) >> 6
    index_ref[0] = sum((needed > size).astype(jnp.int32) for size in choices[:-1])

    metric_copy.wait_recv()
    partner = metric_recv[...]
    own_keys = metric[half:]
    score_send[0] = dot32(own_keys, partner, NT)
    own_keys = own_keys.astype(f32)
    partner = partner.astype(f32)
    score_send[1] = jnp.broadcast_to(jnp.sum(own_keys * own_keys, axis=1, keepdims=True), (half, LANES))
    score_send[2] = jnp.broadcast_to(jnp.sum(partner * partner, axis=1, keepdims=True), (half, LANES))
    score_copy.start()

    own_near.wait()
    for mask in range(1, 8):
        near_copy(mask, True).wait_recv()
    taken = dot32(take, near_in[...].reshape(rows, part + LANES))
    half_send[...] = taken[:, :part].astype(bf16)
    half_copy.start()
    balanced_ref[:, own_columns] = half_send[...]
    bias = jnp.where(filled, taken[:, part : part + 1], -9984.0) * LOG2E
    high = bias.astype(bf16).astype(f32)
    low = bias - high
    tile = iota((16, LANES), 0)
    tiles = jnp.zeros((16, LANES), f32)
    for i, column in enumerate((high[:half], high[half:], low[:half], low[half:])):
        tiles = jnp.where(tile == i, to_row(column), tiles)
    bias_ref[...] = tiles.astype(bf16)
    score_copy.wait_recv()
    sums = score_send[...] + score_recv[...]
    cosine = sums[0] * lax.rsqrt(sums[1] + epsilon) * to_row(lax.rsqrt(sums[2][:, :1] + epsilon))
    best_ref[...] = to_row(jnp.max(cosine, axis=1, keepdims=True))
    half_copy.wait_recv()
    balanced_ref[:, pl.ds(pl.multiple_of((1 - core) * part, part), part)] = half_recv[...]

    shift.wait_send()
    metric_copy.wait_send()
    score_copy.wait_send()
    half_copy.wait_send()
    for mask in range(1, 8):
        counts_to(0, mask).wait_send()
        counts_to(1, mask).wait_send()
        far_copy(mask).wait_send()
        near_copy(mask).wait_send()


def deal(choices, tokens, sizes, source, target, count, gain, qkv_weight):
    rows, width = tokens.shape
    half, part = rows // 2, width // 2
    f32, bf16 = jnp.float32, jnp.bfloat16
    vmem = pl.BlockSpec(memory_space=pltpu.VMEM)
    dma = pltpu.SemaphoreType.DMA
    carried = part + LANES
    hbm = pl.BlockSpec(memory_space=pltpu.HBM)
    smem = pl.BlockSpec(memory_space=pltpu.SMEM)
    local_width = qkv_weight.shape[2]
    return pl.pallas_call(
        functools.partial(deal_kernel, choices),
        in_specs=[hbm, hbm, hbm, hbm, smem, vmem, hbm],
        out_specs=[vmem, vmem, smem, smem, vmem],
        out_shape=[
            jax.ShapeDtypeStruct((rows, width), bf16),
            jax.ShapeDtypeStruct((16, LANES), bf16),
            jax.ShapeDtypeStruct((1,), jnp.int32),
            jax.ShapeDtypeStruct((1,), jnp.int32),
            jax.ShapeDtypeStruct((1, half), f32),
        ],
        scratch_shapes=[
            pltpu.VMEM((rows, width), bf16),
            pltpu.VMEM((1, rows), jnp.int32),
            pltpu.VMEM((1, half), jnp.int32),
            pltpu.VMEM((1, half), jnp.int32),
            pltpu.VMEM((width, local_width), bf16),
            pltpu.VMEM((rows, local_width), bf16),
            pltpu.VMEM((half, carried), bf16),
            pltpu.VMEM((half, carried), bf16),
            pltpu.VMEM((2, 8, LANES), f32),
            pltpu.VMEM((2, 8, 8, LANES), f32),
            pltpu.VMEM((half, local_width), bf16),
            pltpu.VMEM((half, local_width), bf16),
            pltpu.VMEM((3, half, LANES), f32),
            pltpu.VMEM((3, half, LANES), f32),
            pltpu.VMEM((8, rows // 8, carried), bf16),
            pltpu.VMEM((8, rows // 8, carried), bf16),
            pltpu.VMEM((8, rows // 8, carried), bf16),
            pltpu.VMEM((8, rows // 8, carried), bf16),
            pltpu.VMEM((rows, part), bf16),
            pltpu.VMEM((rows, part), bf16),
            dma((2,)),
            dma((2, 8)),
            dma((2, 8)),
            dma((2,)),
            dma((2,)),
            dma((8,)),
            dma((8,)),
            dma((8,)),
            dma((8,)),
            dma((2,)),
            dma((2,)),
            dma((5,)),
        ],
        compiler_params=pltpu.CompilerParams(
            vmem_limit_bytes=62 * 2**20, collective_id=8, has_side_effects=True
        ),
        cost_estimate=pl.CostEstimate(flops=10**9, bytes_accessed=4 * 2**20, transcendentals=0),
    )(tokens, sizes, source, target, count, gain, qkv_weight)


def on_device(
    tokens,
    token_sizes,
    merge_source,
    merge_target,
    merge_count,
    attn_gain,
    qkv_weight,
    out_weight,
    mlp_gain,
    up_weight,
    down_weight,
):
    rows = tokens.shape[0]
    sizes = (208, rows)
    balanced, bias_tile, grand_total, index, best = deal(
        sizes, tokens, token_sizes[None, :], merge_source, merge_target, merge_count, attn_gain[None, :], qkv_weight
    )
    operands = (
        grand_total, balanced, bias_tile, attn_gain[None, :], mlp_gain[None, :],
        qkv_weight, out_weight, up_weight, down_weight,
    )
    merged_out, plain = lax.switch(
        index[0], [functools.partial(layer, size, at + 1, False) for at, size in enumerate(sizes)], *operands
    )
    merged_out = lax.cond(
        plain[0] == 1, lambda done, *_: done, lambda _, *given: layer(rows, 9, True, *given)[0], merged_out, *operands
    )
    return (merged_out, best[0])


def solution(mesh):
    placed = (
        P("seq", None),
        P("seq"),
        P("seq", None),
        P("seq", None),
        P("seq"),
        P(),
        P(None, None, "mp"),
        P("mp", None),
        P(),
        P(None, "mp"),
        P("mp", None),
    )
    return jax.shard_map(
        on_device, mesh=mesh, in_specs=placed, out_specs=(P("seq", None), P("seq")), check_vma=False
    )
```

```python
import functools
import math

import jax
import jax.numpy as jnp
from jax import lax
from jax.experimental import pallas as pl
from jax.experimental.pallas import tpu as pltpu
from jax.sharding import PartitionSpec as P

HEAD_DIM = 64
LANES = 128
epsilon = 1e-06
LOG2E = math.log2(math.e)
NT = (((1,), (1,)), ((), ()))
TN = (((0,), (0,)), ((), ()))
NN = (((1,), (0,)), ((), ()))


def layer_norm(values, gain_vector):
    center = values - jnp.mean(values, axis=-1, keepdims=True)
    spread = jnp.mean(center * center, axis=-1, keepdims=True)
    return center * lax.rsqrt(spread + epsilon) * gain_vector


def dot32(a, b, dims=NN):
    return lax.dot_general(a, b, dims, preferred_element_type=jnp.float32)


MESH = pl.DeviceIdType.MESH
ORDERS = ((1, 2, 4), (2, 4, 1), (4, 1, 2))
PARTS = ((0, 3), (3, 3), (6, 2))
CAME = {1: (0, 0), 2: (1, 0), 3: (2, 0), 4: (1, 1), 5: (2, 1), 6: (2, 2), 7: (2, 4)}


def places():
    me = lax.axis_index("seq")
    return me // 16, me // 4 % 4, me % 4


def near(mask):
    z, y, x = places()
    if mask & 4:
        z = z + 1 - 2 * (z % 2)
    if mask & 2:
        y = y + 1 - 2 * (y % 2)
    if mask & 1:
        x = x + 1 - 2 * (x % 2)
    return z * 16 + y * 4 + x


def far(mask):
    z, y, x = places()
    if mask & 4:
        z = 3 - z
    if mask & 2:
        y = 3 - y
    if mask & 1:
        x = 3 - x
    return z * 16 + y * 4 + x


def cube_index(mask=0):
    z, y, x = places()
    z, y, x = z // 2, y // 2, x // 2
    if mask & 4:
        z = 1 - z
    if mask & 2:
        y = 1 - y
    if mask & 1:
        x = 1 - x
    return z * 4 + y * 2 + x


def layer_kernel(
    rows,
    dropped,
    online,
    total_ref,
    balanced_ref,
    bias_ref,
    attn_gain_ref,
    mlp_gain_ref,
    qkv_hbm,
    out_hbm,
    up_hbm,
    down_hbm,
    result_ref,
    plain_ref,
    qkv_w,
    out_w,
    up_w,
    down_w,
    kv_send,
    q_send,
    kv_buf,
    q_buf,
    tile_send,
    q_all,
    k2,
    v2,
    acc,
    peak,
    o_send,
    o_buf,
    part_send,
    part_recv,
    layer_one,
    hidden_buf,
    norm_send,
    norm_recv,
    weight_sem,
    local_sem,
    spread_send,
    spread_recv,
    pass_send,
    pass_recv,
    back_send,
    back_recv,
    core_send,
    core_recv,
):
    core = lax.axis_index("mp")
    heads = 8
    upper = -(-rows // 32) * 16
    lower = rows - upper
    width = balanced_ref.shape[1]

    weight_copies = [
        pltpu.make_async_copy(src, dst, weight_sem.at[i])
        for i, (src, dst) in enumerate(((qkv_hbm, qkv_w), (out_hbm, out_w), (up_hbm, up_w), (down_hbm, down_w)))
    ]
    weight_copies[0].start()

    barrier = pltpu.get_barrier_semaphore()
    for mask in range(1, 8):
        pl.semaphore_signal(barrier, inc=1, device_id=(far(mask), core), device_id_type=MESH)
    for mask in (1, 2, 4):
        pl.semaphore_signal(barrier, inc=1, device_id=(near(mask), core), device_id_type=MESH)
    pl.semaphore_signal(barrier, inc=1, device_id=(lax.axis_index("seq"), 1 - core), device_id_type=MESH)

    balanced = balanced_ref[:rows].astype(jnp.float32)
    normed = layer_norm(balanced, attn_gain_ref[...]).astype(jnp.bfloat16)
    weight_copies[0].wait()
    for copy in weight_copies[1:]:
        copy.start()
    pl.semaphore_wait(barrier, 11)

    key = dot32(normed, qkv_w[1]).astype(jnp.bfloat16)
    value = dot32(normed, qkv_w[2]).astype(jnp.bfloat16)
    for j in range(heads):
        columns = slice(j * HEAD_DIM, (j + 1) * HEAD_DIM)
        kv_send[j] = jnp.concatenate([key[:, columns], value[:, columns]], axis=1)

    def spread_kv(mask):
        return pltpu.make_async_remote_copy(
            kv_send.at[cube_index(mask)], kv_buf.at[0, mask, pl.ds(0, rows)], spread_send.at[0, mask], spread_recv.at[0, mask],
            device_id=(far(mask), core), device_id_type=MESH,
        )

    def spread_q(mask):
        return pltpu.make_async_remote_copy(
            q_send.at[cube_index(mask)], q_buf.at[mask], spread_send.at[1, mask], spread_recv.at[1, mask],
            device_id=(far(mask), core), device_id_type=MESH,
        )

    def spread_tile(mask):
        return pltpu.make_async_remote_copy(
            tile_send, kv_buf.at[0, mask, pl.ds(rows, 16)], spread_send.at[2, mask], spread_recv.at[2, mask],
            device_id=(far(mask), core), device_id_type=MESH,
        )

    def pass_on(part, target):
        first, size = PARTS[part]
        order, place = CAME[target]
        return pltpu.make_async_remote_copy(
            kv_buf.at[place, pl.ds(first, size)], kv_buf.at[target, pl.ds(first, size)],
            pass_send.at[part, target], pass_recv.at[part, target],
            device_id=(near(ORDERS[part][order]), core), device_id_type=MESH,
        )

    for mask in range(1, 8):
        spread_kv(mask).start()
    own_kv = pltpu.make_async_copy(kv_send.at[cube_index()], kv_buf.at[0, 0, pl.ds(0, rows)], local_sem.at[0])
    own_kv.start()
    query = (dot32(normed, qkv_w[0]) * (HEAD_DIM ** (-0.5) * LOG2E)).astype(jnp.bfloat16)
    for j in range(heads):
        mine = query[:, j * HEAD_DIM : (j + 1) * HEAD_DIM]
        other = mine[upper:]
        if lower < upper:
            other = jnp.concatenate([other, jnp.zeros((upper - lower, HEAD_DIM), jnp.bfloat16)], axis=0)
        q_send[j] = jnp.concatenate([mine[:upper], other], axis=1)
    for mask in range(1, 8):
        spread_q(mask).start()
    own_q = pltpu.make_async_copy(q_send.at[cube_index()], q_buf.at[0], local_sem.at[1])
    own_q.start()

    head_of = (
        iota((heads * HEAD_DIM, LANES), 0) // HEAD_DIM == iota((heads * HEAD_DIM, LANES), 1)
    ).astype(jnp.bfloat16)

    def widest(values):
        values = values.astype(jnp.float32)
        squares = dot32((values * values).astype(jnp.bfloat16), head_of)
        return jnp.max(jnp.max(squares, axis=1, keepdims=True), axis=0, keepdims=True)

    largest = jnp.max(
        jnp.max(jnp.abs(value.astype(jnp.float32)), axis=1, keepdims=True), axis=0, keepdims=True
    )
    tile = bias_ref[...].astype(jnp.float32)
    tile_row = iota((16, LANES), 0)
    for i, bound in ((4, widest(query)), (5, widest(key)), (6, largest)):
        tile = jnp.where(tile_row == i, jnp.minimum(bound * 1.02, 1e37), tile)
    tile_send[...] = tile.astype(jnp.bfloat16)
    for mask in range(1, 8):
        spread_tile(mask).start()
    kv_buf[0, 0, rows:, :] = tile_send[...]

    own_kv.wait()
    for mask in range(1, 8):
        spread_kv(mask).wait_recv()
        spread_tile(mask).wait_recv()
    for target in (1, 2, 3):
        for part in range(3):
            pass_on(part, target).start()

    pick_row = iota((8 * 16, LANES), 0)
    pick_lane = iota((8 * 16, LANES), 1) - HEAD_DIM - pick_row // 16 * 2
    pick_row = pick_row % 16
    picks = [
        (((pick_row == i) & (pick_lane == 0)) | ((pick_row == i + 2) & (pick_lane == 1))).astype(jnp.bfloat16)
        for i in range(2)
    ]
    lane = iota((rows, LANES), 1)

    own_q.wait()
    for mask in range(1, 8):
        spread_q(mask).wait_recv()
    queries = heads * rows
    cut = queries // 2 // 256 * 256
    q_lane = iota((upper, LANES), 1)
    q_tail = ((q_lane >= HEAD_DIM) & (q_lane < HEAD_DIM + 16)).astype(jnp.bfloat16)
    for a in range(heads):
        both = q_buf[a]
        other = jnp.concatenate([both[:, HEAD_DIM:], q_tail[:, HEAD_DIM:]], axis=1)
        q_all[a * rows : a * rows + upper, :] = jnp.where(q_lane < HEAD_DIM, both, q_tail)
        q_all[a * rows + upper : (a + 1) * rows, :] = other[:lower]

    empty = -9984.0 * LOG2E
    head = jnp.where(
        iota((8, queries), 0) == 0,
        float(dropped) if online else float(dropped) * jnp.exp2(jnp.full((8, queries), empty, jnp.float32)),
        0.0,
    )
    acc[...] = jnp.zeros_like(acc)
    acc[:8, :] = head
    peak[...] = jnp.full(peak.shape, empty if dropped else -3e38, jnp.float32)
    zero = jnp.zeros((), jnp.bfloat16)
    value_head = (lane == 0).astype(jnp.bfloat16)

    def back(mask):
        return pltpu.make_async_remote_copy(
            o_send.at[mask], o_buf.at[cube_index()], back_send.at[mask], back_recv.at[mask],
            device_id=(far(mask), core), device_id_type=MESH,
        )

    def back_in(mask):
        return pltpu.make_async_remote_copy(
            o_send.at[mask], o_buf.at[cube_index(mask)], back_send.at[mask], back_recv.at[mask],
            device_id=(far(mask), core), device_id_type=MESH,
        )

    own_o = pltpu.make_async_copy(o_send.at[0], o_buf.at[cube_index()], local_sem.at[2])
    early = cut // rows

    def finish(start, stop):
        begin = start * rows // LANES * LANES
        end = cut if stop == early else queries
        scaled = (acc[:, begin:end] / acc[:1, begin:end]).T.astype(jnp.bfloat16)
        for a in range(start, stop):
            at = a * rows - begin
            first = scaled[at : at + upper, HEAD_DIM:]
            other = scaled[at + upper : at + rows, HEAD_DIM:]
            if lower < upper:
                other = jnp.concatenate([other, jnp.zeros((upper - lower, HEAD_DIM), jnp.bfloat16)], axis=0)
            o_send[a] = jnp.concatenate([first, other], axis=1)
            (back(a) if a else own_o).start()

    def step(i, carry):
        for place in CAME:

            @pl.when(i == place)
            def _(place=place):
                for part in range(3):
                    pass_on(part, place).wait_recv()
                for target, (_, start) in CAME.items():
                    if start == place:
                        for part in range(3):
                            pass_on(part, target).start()

        tiles = kv_buf[i, :, rows:, :].reshape(8 * 16, LANES)
        columns = jnp.concatenate([dot32(tiles, pick, TN) for pick in picks], axis=0)[:rows].astype(jnp.bfloat16)
        for a in range(heads):
            kv = kv_buf[i, a, :rows, :]
            bias = jnp.where((lane - HEAD_DIM) // 2 == a, columns, zero)
            k2[a * rows : (a + 1) * rows, :] = jnp.where(lane < HEAD_DIM, kv, bias)
            v2[a * rows : (a + 1) * rows, :] = jnp.where(lane < HEAD_DIM, value_head, kv)
        for begin, end in ((0, cut), (cut, queries)):
            s = dot32(k2[...], q_all[begin:end, :], NT)
            if online:
                old = peak[:, begin:end]
                new = jnp.maximum(old, jnp.max(s, axis=0, keepdims=True))
                p = jnp.exp2(s - new).astype(jnp.bfloat16)
                peak[:, begin:end] = new
                acc[:, begin:end] = acc[:, begin:end] * jnp.exp2(old - new) + dot32(v2[...], p, TN)
            else:
                p = jnp.exp2(s).astype(jnp.bfloat16)
                acc[:, begin:end] += dot32(v2[...], p, TN)
            if end == cut:

                @pl.when(i == 7)
                def _():
                    finish(0, early)

        return carry

    lax.fori_loop(0, 8, step, 0)

    finish(early, heads)
    weight_copies[1].wait()
    own_o.wait()
    for mask in range(1, 8):
        back_in(mask).wait_recv()

    def swap(which, piece):
        return pltpu.make_async_remote_copy(
            part_send.at[which, piece], part_recv.at[which, piece],
            core_send.at[2 * which + piece], core_recv.at[2 * which + piece],
            device_id=(lax.axis_index("seq"), 1 - core), device_id_type=MESH,
        )

    half = width // 2

    def both(which):
        return jnp.concatenate(
            [
                part_send[which, piece].astype(jnp.float32) + part_recv[which, piece].astype(jnp.float32)
                for piece in range(2)
            ],
            axis=1,
        )

    mixed = jnp.concatenate(
        [
            jnp.concatenate([o_buf[j, :, :HEAD_DIM] for j in range(heads)], axis=1),
            jnp.concatenate([o_buf[j, :lower, HEAD_DIM:] for j in range(heads)], axis=1),
        ],
        axis=0,
    )
    for piece in range(2):
        part_send[0, piece] = dot32(mixed, out_w[:, piece * half : (piece + 1) * half]).astype(jnp.bfloat16)
        swap(0, piece).start()
    bounds = jnp.max(kv_buf[:, :, rows:, :].reshape(8 * heads, 16, LANES).astype(jnp.float32), axis=0)
    norm_send[...] = bounds
    norm_swap = pltpu.make_async_remote_copy(
        norm_send, norm_recv, core_send.at[4], core_recv.at[4],
        device_id=(lax.axis_index("seq"), 1 - core), device_id_type=MESH,
    )
    norm_swap.start()
    swap(0, 0).wait_recv()
    swap(0, 1).wait_recv()
    attention = both(0)
    layer_one[...] = (balanced_ref[:rows].astype(jnp.float32) + attention).astype(jnp.bfloat16)
    normed_mlp = layer_norm(layer_one[...].astype(jnp.float32), mlp_gain_ref[...]).astype(jnp.bfloat16)
    weight_copies[2].wait()
    weight_copies[3].wait()
    step_width = up_w.shape[1] // 4
    for piece in range(4):
        columns = slice(piece * step_width, (piece + 1) * step_width)
        hidden = dot32(normed_mlp, up_w[:, columns])
        hidden_buf[:, columns] = (0.5 * hidden * (1.0 + lax.erf(hidden * math.sqrt(0.5)))).astype(jnp.bfloat16)
    for piece in range(2):
        part_send[1, piece] = dot32(hidden_buf[...], down_w[:, piece * half : (piece + 1) * half]).astype(jnp.bfloat16)
        swap(1, piece).start()
    norm_swap.wait_recv()
    bounds = jnp.maximum(norm_send[...], norm_recv[...])
    plain = (bounds[4:5] * bounds[5:6] <= 68.0 * 68.0) & (bounds[6:7] <= 2.0**30)
    plain_ref[0] = jnp.min(jnp.where(plain, 1, 0))
    swap(1, 0).wait_recv()
    swap(1, 1).wait_recv()
    mlp = both(1)
    result = layer_one[...].astype(jnp.float32) + mlp
    slot = lax.broadcasted_iota(jnp.int32, (rows, width), 0) * 64 + lax.axis_index("seq")
    result_ref[:rows, :] = jnp.where(slot < total_ref[0], result, 0.0).astype(jnp.bfloat16)
    if rows < result_ref.shape[0]:
        result_ref[rows:, :] = jnp.zeros((result_ref.shape[0] - rows, width), jnp.bfloat16)

    for mask in range(1, 8):
        spread_kv(mask).wait_send()
        spread_q(mask).wait_send()
        spread_tile(mask).wait_send()
        back(mask).wait_send()
    for part in range(3):
        for target in CAME:
            pass_on(part, target).wait_send()
    for which in range(2):
        swap(which, 0).wait_send()
        swap(which, 1).wait_send()
    norm_swap.wait_send()


def layer(rows, which, online, total, balanced, bias_tile, attn_gain, mlp_gain, qkv_weight, out_weight, up_weight, down_weight):
    total_rows, width = balanced.shape
    heads = 8
    hidden = up_weight.shape[1]
    queries = heads * rows
    packed = -(-rows // 32) * 16
    bf16 = jnp.bfloat16
    vmem = pl.BlockSpec(memory_space=pltpu.VMEM)
    anywhere = pl.BlockSpec(memory_space=pl.ANY)
    dma = pltpu.SemaphoreType.DMA
    return pl.pallas_call(
        functools.partial(layer_kernel, rows, 64 * (total_rows - rows), online),
        in_specs=[pl.BlockSpec(memory_space=pltpu.SMEM), vmem, vmem, vmem, vmem] + [anywhere] * 4,
        out_specs=[vmem, pl.BlockSpec(memory_space=pltpu.SMEM)],
        out_shape=[
            jax.ShapeDtypeStruct((total_rows, width), bf16),
            jax.ShapeDtypeStruct((1,), jnp.int32),
        ],
        scratch_shapes=[
            pltpu.VMEM(qkv_weight.shape, bf16),
            pltpu.VMEM(out_weight.shape, bf16),
            pltpu.VMEM(up_weight.shape, bf16),
            pltpu.VMEM(down_weight.shape, bf16),
            pltpu.VMEM((heads, rows, LANES), bf16),
            pltpu.VMEM((heads, packed, LANES), bf16),
            pltpu.VMEM((8, heads, rows + 16, LANES), bf16),
            pltpu.VMEM((heads, packed, LANES), bf16),
            pltpu.VMEM((16, LANES), bf16),
            pltpu.VMEM((queries, LANES), bf16),
            pltpu.VMEM((queries, LANES), bf16),
            pltpu.VMEM((queries, LANES), bf16),
            pltpu.VMEM((LANES, queries), jnp.float32),
            pltpu.VMEM((1, queries), jnp.float32),
            pltpu.VMEM((heads, packed, LANES), bf16),
            pltpu.VMEM((heads, packed, LANES), bf16),
            pltpu.VMEM((2, 2, rows, width // 2), bf16),
            pltpu.VMEM((2, 2, rows, width // 2), bf16),
            pltpu.VMEM((rows, width), bf16),
            pltpu.VMEM((rows, hidden), bf16),
            pltpu.VMEM((16, LANES), jnp.float32),
            pltpu.VMEM((16, LANES), jnp.float32),
            dma((4,)),
            dma((3,)),
            dma((3, 8)),
            dma((3, 8)),
            dma((3, 8)),
            dma((3, 8)),
            dma((8,)),
            dma((8,)),
            dma((5,)),
            dma((5,)),
        ],
        compiler_params=pltpu.CompilerParams(
            vmem_limit_bytes=60 * 2**20, collective_id=which, has_side_effects=True
        ),
        cost_estimate=pl.CostEstimate(
            flops=queries * queries * 8 * 256, bytes_accessed=16 * 2**20, transcendentals=queries * queries * 8
        ),
    )(total, balanced, bias_tile, attn_gain, mlp_gain, qkv_weight, out_weight, up_weight, down_weight)


def near_index(mask=0):
    z, y, x = places()
    bits = [(c // 2 + c % 2) % 2 for c in (z, y, x)]
    bits = [1 - b if mask & m else b for b, m in zip(bits, (4, 2, 1))]
    return bits[0] * 4 + bits[1] * 2 + bits[2]


def cube_and_near(shard):
    parts = (shard >> 4, (shard >> 2) & 3, shard & 3)
    cube = sum((c >> 1) * m for c, m in zip(parts, (4, 2, 1)))
    near = sum(((c >> 1) ^ (c & 1)) * m for c, m in zip(parts, (4, 2, 1)))
    return cube, near


def iota(shape, dim):
    return lax.broadcasted_iota(jnp.int32, shape, dim)


def to_column(row):
    n = row.shape[1]
    return jnp.sum(jnp.where(iota((n, n), 0) == iota((n, n), 1), row, 0), axis=1, keepdims=True)


def to_row(column):
    n = column.shape[0]
    return jnp.sum(jnp.where(iota((n, n), 0) == iota((n, n), 1), column, 0), axis=0, keepdims=True)


def deal_kernel(
    choices,
    tokens_hbm,
    sizes_hbm,
    source_hbm,
    target_hbm,
    count_ref,
    gain_ref,
    qkv_hbm,
    balanced_ref,
    bias_ref,
    total_ref,
    index_ref,
    best_ref,
    tokens_ref,
    sizes_ref,
    source_ref,
    target_ref,
    key_w,
    metric,
    shift_send,
    shift_recv,
    count_send,
    count_recv,
    metric_send,
    metric_recv,
    score_send,
    score_recv,
    far_out,
    far_in,
    near_out,
    near_in,
    half_send,
    half_recv,
    shift_sem,
    count_send_sem,
    count_recv_sem,
    metric_sem,
    score_sem,
    far_send_sem,
    far_recv_sem,
    near_send_sem,
    near_recv_sem,
    half_sem,
    local_sem,
    load_sem,
):
    me = lax.axis_index("seq")
    core = lax.axis_index("mp")
    shards = 64
    rows, width = tokens_ref.shape
    half = rows // 2
    part = width // 2
    slots = rows // shards
    ahead, behind = (me + 1) % shards, (me + shards - 1) % shards
    own_columns = pl.ds(pl.multiple_of(core * part, part), part)
    f32, bf16 = jnp.float32, jnp.bfloat16

    loads = [
        pltpu.make_async_copy(src, dst, load_sem.at[i])
        for i, (src, dst) in enumerate(
            (
                (sizes_hbm, sizes_ref),
                (source_hbm, source_ref),
                (target_hbm, target_ref),
                (tokens_hbm, tokens_ref),
                (qkv_hbm.at[1], key_w),
            )
        )
    ]
    for load in loads:
        load.start()
    barrier = pltpu.get_barrier_semaphore()
    for mask in range(1, 8):
        pl.semaphore_signal(barrier, inc=1, device_id=(far(mask), core), device_id_type=MESH)
        pl.semaphore_signal(barrier, inc=1, device_id=(near(mask), core), device_id_type=MESH)
    for other in (ahead, behind):
        pl.semaphore_signal(barrier, inc=1, device_id=(other, core), device_id_type=MESH)
    pl.semaphore_signal(barrier, inc=1, device_id=(me, 1 - core), device_id_type=MESH)

    def remote(src, dst, send_sem, recv_sem, seq, mp):
        return pltpu.make_async_remote_copy(
            src, dst, send_sem, recv_sem, device_id=(seq, mp), device_id_type=MESH
        )

    shift = remote(shift_send, shift_recv, shift_sem.at[0], shift_sem.at[1], ahead, core)
    metric_copy = remote(metric_send, metric_recv, metric_sem.at[0], metric_sem.at[1], behind, core)
    score_copy = remote(score_send, score_recv, score_sem.at[0], score_sem.at[1], me, 1 - core)
    half_copy = remote(half_send, half_recv, half_sem.at[0], half_sem.at[1], me, 1 - core)

    def counts_to(stage, mask):
        return remote(
            count_send.at[stage], count_recv.at[stage, mask], count_send_sem.at[stage, mask],
            count_recv_sem.at[stage, mask], (far, near)[stage](mask), core,
        )

    def far_copy(mask, landed=False):
        return remote(
            far_out.at[cube_index(mask)], far_in.at[cube_index(mask) if landed else cube_index()],
            far_send_sem.at[mask], far_recv_sem.at[mask], far(mask), core,
        )

    def near_copy(mask, landed=False):
        return remote(
            near_out.at[near_index(mask)], near_in.at[near_index(mask) if landed else near_index()],
            near_send_sem.at[mask], near_recv_sem.at[mask], near(mask), core,
        )

    for load in loads[:4]:
        load.wait()
    count = count_ref[0]
    active = iota((1, half), 1) < count
    hit = (source_ref[...] == iota((half, half), 0)) & active
    removed = jnp.max(jnp.where(hit, 1, 0), axis=1, keepdims=True)
    goal = jnp.sum(jnp.where(hit, target_ref[...], 0), axis=1, keepdims=True)
    late_size = to_column(sizes_ref[:, half:])
    weights = jnp.where((goal == iota((half, half), 1)) & (removed > 0), late_size, 0)
    shift_send[:, :part] = tokens_ref[half:, own_columns]
    shift_send[:, part:] = weights.astype(f32).astype(bf16)
    lanes = iota((8, LANES), 1)
    count_send[0] = jnp.where(lanes == me, rows - count, 0).astype(f32)

    pl.semaphore_wait(barrier, 17)
    shift.start()
    for mask in range(1, 8):
        counts_to(0, mask).start()

    for mask in range(1, 8):
        counts_to(0, mask).wait_recv()
    total = count_send[0]
    for mask in range(1, 8):
        total = total + count_recv[0, mask]
    count_send[1] = total
    for mask in range(1, 8):
        counts_to(1, mask).start()

    survive = jnp.concatenate([jnp.ones((1, half), f32), 1.0 - to_row(removed.astype(f32))], axis=1)
    upper = (iota((rows, rows), 0) < iota((rows, rows), 1)).astype(bf16)
    local_rank = dot32(jnp.broadcast_to(survive, (16, rows)).astype(bf16), upper)[:1].astype(jnp.int32)
    early_size = to_column(sizes_ref[:, :half]).astype(f32)

    shift.wait_recv()
    came = shift_recv[:, part:]
    added_size = dot32(came, jnp.ones((half, LANES), bf16), TN)[:, :1]
    added_rows = dot32(came, shift_recv[:, :part], TN)
    new_size = early_size + added_size
    merged = (early_size * tokens_ref[:half, own_columns].astype(f32) + added_rows) / new_size
    biases = jnp.log(jnp.concatenate([new_size, late_size.astype(f32)], axis=0))
    payload = jnp.concatenate(
        [
            jnp.concatenate([merged.astype(bf16), tokens_ref[half:, own_columns]], axis=0),
            jnp.where(iota((rows, LANES), 1) == 0, biases, 0.0).astype(bf16),
        ],
        axis=1,
    )

    for mask in range(1, 8):
        counts_to(1, mask).wait_recv()
    total = count_send[1]
    for mask in range(1, 8):
        total = total + count_recv[1, mask]
    counts = total[:1]
    before = dot32(
        total.astype(bf16), (iota((LANES, LANES), 0) < iota((LANES, LANES), 1)).astype(bf16)
    )[:1].astype(jnp.int32)
    shard_lane = iota((1, LANES), 1)
    start = jnp.sum(jnp.where(shard_lane == me, before, 0), axis=1, keepdims=True)
    everyone = jnp.sum(counts, axis=1, keepdims=True).astype(jnp.int32)
    owner_cube, owner_near = cube_and_near((start + local_rank) & (shards - 1))
    spot = owner_cube * 32 + owner_near * slots + (local_rank >> 6)
    spot = jnp.where(survive > 0, spot, rows)
    put = (spot == iota((rows, rows), 0)).astype(bf16)
    far_out[...] = dot32(put, payload).astype(bf16).reshape(far_out.shape)
    for mask in range(1, 8):
        far_copy(mask).start()
    own_far = pltpu.make_async_copy(far_out.at[cube_index()], far_in.at[cube_index()], local_sem.at[0])
    own_far.start()

    normed = layer_norm(tokens_ref[...].astype(f32), gain_ref[...]).astype(bf16)
    loads[4].wait()
    metric[...] = dot32(normed, key_w[...]).astype(bf16)
    metric_send[...] = metric[:half]
    metric_copy.start()
    own_far.wait()
    for mask in range(1, 8):
        far_copy(mask, True).wait_recv()
    line = iota((rows, rows), 0)
    turned = ((line // slots) % 8) * 32 + (line // 32) * slots + line % slots
    turn = (turned == iota((rows, rows), 1)).astype(bf16)
    near_out[...] = dot32(turn, far_in[...].reshape(rows, part + LANES)).astype(bf16).reshape(near_out.shape)
    for mask in range(1, 8):
        near_copy(mask).start()
    own_near = pltpu.make_async_copy(near_out.at[near_index()], near_in.at[near_index()], local_sem.at[1])
    own_near.start()

    wanted = iota((rows, LANES), 0) * shards + me
    from_cube, from_near = cube_and_near(shard_lane)
    mine = (before <= wanted) & (wanted < before + counts.astype(jnp.int32))
    fetch = jnp.sum(
        jnp.where(mine, from_near * 32 + from_cube * slots + ((wanted - before) >> 6), 0), axis=1, keepdims=True
    )
    filled = wanted[:, :1] < everyone
    take = ((fetch == iota((rows, rows), 1)) & filled).astype(bf16)
    everything = jnp.sum(counts.astype(jnp.int32))
    total_ref[0] = everything
    needed = (everything + shards - 1) >> 6
    index_ref[0] = sum((needed > size).astype(jnp.int32) for size in choices[:-1])

    metric_copy.wait_recv()
    partner = metric_recv[...]
    own_keys = metric[half:]
    score_send[0] = dot32(own_keys, partner, NT)
    own_keys = own_keys.astype(f32)
    partner = partner.astype(f32)
    score_send[1] = jnp.broadcast_to(jnp.sum(own_keys * own_keys, axis=1, keepdims=True), (half, LANES))
    score_send[2] = jnp.broadcast_to(jnp.sum(partner * partner, axis=1, keepdims=True), (half, LANES))
    score_copy.start()

    own_near.wait()
    for mask in range(1, 8):
        near_copy(mask, True).wait_recv()
    taken = dot32(take, near_in[...].reshape(rows, part + LANES))
    half_send[...] = taken[:, :part].astype(bf16)
    half_copy.start()
    balanced_ref[:, own_columns] = half_send[...]
    bias = jnp.where(filled, taken[:, part : part + 1], -9984.0) * LOG2E
    high = bias.astype(bf16).astype(f32)
    low = bias - high
    tile = iota((16, LANES), 0)
    tiles = jnp.zeros((16, LANES), f32)
    for i, column in enumerate((high[:half], high[half:], low[:half], low[half:])):
        tiles = jnp.where(tile == i, to_row(column), tiles)
    bias_ref[...] = tiles.astype(bf16)
    score_copy.wait_recv()
    sums = score_send[...] + score_recv[...]
    cosine = sums[0] * lax.rsqrt(sums[1] + epsilon) * to_row(lax.rsqrt(sums[2][:, :1] + epsilon))
    best_ref[...] = to_row(jnp.max(cosine, axis=1, keepdims=True))
    half_copy.wait_recv()
    balanced_ref[:, pl.ds(pl.multiple_of((1 - core) * part, part), part)] = half_recv[...]

    shift.wait_send()
    metric_copy.wait_send()
    score_copy.wait_send()
    half_copy.wait_send()
    for mask in range(1, 8):
        counts_to(0, mask).wait_send()
        counts_to(1, mask).wait_send()
        far_copy(mask).wait_send()
        near_copy(mask).wait_send()


def deal(choices, tokens, sizes, source, target, count, gain, qkv_weight):
    rows, width = tokens.shape
    half, part = rows // 2, width // 2
    f32, bf16 = jnp.float32, jnp.bfloat16
    vmem = pl.BlockSpec(memory_space=pltpu.VMEM)
    dma = pltpu.SemaphoreType.DMA
    carried = part + LANES
    hbm = pl.BlockSpec(memory_space=pltpu.HBM)
    smem = pl.BlockSpec(memory_space=pltpu.SMEM)
    local_width = qkv_weight.shape[2]
    return pl.pallas_call(
        functools.partial(deal_kernel, choices),
        in_specs=[hbm, hbm, hbm, hbm, smem, vmem, hbm],
        out_specs=[vmem, vmem, smem, smem, vmem],
        out_shape=[
            jax.ShapeDtypeStruct((rows, width), bf16),
            jax.ShapeDtypeStruct((16, LANES), bf16),
            jax.ShapeDtypeStruct((1,), jnp.int32),
            jax.ShapeDtypeStruct((1,), jnp.int32),
            jax.ShapeDtypeStruct((1, half), f32),
        ],
        scratch_shapes=[
            pltpu.VMEM((rows, width), bf16),
            pltpu.VMEM((1, rows), jnp.int32),
            pltpu.VMEM((1, half), jnp.int32),
            pltpu.VMEM((1, half), jnp.int32),
            pltpu.VMEM((width, local_width), bf16),
            pltpu.VMEM((rows, local_width), bf16),
            pltpu.VMEM((half, carried), bf16),
            pltpu.VMEM((half, carried), bf16),
            pltpu.VMEM((2, 8, LANES), f32),
            pltpu.VMEM((2, 8, 8, LANES), f32),
            pltpu.VMEM((half, local_width), bf16),
            pltpu.VMEM((half, local_width), bf16),
            pltpu.VMEM((3, half, LANES), f32),
            pltpu.VMEM((3, half, LANES), f32),
            pltpu.VMEM((8, rows // 8, carried), bf16),
            pltpu.VMEM((8, rows // 8, carried), bf16),
            pltpu.VMEM((8, rows // 8, carried), bf16),
            pltpu.VMEM((8, rows // 8, carried), bf16),
            pltpu.VMEM((rows, part), bf16),
            pltpu.VMEM((rows, part), bf16),
            dma((2,)),
            dma((2, 8)),
            dma((2, 8)),
            dma((2,)),
            dma((2,)),
            dma((8,)),
            dma((8,)),
            dma((8,)),
            dma((8,)),
            dma((2,)),
            dma((2,)),
            dma((5,)),
        ],
        compiler_params=pltpu.CompilerParams(
            vmem_limit_bytes=62 * 2**20, collective_id=8, has_side_effects=True
        ),
        cost_estimate=pl.CostEstimate(flops=10**9, bytes_accessed=4 * 2**20, transcendentals=0),
    )(tokens, sizes, source, target, count, gain, qkv_weight)


def on_device(
    tokens,
    token_sizes,
    merge_source,
    merge_target,
    merge_count,
    attn_gain,
    qkv_weight,
    out_weight,
    mlp_gain,
    up_weight,
    down_weight,
):
    rows = tokens.shape[0]
    sizes = (208, rows)
    balanced, bias_tile, grand_total, index, best = deal(
        sizes, tokens, token_sizes[None, :], merge_source, merge_target, merge_count, attn_gain[None, :], qkv_weight
    )
    operands = (
        grand_total, balanced, bias_tile, attn_gain[None, :], mlp_gain[None, :],
        qkv_weight, out_weight, up_weight, down_weight,
    )
    merged_out, plain = lax.switch(
        index[0], [functools.partial(layer, size, at + 1, False) for at, size in enumerate(sizes)], *operands
    )
    merged_out = lax.cond(
        plain[0] == 1, lambda done, *_: done, lambda _, *given: layer(rows, 9, True, *given)[0], merged_out, *operands
    )
    return (merged_out, best[0])


def solution(mesh):
    placed = (
        P("seq", None),
        P("seq"),
        P("seq", None),
        P("seq", None),
        P("seq"),
        P(),
        P(None, None, "mp"),
        P("mp", None),
        P(),
        P(None, "mp"),
        P("mp", None),
    )
    return jax.shard_map(
        on_device, mesh=mesh, in_specs=placed, out_specs=(P("seq", None), P("seq")), check_vma=False
    )
```
